32 devices in a mesh: dp: 8 (over z, x), tensor: 4 (over y, core).
Axes of the slice: x: 2, y: 2, z: 4, core: 2. Of those that a mesh axis runs over, the one named last changes fastest.
Arguments:
- tokens: bfloat16 [2048, 1536], P('dp'), may hold values from -6 to 6
- targets: bfloat16 [2048, 1536], P('dp'), may hold values from -6 to 6
- modulation: bfloat16 [16, 3, 1536], P('dp'), may hold values from -2.5 to 2.5
- live_block_count: int32 [8], P('dp'), may hold values from 2 to 4, as said below
- preferred_blocks: int32 [8], P('dp'), may hold values from 1 to 3, as said below
- last_block_rows: int32 [8, 2], P('dp'), may hold values from 1 to 64
- up_projection_weight: bfloat16 [1536, 6144], P('dp', 'tensor'), may hold values from -0.15625 to 0.15625
- down_weight_transposed: bfloat16 [1536, 6144], P('dp', 'tensor'), may hold values from -0.078125 to 0.078125
- adapter_input_factor: bfloat16 [1536, 64], replicated, may hold values from -0.15625 to 0.15625
- adapter_output_factor: bfloat16 [64, 6144], P(None, 'tensor'), may hold values from -0.75 to 0.75
Outputs:
- losses: float32 [8], P('dp')
- grad_tokens: bfloat16 [2048, 1536], P('dp')
- grad_lora_a: float32 [1536, 64], replicated
- grad_lora_b: float32 [64, 6144], P(None, 'tensor')
The draws below stay inside these ranges and needn't reach their ends.
Inputs may be any that keep to these rules, and one draw needn't show every extreme that they name: `live_block_count`: device i of dp and device (i + 4) modulo 8 together hold 6 live blocks; some pair holds 4. `preferred_blocks`: at most live_block_count - 1 for each pair, so the loser has a block too.
All inputs are finite; a program needn't handle non-finite values.
Results may differ from the reference program's by a relative error of at most 0.035.
Values may be sent and summed in bfloat16 or wider, within the bound.
A program may use at most 64 MiB of HBM per device.

```python
import jax
import jax.numpy as jnp
from jax import lax

MODEL_WIDTH = 1536
HIDDEN_UNITS = 6144
LOW_RANK_SIZE = 64
BLK = 64
HOLD = 3
CAP = 4
SAMPLES = 16
ROWS = 2048
N_DP = 8
N_TENSOR = 4


def pair_loads(key):
    half = N_DP // 2
    offset = jax.random.randint(key, (half,), -1, 2)
    offset = offset.at[0].set(1)
    return jnp.concatenate([HOLD + offset, HOLD - offset]).astype(jnp.int32)


def draw_live_block_count(key, part):
    return pair_loads(key)


def draw_preferred_blocks(key, part):
    loads = pair_loads(key)
    key = jax.random.fold_in(key, 7)
    spread = jax.random.randint(key, (N_DP,), 0, 1 << 20)
    chosen = 1 + spread % (loads - 1)
    chosen = chosen.at[0].set(loads[0] - 1)
    return chosen.astype(jnp.int32)


def draw_last_block_rows(key, part):
    key = jax.random.fold_in(key, 11)
    rows = jax.random.randint(key, (N_DP, 2), 1, BLK + 1)
    rows = rows.at[0, 0].set(BLK)
    rows = rows.at[0, 1].set(1)
    return rows.astype(jnp.int32)


def shard_levels(rng, shape, split, least, high):
    def one(dim, blocks):
        steps = jax.random.uniform(jax.random.fold_in(jax.random.fold_in(rng, 6), dim), (blocks,), jnp.float32, least / len(split), high / len(split))
        return jnp.repeat(jnp.exp(steps), shape[dim] // blocks).reshape((-1,) + (1,) * (len(shape) - dim - 1))

    loudness = one(*split[0])
    for cut in split[1:]:
        loudness = loudness * one(*cut)
    return loudness


def noise(rng, shape, deviation, limit, pieces=(), held_as=jnp.bfloat16):
    array = jax.random.normal(rng, shape, jnp.float32) * deviation
    if len(pieces) > 0:
        array = shard_levels(rng, shape, pieces, -0.22, 0.18) * array
    return jnp.clip(array, min=-limit, max=limit).astype(held_as)


def setup_inputs(seed: int = 0) -> dict:
    splits = jax.random.split(jax.random.key(seed), 11)
    tokens = noise(splits[0], (ROWS, MODEL_WIDTH), 1.0, 6.0, ((0, 8),))
    targets = noise(splits[1], (ROWS, MODEL_WIDTH), 1.0, 6.0, ((0, 8),))
    modulation = noise(splits[2], (SAMPLES, 3, MODEL_WIDTH), 0.5, 2.5, ((0, 8),))
    live_block_count = draw_live_block_count(jax.random.fold_in(splits[10], 71), 0)
    preferred_blocks = draw_preferred_blocks(jax.random.fold_in(splits[10], 71), 0)
    last_block_rows = draw_last_block_rows(jax.random.fold_in(splits[10], 71), 0)
    up_projection_weight = noise(splits[6], (MODEL_WIDTH, HIDDEN_UNITS), MODEL_WIDTH ** -0.5, 0.15625, ((0, 8), (1, 4)))
    down_weight_transposed = noise(splits[7], (MODEL_WIDTH, HIDDEN_UNITS), HIDDEN_UNITS ** -0.5, 0.078125, ((0, 8), (1, 4)))
    adapter_input_factor = noise(splits[8], (MODEL_WIDTH, LOW_RANK_SIZE), MODEL_WIDTH ** -0.5, 0.15625)
    adapter_output_factor = noise(splits[9], (LOW_RANK_SIZE, HIDDEN_UNITS), LOW_RANK_SIZE ** -0.5, 0.75, ((1, 4),))
    return {"tokens": tokens, "targets": targets, "modulation": modulation, "live_block_count": live_block_count, "preferred_blocks": preferred_blocks, "last_block_rows": last_block_rows, "up_projection_weight": up_projection_weight, "down_weight_transposed": down_weight_transposed, "adapter_input_factor": adapter_input_factor, "adapter_output_factor": adapter_output_factor}


EPS = 1e-06
BETA = 20.0
LOSS_SCALE = 4096.0

def settle_gradients(value):
    return lax.optimization_barrier(value.astype(jnp.bfloat16)).astype(jnp.float32)

def layer_norm(image_blocks):
    wide = image_blocks.astype(jnp.float32)
    center = wide - lax.optimization_barrier(jnp.mean(wide, axis=-1, keepdims=True))
    inverse_deviation = lax.rsqrt(lax.optimization_barrier(jnp.mean(center * center, axis=-1, keepdims=True)) + EPS)
    return (center * inverse_deviation, inverse_deviation)

def gelu_and_slope(pre):

    def act(value):
        return jax.nn.gelu(value, approximate=True)
    value, back = jax.vjp(act, pre)
    return (value, back(jnp.ones_like(pre))[0])

def contract_trailing(left, right):
    return lax.dot_general(left, right, (((1,), (1,)), ((), ())), preferred_element_type=jnp.float32)

def device_partial_sum(left, right):
    group = left.shape[1] // N_TENSOR
    total = jnp.zeros((left.shape[0], right.shape[0]), jnp.float32)
    for part in range(N_TENSOR):
        total = total + settle_gradients(contract_trailing(left[:, part * group:(part + 1) * group], right[:, part * group:(part + 1) * group]))
    return total

def slot_layout(live_block_count, preferred_blocks, last_block_rows):
    slots = jnp.arange(CAP, dtype=jnp.int32)[None, :]
    count = live_block_count[:, None]
    wins = preferred_blocks[:, None]
    flags = (slots >= wins).astype(jnp.int32)
    last = jnp.where(flags == 0, wins - 1, count - 1)
    tail = jnp.where(flags == 0, last_block_rows[:, 0:1], last_block_rows[:, 1:2])
    live = jnp.where(slots < count, jnp.where(slots == last, tail, BLK), 0)
    masks = (jnp.arange(BLK, dtype=jnp.int32)[None, None, :] < live[:, :, None]).astype(jnp.float32)
    return (flags, live, masks)

def forward_pass(image_blocks, modulation_slots, up_projection_weight, down_weight_transposed, adapter_input_factor, adapter_output_factor):
    modulation_vectors = modulation_slots.astype(jnp.float32)
    shift = modulation_vectors[:, None, 0]
    modulation_scale = 1.0 + modulation_vectors[:, None, 1]
    output_gate = modulation_vectors[:, None, 2]
    normalized_input, inverse_deviation = layer_norm(image_blocks)
    count_rows = image_blocks.shape[0] * image_blocks.shape[1]
    modulated_input = (normalized_input * modulation_scale + shift).astype(jnp.bfloat16).reshape(count_rows, image_blocks.shape[2])
    low_rank_hidden = jnp.dot(modulated_input, adapter_input_factor, preferred_element_type=jnp.float32).astype(jnp.bfloat16)
    reference_preactivation = jnp.dot(modulated_input, up_projection_weight, preferred_element_type=jnp.float32)
    policy_preactivation = reference_preactivation + jnp.dot(low_rank_hidden, adapter_output_factor, preferred_element_type=jnp.float32)
    act_pol, policy_activation_slope = gelu_and_slope(policy_preactivation)
    hid_pol = act_pol.astype(jnp.bfloat16)
    hid_ref = jax.nn.gelu(reference_preactivation, approximate=True).astype(jnp.bfloat16)
    sum_pol = device_partial_sum(hid_pol, down_weight_transposed).reshape(image_blocks.shape)
    sum_ref = device_partial_sum(hid_ref, down_weight_transposed).reshape(image_blocks.shape)
    wide = image_blocks.astype(jnp.float32)
    return (normalized_input, inverse_deviation, modulation_scale, output_gate, modulated_input, low_rank_hidden, policy_activation_slope, wide + output_gate * sum_pol, wide + output_gate * sum_ref)

def reference(tokens, targets, modulation, live_block_count, preferred_blocks, last_block_rows, up_projection_weight, down_weight_transposed, adapter_input_factor, adapter_output_factor):
    flags, live, masks = slot_layout(live_block_count, preferred_blocks, last_block_rows)
    token_blocks = tokens.reshape(N_DP, CAP, BLK, MODEL_WIDTH)
    target_blocks = targets.reshape(N_DP, CAP, BLK, MODEL_WIDTH)
    mod_pairs = modulation.reshape(N_DP, 2, 3, MODEL_WIDTH)
    modulation_slots = jnp.where(flags[:, :, None, None] == 0, mod_pairs[:, 0:1], mod_pairs[:, 1:2])

    def errors(item):
        image_blocks, goals, modulation_vectors, mask = item
        step_result = forward_pass(image_blocks, modulation_vectors, up_projection_weight, down_weight_transposed, adapter_input_factor, adapter_output_factor)
        goal = goals.astype(jnp.float32)
        miss_pol = step_result[7] - goal
        miss_ref = step_result[8] - goal
        return (lax.optimization_barrier(jnp.sum(mask[:, :, None] * miss_pol * miss_pol, axis=(1, 2))), lax.optimization_barrier(jnp.sum(mask[:, :, None] * miss_ref * miss_ref, axis=(1, 2))))
    err_pol, err_ref = lax.map(errors, (token_blocks, target_blocks, modulation_slots, masks))
    ids = (2 * jnp.arange(N_DP, dtype=jnp.int32)[:, None] + flags).reshape(-1)
    picks = (ids[:, None] == jnp.arange(2 * N_DP, dtype=jnp.int32)[None, :]).astype(jnp.float32)
    tot_pol = lax.optimization_barrier(jnp.sum(err_pol.reshape(-1)[:, None] * picks, axis=0))
    tot_ref = lax.optimization_barrier(jnp.sum(err_ref.reshape(-1)[:, None] * picks, axis=0))
    rows_of = lax.optimization_barrier(jnp.sum(live.reshape(-1)[:, None].astype(jnp.float32) * picks, axis=0))
    scale_rows = 1.0 / (MODEL_WIDTH * rows_of)
    pair_gap = ((tot_pol - tot_ref) * scale_rows).reshape(N_DP, 2)
    inside = -BETA * (pair_gap[:, 0] - pair_gap[:, 1])
    losses = jax.nn.softplus(-inside)
    weight = BETA * LOSS_SCALE * jax.nn.sigmoid(-inside)
    coef = jnp.stack([weight, -weight], axis=1).reshape(2 * N_DP) * scale_rows
    slot_coef = coef[ids].reshape(N_DP, CAP)

    def backward(carry, item):
        image_blocks, goals, modulation_vectors, mask, factor = item
        normalized_input, inverse_deviation, modulation_scale, output_gate, modulated_input, low_rank_hidden, policy_activation_slope, policy_output, ignored_value = forward_pass(image_blocks, modulation_vectors, up_projection_weight, down_weight_transposed, adapter_input_factor, adapter_output_factor)
        out_grad = factor[:, None, None] * 2.0 * mask[:, :, None] * (policy_output - goals.astype(jnp.float32))
        count_rows = image_blocks.shape[0] * image_blocks.shape[1]
        dy = (output_gate * out_grad).astype(jnp.bfloat16).reshape(count_rows, MODEL_WIDTH)
        dh = jnp.dot(dy, down_weight_transposed, preferred_element_type=jnp.float32)
        preactivation_gradient = (dh * policy_activation_slope).astype(jnp.bfloat16)
        grad_b = lax.dot_general(low_rank_hidden, preactivation_gradient, (((0,), (0,)), ((), ())), preferred_element_type=jnp.float32)
        low_rank_gradient = device_partial_sum(preactivation_gradient, adapter_output_factor).astype(jnp.bfloat16)
        modulation_gradient = device_partial_sum(preactivation_gradient, up_projection_weight) + contract_trailing(low_rank_gradient, adapter_input_factor)
        dn = modulation_gradient.reshape(image_blocks.shape) * modulation_scale
        back = inverse_deviation * (dn - lax.optimization_barrier(jnp.sum(dn, axis=-1, keepdims=True)) / MODEL_WIDTH - normalized_input * lax.optimization_barrier(jnp.sum(dn * normalized_input, axis=-1, keepdims=True)) / MODEL_WIDTH)
        grad = (out_grad + back).astype(jnp.bfloat16)
        grad_a = lax.dot_general(modulated_input, low_rank_gradient, (((0,), (0,)), ((), ())), preferred_element_type=jnp.float32)
        return ((carry[0] + grad_a, carry[1] + grad_b), grad)
    start = (jnp.zeros((MODEL_WIDTH, LOW_RANK_SIZE), jnp.float32), jnp.zeros((LOW_RANK_SIZE, HIDDEN_UNITS), jnp.float32))
    totals, grads = lax.scan(backward, start, (token_blocks, target_blocks, modulation_slots, masks, slot_coef))
    return (losses, grads.reshape(N_DP * CAP * BLK, MODEL_WIDTH), totals[0] / N_DP, totals[1] / N_DP)
```

```python
import jax
import jax.numpy as jnp
from jax import lax
from jax.experimental import pallas as pl
from jax.experimental.pallas import tpu as pltpu
from jax.sharding import PartitionSpec as P

BLK = 64
CAP = 4


EPS = 1e-06
BETA = 20.0
LOSS_SCALE = 4096.0


def settle_gradients(value):
    return lax.optimization_barrier(value.astype(jnp.bfloat16)).astype(jnp.float32)


def layer_norm(image_blocks):
    wide = image_blocks.astype(jnp.float32)
    center = wide - jnp.mean(wide, axis=-1, keepdims=True)
    inverse_deviation = lax.rsqrt(jnp.mean(center * center, axis=-1, keepdims=True) + EPS)
    return (center * inverse_deviation, inverse_deviation)


def gelu_and_slope(pre):

    def act(value):
        return jax.nn.gelu(value, approximate=True)

    value, back = jax.vjp(act, pre)
    return (value, back(jnp.ones_like(pre))[0])


def contract_trailing(left, right):
    return lax.dot_general(
        left, right, (((1,), (1,)), ((), ())), preferred_element_type=jnp.float32
    )


def contract_first(left, right):
    return lax.dot_general(
        left, right, (((0,), (0,)), ((), ())), preferred_element_type=jnp.float32
    )


def slot_state(live_block_count, preferred_blocks, last_block_rows):
    count = live_block_count[0]
    wins = preferred_blocks[0]
    slots = jnp.arange(CAP, dtype=jnp.int32)
    flags = (slots >= wins).astype(jnp.int32)
    last = jnp.where(flags == 0, wins - 1, count - 1)
    tail = jnp.where(flags == 0, last_block_rows[0, 0], last_block_rows[0, 1])
    live = jnp.where(slots < count, jnp.where(slots == last, tail, BLK), 0)
    masks = (jnp.arange(BLK, dtype=jnp.int32)[None, :] < live[:, None]).astype(jnp.float32)
    own_counts = jnp.stack(
        [jnp.sum(jnp.where(flags == 0, live, 0)), jnp.sum(jnp.where(flags == 1, live, 0))]
    ).astype(jnp.float32)
    return flags, masks, own_counts


def per_device(
    tokens,
    targets,
    modulation,
    live_block_count,
    preferred_blocks,
    last_block_rows,
    up_projection_weight,
    down_weight_transposed,
    adapter_input_factor,
    adapter_output_factor,
):
    width = tokens.shape[1]
    n_dp = lax.axis_size("dp")
    here = lax.axis_index("dp")
    flags, masks, own_counts = slot_state(live_block_count, preferred_blocks, last_block_rows)
    blocks_x = tokens.reshape(CAP, BLK, width)
    blocks_t = targets.reshape(CAP, BLK, width)
    blocks_mod = jnp.where(flags[:, None, None] == 0, modulation[0][None], modulation[1][None])
    homes = jnp.full((CAP,), here, jnp.int32)
    work_x, work_t, work_mod = (blocks_x, blocks_t, blocks_mod)
    work_mask, work_flag, work_home = (masks, flags, homes)
    spots = work_x.shape[0]
    count_rows = spots * BLK
    samples = 2 * n_dp
    ids = work_home * 2 + work_flag
    picks = (ids[:, None] == jnp.arange(samples, dtype=jnp.int32)[None, :]).astype(jnp.float32)
    modulation_vectors = work_mod.astype(jnp.float32)
    shift = modulation_vectors[:, None, 0]
    modulation_scale = 1.0 + modulation_vectors[:, None, 1]
    output_gate = modulation_vectors[:, None, 2]
    normalized_input, inverse_deviation = layer_norm(work_x)
    modulated_input = (
        (normalized_input * modulation_scale + shift)
        .astype(jnp.bfloat16)
        .reshape(count_rows, width)
    )
    w_up, w_down = (
        lax.all_gather(up_projection_weight, "dp", axis=0, tiled=True),
        lax.all_gather(down_weight_transposed, "dp", axis=0, tiled=True),
    )
    low_rank_hidden = jnp.dot(
        modulated_input, adapter_input_factor, preferred_element_type=jnp.float32
    ).astype(jnp.bfloat16)
    reference_preactivation = jnp.dot(modulated_input, w_up, preferred_element_type=jnp.float32)
    policy_preactivation = reference_preactivation + jnp.dot(
        low_rank_hidden, adapter_output_factor, preferred_element_type=jnp.float32
    )
    act_pol, policy_activation_slope = gelu_and_slope(policy_preactivation)
    hid_pol = act_pol.astype(jnp.bfloat16)
    hid_ref = jax.nn.gelu(reference_preactivation, approximate=True).astype(jnp.bfloat16)
    part_pol = settle_gradients(contract_trailing(hid_pol, w_down))
    part_ref = settle_gradients(contract_trailing(hid_ref, w_down))
    sum_pol, sum_ref = (
        lax.psum(part_pol.astype(jnp.bfloat16), "tensor").astype(jnp.float32),
        lax.psum(part_ref.astype(jnp.bfloat16), "tensor").astype(jnp.float32),
    )
    x_part = work_x.astype(jnp.float32)
    t_part = work_t.astype(jnp.float32)
    wmask = work_mask[:, :, None]
    miss_pol = x_part + output_gate * sum_pol.reshape(spots, BLK, width) - t_part
    miss_ref = x_part + output_gate * sum_ref.reshape(spots, BLK, width) - t_part
    vec_pol = jnp.sum(jnp.sum(wmask * miss_pol * miss_pol, axis=(1, 2))[:, None] * picks, axis=0)
    vec_ref = jnp.sum(jnp.sum(wmask * miss_ref * miss_ref, axis=(1, 2))[:, None] * picks, axis=0)
    owned = (jnp.arange(samples, dtype=jnp.int32) // 2 == here).astype(jnp.float32) * jnp.tile(
        own_counts, n_dp
    )
    tot_pol, tot_ref, tot_rows = lax.psum((vec_pol, vec_ref, owned), "dp")
    scale_rows = 1.0 / (width * tot_rows)
    pair_gap = ((tot_pol - tot_ref) * scale_rows).reshape(n_dp, 2)
    inside = -BETA * (pair_gap[:, 0] - pair_gap[:, 1])
    losses = lax.dynamic_slice_in_dim(jax.nn.softplus(-inside), here, 1)
    weight = BETA * LOSS_SCALE * jax.nn.sigmoid(-inside)
    coef = jnp.stack([weight, -weight], axis=1).reshape(samples) * scale_rows
    slot_coef = jnp.sum(picks * coef[None, :], axis=1)
    out_grad = slot_coef[:, None, None] * 2.0 * wmask * miss_pol
    dy_part = (output_gate * out_grad).astype(jnp.bfloat16).reshape(count_rows, width)
    dh = jnp.dot(dy_part, w_down, preferred_element_type=jnp.float32)
    preactivation_gradient = (dh * policy_activation_slope).astype(jnp.bfloat16)
    grad_b = contract_first(low_rank_hidden, preactivation_gradient)
    low_rank_gradient_piece = settle_gradients(
        contract_trailing(preactivation_gradient, adapter_output_factor)
    )
    dm_part = settle_gradients(contract_trailing(preactivation_gradient, w_up))
    modulation_gradient_sum, dlow_sum = (
        lax.psum(dm_part.astype(jnp.bfloat16), "tensor").astype(jnp.float32),
        lax.psum(low_rank_gradient_piece.astype(jnp.bfloat16), "tensor").astype(jnp.float32),
    )
    low_rank_gradient = dlow_sum.astype(jnp.bfloat16)
    modulation_gradient = modulation_gradient_sum + contract_trailing(
        low_rank_gradient, adapter_input_factor
    )
    dn = modulation_gradient.reshape(spots, BLK, width) * modulation_scale
    first_sum = jnp.sum(dn, axis=-1, keepdims=True)
    second_sum = jnp.sum(dn * normalized_input, axis=-1, keepdims=True)
    back_part = inverse_deviation * (dn - first_sum / width - normalized_input * second_sum / width)
    grad_part = (out_grad + back_part).astype(jnp.bfloat16)
    grad_a = contract_first(modulated_input, low_rank_gradient)
    sum_a, sum_b = lax.psum((grad_a, grad_b), "dp")
    return (losses, grad_part.reshape(CAP * BLK, width), sum_a / n_dp, sum_b / n_dp)


MESH = pl.DeviceIdType.MESH
F32 = jnp.float32
BF16 = jnp.bfloat16
SIDE = 32
TILE = 384
PAD = 128
GELU_ROOT = 0.7978845608028654
GELU_CUBE = 0.044715


def activation(pre, want_slope):
    square = pre * pre
    bend = jnp.tanh(GELU_ROOT * pre * (1.0 + GELU_CUBE * square))
    half = 0.5 * (1.0 + bend)
    if not want_slope:
        return pre * half
    slope = half + 0.5 * pre * (1.0 - bend * bend) * GELU_ROOT * (1.0 + 3.0 * GELU_CUBE * square)
    return pre * half, slope


def step_kernel(
    x_ref, t_ref, mod_ref, mask_ref, flag_ref, inv_ref, up_ref, dn_ref, at_ref, b_ref,
    u_ref, grad_ref, ga_ref, gb_ref,
    w_ref, modded, low_ref, lowt_ref, slope_ref, hid_ref,
    ypart, crecv, ysend, yrecv, ysum, miss_ref, vbuf, ebuf, cf_ref,
    dpre_ref, dmpart, dmc, dmsend, dmrecv, dmsum,
    dlpart, dlc, dlsend, dlrecv, dlsum,
    gat, gatr, gap, gapr, gbp, gbr,
    z_send, z_recv, x_send, x_recv, c_send, c_recv, y_send, y_recv, v_send, v_recv,
    e_send, e_recv, dc_send, dc_recv, dy_send, dy_recv, g_send, g_recv,
    at_send, at_recv, rs_send, rs_recv, ag_send, ag_recv, tg_send, tg_recv,
):
    d = lax.axis_index("dp")
    t = lax.axis_index("tensor")
    z, x = d // 2, d % 2
    y, core = t // 2, t % 2
    high = z // 2
    middle = (z + high) % 2
    base = [middle, 1 - middle, 2, 3]
    place = [p + high * (3 - 2 * p) for p in base]
    inner = ((z + 1 - 2 * high) * 2 + x, t)
    edge_z = z - 1 + 2 * high
    edge = ((edge_z * middle + (1 - middle) * (z + 1 - 2 * high)) * 2 + x, t)
    across = (z * 2 + 1 - x, t)
    t_core = y * 2 + 1 - core
    t_y = (1 - y) * 2 + core
    t_far = (1 - y) * 2 + 1 - core
    mate = (d, t_core)
    over = (d, t_y)
    far = (d, t_far)
    peers = [mate, over, far]
    is_middle = middle == 1

    barrier = pltpu.get_barrier_semaphore()
    for k in range(1, 8):
        pl.semaphore_signal(barrier, inc=1, device_id=((d + k) % 8, t), device_id_type=MESH)
    for peer in peers:
        pl.semaphore_signal(barrier, inc=1, device_id=peer, device_id_type=MESH)

    shard = up_ref.shape[0]
    main = shard - SIDE
    w_ref[0, pl.ds(d * shard, shard), :] = up_ref[...]
    w_ref[1, pl.ds(d * shard, shard), :] = dn_ref[...]
    pl.semaphore_wait(barrier, 10)

    def copy(src, dst, send, recv, device):
        return pltpu.make_async_remote_copy(
            src_ref=src, dst_ref=dst, send_sem=send, recv_sem=recv,
            device_id=device, device_id_type=MESH)

    def rows(m, kind, slot):
        if kind == 0:
            return w_ref.at[m, pl.ds((place[slot] * 2 + x) * shard, shard), :]
        return w_ref.at[m, pl.ds((place[slot] * 2 + 1 - x) * shard + main, SIDE), :]

    def x_rows(m, slot, column):
        if slot == 4:
            return w_ref.at[m, pl.ds((place[0] * 2 + column) * shard + main, SIDE), :]
        return w_ref.at[m, pl.ds((place[slot] * 2 + column) * shard, main), :]

    def z_copy(m, kind, which):
        slot = [0, 0, 1, 2, 3][which]
        target = [1 + middle, 1, 3, 2, 3][which]
        device = inner if which in (0, 2) else edge
        ref = rows(m, kind, slot)
        return copy(ref, ref, z_send.at[m, kind, which], z_recv.at[m, kind, target], device)

    def z_arrive(m, kind, slot):
        ref = rows(m, kind, slot)
        copy(ref, ref, z_send.at[m, kind, 0], z_recv.at[m, kind, slot], inner).wait_recv()

    def x_copy(m, slot):
        ref = x_rows(m, slot, x)
        return copy(ref, ref, x_send.at[m, slot], x_recv.at[m, slot], across)

    def x_arrive(m, slot):
        ref = x_rows(m, slot, 1 - x)
        copy(ref, ref, x_send.at[m, slot], x_recv.at[m, slot], across).wait_recv()

    def begin(m):
        z_copy(m, 0, 0).start()

        @pl.when(is_middle)
        def _():
            z_copy(m, 0, 1).start()

        x_copy(m, 4).start()
        x_copy(m, 0).start()

    def side_begin(m):
        x_arrive(m, 4)
        z_copy(m, 1, 0).start()

        @pl.when(is_middle)
        def _():
            z_copy(m, 1, 1).start()

    def relay(m, slot):
        z_arrive(m, 0, slot)

        @pl.when(is_middle)
        def _():
            z_copy(m, 0, slot + 1).start()

        x_copy(m, slot).start()

    def side_relay(m, slot):
        z_arrive(m, 1, slot)

        @pl.when(is_middle)
        def _():
            z_copy(m, 1, slot + 1).start()

    begin(0)

    def norm(block, b):
        wide = x_ref[block, :].astype(F32)
        center = wide - jnp.mean(wide, axis=-1, keepdims=True)
        inverse = lax.rsqrt(jnp.mean(center * center, axis=-1, keepdims=True) + EPS)
        vectors = mod_ref[b]
        return wide, center * inverse, inverse, vectors[0:1], 1.0 + vectors[1:2], vectors[2:3]

    @pl.loop(0, CAP)
    def _(b):
        block = pl.ds(b * BLK, BLK)
        _, normed, _, shift, scale, _ = norm(block, b)
        modded[block, :] = (normed * scale + shift).astype(BF16)

    low_ref[...] = contract_trailing(modded[...], at_ref[...]).astype(BF16)
    lowt_ref[...] = contract_trailing(at_ref[...], modded[...]).astype(BF16)

    side_begin(0)
    relay(0, 1)
    relay(0, 2)
    begin(1)
    side_relay(0, 1)
    side_relay(0, 2)
    relay(0, 3)
    side_begin(1)
    side_relay(0, 3)
    for slot in range(4):
        x_arrive(0, slot)

    @pl.loop(0, 4)
    def _(n):
        cols = pl.ds(pl.multiple_of(n * TILE, TILE), TILE)
        pre = jnp.dot(modded[...], w_ref[0, :, cols], preferred_element_type=F32)
        hid_ref[1, :, cols] = activation(pre, False).astype(BF16)
        pol = pre + jnp.dot(low_ref[...], b_ref[:, cols], preferred_element_type=F32)
        act, slope = activation(pol, True)
        hid_ref[0, :, cols] = act.astype(BF16)
        slope_ref[:, cols] = slope

    def y_core(j):
        src = ypart.at[j, 1 - core]
        return copy(src, crecv.at[j], c_send.at[j], c_recv.at[j], mate)

    def y_over(j):
        return copy(ysend.at[j], yrecv.at[j], y_send.at[j], y_recv.at[j], over)

    def v_copy(j, which):
        if which == 2:
            ref = vbuf.at[j, t_y]
        else:
            ref = vbuf.at[j, t]
        device = over if which == 1 else mate
        return copy(ref, ref, v_send.at[j, which], v_recv.at[j, which], device)

    def v_arrive(j, which):
        ref = vbuf.at[j, [t_core, t_y, t_far][which]]
        copy(ref, ref, v_send.at[j, which], v_recv.at[j, which], mate).wait_recv()

    def columns(j):
        return pl.ds(pl.multiple_of(place[j] * TILE, TILE), TILE)

    def stage_product(j):
        @pl.loop(0, 2)
        def _(p):
            part = contract_trailing(hid_ref[p], w_ref[1, pl.ds(place[j] * TILE, TILE), :])
            part = part.astype(BF16)
            for b in range(CAP):
                ypart[j, b % 2, b // 2, p] = part[b * BLK:(b + 1) * BLK, :]
        y_core(j).start()

    def stage_pair(j):
        y_core(j).wait_recv()
        ysend[j] = (ypart[j, core, 1 - y].astype(F32) + crecv[j, 1 - y].astype(F32)).astype(BF16)
        y_over(j).start()
        ysum[j] = ypart[j, core, y].astype(F32) + crecv[j, y].astype(F32)

    own = pl.ds(t * BLK, BLK)

    def stage_total(j):
        y_over(j).wait_recv()
        cols = columns(j)
        total = ysum[j] + yrecv[j].astype(F32)
        gate = mod_ref[t, 2:3, cols]
        residual = x_ref[own, cols].astype(F32) - t_ref[own, cols].astype(F32)
        mask = mask_ref[own, :]
        miss = residual + gate * total[0]
        miss_ref2 = residual + gate * total[1]
        slope = 2.0 * mask * miss
        miss_ref[:, cols] = slope
        vbuf[j, t] = (gate * slope).astype(BF16)
        v_copy(j, 0).start()
        v_copy(j, 1).start()
        err = jnp.concatenate([
            jnp.sum(mask * miss * miss, axis=(0, 1), keepdims=True),
            jnp.sum(mask * miss_ref2 * miss_ref2, axis=(0, 1), keepdims=True)], axis=0)
        return jnp.broadcast_to(err, (2, PAD))

    def stage_share(j):
        v_arrive(j, 1)
        v_copy(j, 2).start()

    def ready(j):
        x_arrive(1, j)
        if j > 0:
            side_relay(1, j)

    relay(1, 1)
    ready(0)
    stage_product(0)
    stage_pair(0)
    relay(1, 2)
    ready(1)
    stage_product(1)
    stage_pair(1)
    relay(1, 3)
    err = stage_total(0)
    ready(2)
    stage_product(2)
    stage_pair(2)
    err = err + stage_total(1)
    stage_share(0)
    ready(3)
    stage_product(3)
    stage_pair(3)
    err = err + stage_total(2)
    stage_share(1)
    err = err + stage_total(3)
    ebuf[t, 0:2, :] = err
    ebuf[t, 2:8, :] = jnp.zeros((6, PAD), F32)

    def e_copy(k):
        ref = ebuf.at[t]
        return copy(ref, ref, e_send.at[k], e_recv.at[k], peers[k])

    for k in range(3):
        e_copy(k).start()
    stage_share(2)
    stage_share(3)
    for k, peer in enumerate(peers):
        ref = ebuf.at[peer[1]]
        copy(ref, ref, e_send.at[k], e_recv.at[k], peer).wait_recv()
    wins = jnp.zeros((1, PAD), F32)
    loses = jnp.zeros((1, PAD), F32)
    for b in range(CAP):
        drop = ebuf[b, 0:1, :] - ebuf[b, 1:2, :]
        loser = flag_ref[b:b + 1, :]
        wins = wins + (1.0 - loser) * drop
        loses = loses + loser * drop
    inv_w, inv_l = inv_ref[0:1, :], inv_ref[1:2, :]
    outside = BETA * (wins * inv_w - loses * inv_l)
    u_ref[...] = jnp.broadcast_to(outside, u_ref.shape)
    weight = BETA * LOSS_SCALE / (1.0 + jnp.exp(-outside))
    loser = flag_ref[...]
    cf_ref[...] = weight * ((1.0 - loser) * inv_w - loser * inv_l)

    for j in range(4):
        v_arrive(j, 0)
        v_arrive(j, 2)

    @pl.loop(0, 4)
    def _(n):
        cols = pl.ds(pl.multiple_of(n * TILE, TILE), TILE)
        dh = jnp.zeros((CAP * BLK, TILE), F32)
        for j in range(4):
            dy = vbuf[j].reshape(CAP * BLK, TILE)
            dh = dh + jnp.dot(dy, w_ref[1, pl.ds(place[j] * TILE, TILE), cols],
                              preferred_element_type=F32)
        for b in range(CAP):
            block = slice(b * BLK, (b + 1) * BLK)
            dpre_ref[block, cols] = (
                dh[block] * (cf_ref[b:b + 1, 0:1] * slope_ref[block, cols])).astype(BF16)

    def dl_core():
        return copy(dlpart.at[1 - core], dlc, dc_send.at[4], dc_recv.at[4], mate)

    def dl_over():
        return copy(dlsend, dlrecv, dy_send.at[4], dy_recv.at[4], over)

    def dm_core(n):
        return copy(dmpart.at[n, 1 - core], dmc.at[n], dc_send.at[n], dc_recv.at[n], mate)

    def dm_over(n):
        return copy(dmsend.at[n], dmrecv.at[n], dy_send.at[n], dy_recv.at[n], over)

    dlow = contract_trailing(dpre_ref[...], b_ref[...]).astype(BF16)
    for b in range(CAP):
        dlpart[b % 2, b // 2] = dlow[b * BLK:(b + 1) * BLK, :]
    dl_core().start()

    @pl.loop(0, 4)
    def _(n):
        part = contract_trailing(
            dpre_ref[...], w_ref[0, pl.ds(pl.multiple_of(n * TILE, TILE), TILE), :]).astype(BF16)
        for b in range(CAP):
            dmpart[n, b % 2, b // 2] = part[b * BLK:(b + 1) * BLK, :]
        dm_core(n).start()

    dlowt = contract_trailing(b_ref[...], dpre_ref[...]).astype(BF16)
    ga = jnp.dot(dlowt, modded[...], preferred_element_type=F32).astype(BF16)
    for k in range(4):
        gat[k] = ga[k * 16:(k + 1) * 16, :]

    def at_copy(k):
        return copy(gat.at[peers[k][1]], gatr.at[k], at_send.at[k], at_recv.at[k], peers[k])

    for k in range(3):
        at_copy(k).start()
    for n in range(4):
        dm_core(n).wait_recv()
        dmsend[n] = (dmpart[n, core, 1 - y].astype(F32) + dmc[n, 1 - y].astype(F32)).astype(BF16)
        dm_over(n).start()
        dmsum[n] = dmpart[n, core, y].astype(F32) + dmc[n, y].astype(F32)
    dl_core().wait_recv()
    dlsend[...] = (dlpart[core, 1 - y].astype(F32) + dlc[1 - y].astype(F32)).astype(BF16)
    dl_over().start()
    dlsum[...] = dlpart[core, y].astype(F32) + dlc[y].astype(F32)

    gb = jnp.dot(lowt_ref[...], dpre_ref[...], preferred_element_type=F32).astype(BF16)
    half = gb.shape[1] // 2
    for k in range(8):
        gbp[k] = gb[(k // 2) * 16:(k // 2 + 1) * 16, (k % 2) * half:(k % 2 + 1) * half]

    def rs_copy(which, k):
        to = (d + k) % 8
        part, land = ((gap, gapr), (gbp, gbr))[which]
        return copy(part.at[to], land.at[k], rs_send.at[which, k], rs_recv.at[which, k], (to, t))

    def ag_copy(which, k):
        to = (d + k) % 8
        ref = ga_ref.at[t, d] if which == 0 else gb_ref.at[d]
        return copy(ref, ref, ag_send.at[which, k], ag_recv.at[which, k], (to, t))

    def ag_arrive(which, k):
        source = (d + 8 - k) % 8
        ref = ga_ref.at[t, source] if which == 0 else gb_ref.at[source]
        copy(ref, ref, ag_send.at[which, k], ag_recv.at[which, k], (source, t)).wait_recv()

    for k in range(1, 8):
        rs_copy(1, k).start()
    total = gat[t].astype(F32)
    for k in range(3):
        at_copy(k).wait_recv()
        total = total + gatr[k].astype(F32)
    total = total.astype(BF16)
    wide = total.shape[1] // 8
    for k in range(8):
        gap[k] = total[:, k * wide:(k + 1) * wide]
    for k in range(1, 8):
        rs_copy(0, k).start()

    _, normed, inverse, _, scale, _ = norm(own, t)
    dl_over().wait_recv()
    dlow = (dlsum[...] + dlrecv[...].astype(F32)).astype(BF16)
    for n in range(4):
        dm_over(n).wait_recv()
    dm = jnp.concatenate([dmsum[n] + dmrecv[n].astype(F32) for n in range(4)], axis=1)
    dm = dm + jnp.dot(dlow, at_ref[...], preferred_element_type=F32)
    dn = dm * scale
    first = jnp.mean(dn, axis=-1, keepdims=True)
    second = jnp.mean(dn * normed, axis=-1, keepdims=True)
    out_grad = cf_ref[pl.ds(t, 1), 0:1] * miss_ref[...]
    grad_ref[t] = (out_grad + inverse * (dn - first - normed * second)).astype(BF16)

    def g_copy(which):
        ref = grad_ref.at[t_y] if which == 2 else grad_ref.at[t]
        return copy(ref, ref, g_send.at[which], g_recv.at[which], over if which == 1 else mate)

    def g_arrive(which):
        ref = grad_ref.at[[t_core, t_y, t_far][which]]
        copy(ref, ref, g_send.at[which], g_recv.at[which], mate).wait_recv()

    g_copy(1).start()
    g_copy(0).start()

    for which, (part, land) in ((1, (gbp, gbr)), (0, (gap, gapr))):
        total = part[d].astype(F32)
        for k in range(1, 8):
            rs_copy(which, k).wait_recv()
            total = total + land[k].astype(F32)
        if which == 1:
            gb_ref[d] = total.astype(BF16)
        else:
            ga_ref[t, d] = total.astype(BF16)
        for k in range(1, 8):
            ag_copy(which, k).start()

    g_arrive(1)
    g_copy(2).start()
    for k in range(1, 8):
        ag_arrive(0, k)

    def tg_copy(k):
        ref = ga_ref.at[t]
        return copy(ref, ref, tg_send.at[k], tg_recv.at[k], peers[k])

    for k in range(3):
        tg_copy(k).start()
    for k in range(1, 8):
        ag_arrive(1, k)
    g_arrive(0)
    g_arrive(2)
    for k, peer in enumerate(peers):
        ref = ga_ref.at[peer[1]]
        copy(ref, ref, tg_send.at[k], tg_recv.at[k], peer).wait_recv()

    for m in range(2):
        for slot in range(5):
            x_copy(m, slot).wait_send()
        for kind in range(2):
            z_copy(m, kind, 0).wait_send()

            @pl.when(is_middle)
            def _():
                for which in range(1, 5):
                    z_copy(m, kind, which).wait_send()
    for j in range(4):
        y_core(j).wait_send()
        y_over(j).wait_send()
        dm_core(j).wait_send()
        dm_over(j).wait_send()
        for which in range(3):
            v_copy(j, which).wait_send()
    dl_core().wait_send()
    dl_over().wait_send()
    for k in range(3):
        e_copy(k).wait_send()
        at_copy(k).wait_send()
        g_copy(k).wait_send()
        tg_copy(k).wait_send()
    for which in range(2):
        for k in range(1, 8):
            rs_copy(which, k).wait_send()
            ag_copy(which, k).wait_send()


def fused_device(
    tokens, targets, modulation, live_block_count, preferred_blocks, last_block_rows,
    up_projection_weight, down_weight_transposed, adapter_input_factor, adapter_output_factor,
):
    width = tokens.shape[1]
    rank = adapter_input_factor.shape[1]
    hidden = adapter_output_factor.shape[1]
    flags, masks, own_counts = slot_state(live_block_count, preferred_blocks, last_block_rows)
    blocks_mod = jnp.where(
        flags[:, None, None] == 0, modulation[0][None], modulation[1][None]).astype(F32)
    mask_rows = masks.reshape(CAP * BLK, 1)
    flag_tile = jnp.zeros((8, PAD), F32).at[:CAP].set(flags.astype(F32)[:, None])
    inv_tile = jnp.zeros((8, PAD), F32).at[:2].set((1.0 / (width * own_counts))[:, None])
    a_rows = jnp.zeros((PAD, width), BF16).at[:rank].set(adapter_input_factor.T)
    b_rows = jnp.zeros((PAD, hidden), BF16).at[:rank].set(adapter_output_factor)
    dma = pltpu.SemaphoreType.DMA
    vm = pltpu.VMEM
    rows = CAP * BLK
    outs = pl.pallas_call(
        step_kernel,
        out_shape=(
            jax.ShapeDtypeStruct((8, PAD), F32),
            jax.ShapeDtypeStruct((CAP, BLK, width), BF16),
            jax.ShapeDtypeStruct((4, 8, 16, width // 8), BF16),
            jax.ShapeDtypeStruct((8, 16, hidden // 2), BF16),
        ),
        in_specs=[pl.BlockSpec(memory_space=pltpu.VMEM)] * 10,
        out_specs=(pl.BlockSpec(memory_space=pltpu.VMEM),) * 4,
        scratch_shapes=[
            vm((2, width, hidden), BF16),
            vm((rows, width), BF16),
            vm((rows, PAD), BF16),
            vm((PAD, rows), BF16),
            vm((rows, hidden), F32),
            vm((2, rows, hidden), BF16),
            vm((4, 2, 2, 2, BLK, TILE), BF16),
            vm((4, 2, 2, BLK, TILE), BF16),
            vm((4, 2, BLK, TILE), BF16),
            vm((4, 2, BLK, TILE), BF16),
            vm((4, 2, BLK, TILE), F32),
            vm((BLK, width), F32),
            vm((4, CAP, BLK, TILE), BF16),
            vm((CAP, 8, PAD), F32),
            vm((8, PAD), F32),
            vm((rows, hidden), BF16),
            vm((4, 2, 2, BLK, TILE), BF16),
            vm((4, 2, BLK, TILE), BF16),
            vm((4, BLK, TILE), BF16),
            vm((4, BLK, TILE), BF16),
            vm((4, BLK, TILE), F32),
            vm((2, 2, BLK, PAD), BF16),
            vm((2, BLK, PAD), BF16),
            vm((BLK, PAD), BF16),
            vm((BLK, PAD), BF16),
            vm((BLK, PAD), F32),
            vm((4, 16, width), BF16),
            vm((3, 16, width), BF16),
            vm((8, 16, width // 8), BF16),
            vm((8, 16, width // 8), BF16),
            vm((8, 16, hidden // 2), BF16),
            vm((8, 16, hidden // 2), BF16),
            dma((2, 2, 5)), dma((2, 2, 4)), dma((2, 5)), dma((2, 5)),
            dma((4,)), dma((4,)), dma((4,)), dma((4,)), dma((4, 3)), dma((4, 3)),
            dma((3,)), dma((3,)), dma((5,)), dma((5,)), dma((5,)), dma((5,)),
            dma((3,)), dma((3,)), dma((3,)), dma((3,)),
            dma((2, 8)), dma((2, 8)), dma((2, 8)), dma((2, 8)), dma((3,)), dma((3,)),
        ],
        compiler_params=pltpu.CompilerParams(
            collective_id=0, has_side_effects=True, vmem_limit_bytes=48 * 1024 * 1024),
    )(tokens, targets, blocks_mod, mask_rows, flag_tile, inv_tile,
      up_projection_weight, down_weight_transposed, a_rows, b_rows)
    outside, grad, ga, gb = outs
    losses = jax.nn.softplus(outside[0, :1])
    n_dp = lax.axis_size("dp")
    grad_a = ga.astype(F32).transpose(1, 3, 0, 2).reshape(width, rank) / n_dp
    grad_b = gb.astype(F32).reshape(4, 2, 16, hidden // 2).transpose(0, 2, 1, 3)
    return losses, grad.reshape(rows, width), grad_a, grad_b.reshape(rank, hidden) / n_dp


def fits_fused(mesh):
    return dict(mesh.shape) == {"dp": 8, "tensor": 4}


def solution(mesh):
    return jax.shard_map(
        fused_device if fits_fused(mesh) else per_device,
        mesh=mesh,
        in_specs=(
            P("dp", None),
            P("dp", None),
            P("dp", None, None),
            P("dp"),
            P("dp"),
            P("dp", None),
            P("dp", "tensor"),
            P("dp", "tensor"),
            P(),
            P(None, "tensor"),
        ),
        out_specs=(P("dp"), P("dp", None), P(), P(None, "tensor")),
        check_vma=False,
    )
```

```python
import jax
import jax.numpy as jnp
from jax import lax
from jax.experimental import pallas as pl
from jax.experimental.pallas import tpu as pltpu
from jax.sharding import PartitionSpec as P

BLK = 64
CAP = 4


EPS = 1e-06
BETA = 20.0
LOSS_SCALE = 4096.0


def settle_gradients(value):
    return lax.optimization_barrier(value.astype(jnp.bfloat16)).astype(jnp.float32)


def layer_norm(image_blocks):
    wide = image_blocks.astype(jnp.float32)
    center = wide - jnp.mean(wide, axis=-1, keepdims=True)
    inverse_deviation = lax.rsqrt(jnp.mean(center * center, axis=-1, keepdims=True) + EPS)
    return (center * inverse_deviation, inverse_deviation)


def gelu_and_slope(pre):

    def act(value):
        return jax.nn.gelu(value, approximate=True)

    value, back = jax.vjp(act, pre)
    return (value, back(jnp.ones_like(pre))[0])


def contract_trailing(left, right):
    return lax.dot_general(
        left, right, (((1,), (1,)), ((), ())), preferred_element_type=jnp.float32
    )


def contract_first(left, right):
    return lax.dot_general(
        left, right, (((0,), (0,)), ((), ())), preferred_element_type=jnp.float32
    )


def slot_state(live_block_count, preferred_blocks, last_block_rows):
    count = live_block_count[0]
    wins = preferred_blocks[0]
    slots = jnp.arange(CAP, dtype=jnp.int32)
    flags = (slots >= wins).astype(jnp.int32)
    last = jnp.where(flags == 0, wins - 1, count - 1)
    tail = jnp.where(flags == 0, last_block_rows[0, 0], last_block_rows[0, 1])
    live = jnp.where(slots < count, jnp.where(slots == last, tail, BLK), 0)
    masks = (jnp.arange(BLK, dtype=jnp.int32)[None, :] < live[:, None]).astype(jnp.float32)
    own_counts = jnp.stack(
        [jnp.sum(jnp.where(flags == 0, live, 0)), jnp.sum(jnp.where(flags == 1, live, 0))]
    ).astype(jnp.float32)
    return flags, masks, own_counts


def per_device(
    tokens,
    targets,
    modulation,
    live_block_count,
    preferred_blocks,
    last_block_rows,
    up_projection_weight,
    down_weight_transposed,
    adapter_input_factor,
    adapter_output_factor,
):
    width = tokens.shape[1]
    n_dp = lax.axis_size("dp")
    here = lax.axis_index("dp")
    flags, masks, own_counts = slot_state(live_block_count, preferred_blocks, last_block_rows)
    blocks_x = tokens.reshape(CAP, BLK, width)
    blocks_t = targets.reshape(CAP, BLK, width)
    blocks_mod = jnp.where(flags[:, None, None] == 0, modulation[0][None], modulation[1][None])
    homes = jnp.full((CAP,), here, jnp.int32)
    work_x, work_t, work_mod = (blocks_x, blocks_t, blocks_mod)
    work_mask, work_flag, work_home = (masks, flags, homes)
    spots = work_x.shape[0]
    count_rows = spots * BLK
    samples = 2 * n_dp
    ids = work_home * 2 + work_flag
    picks = (ids[:, None] == jnp.arange(samples, dtype=jnp.int32)[None, :]).astype(jnp.float32)
    modulation_vectors = work_mod.astype(jnp.float32)
    shift = modulation_vectors[:, None, 0]
    modulation_scale = 1.0 + modulation_vectors[:, None, 1]
    output_gate = modulation_vectors[:, None, 2]
    normalized_input, inverse_deviation = layer_norm(work_x)
    modulated_input = (
        (normalized_input * modulation_scale + shift)
        .astype(jnp.bfloat16)
        .reshape(count_rows, width)
    )
    w_up, w_down = (
        lax.all_gather(up_projection_weight, "dp", axis=0, tiled=True),
        lax.all_gather(down_weight_transposed, "dp", axis=0, tiled=True),
    )
    low_rank_hidden = jnp.dot(
        modulated_input, adapter_input_factor, preferred_element_type=jnp.float32
    ).astype(jnp.bfloat16)
    reference_preactivation = jnp.dot(modulated_input, w_up, preferred_element_type=jnp.float32)
    policy_preactivation = reference_preactivation + jnp.dot(
        low_rank_hidden, adapter_output_factor, preferred_element_type=jnp.float32
    )
    act_pol, policy_activation_slope = gelu_and_slope(policy_preactivation)
    hid_pol = act_pol.astype(jnp.bfloat16)
    hid_ref = jax.nn.gelu(reference_preactivation, approximate=True).astype(jnp.bfloat16)
    part_pol = settle_gradients(contract_trailing(hid_pol, w_down))
    part_ref = settle_gradients(contract_trailing(hid_ref, w_down))
    sum_pol, sum_ref = (
        lax.psum(part_pol.astype(jnp.bfloat16), "tensor").astype(jnp.float32),
        lax.psum(part_ref.astype(jnp.bfloat16), "tensor").astype(jnp.float32),
    )
    x_part = work_x.astype(jnp.float32)
    t_part = work_t.astype(jnp.float32)
    wmask = work_mask[:, :, None]
    miss_pol = x_part + output_gate * sum_pol.reshape(spots, BLK, width) - t_part
    miss_ref = x_part + output_gate * sum_ref.reshape(spots, BLK, width) - t_part
    vec_pol = jnp.sum(jnp.sum(wmask * miss_pol * miss_pol, axis=(1, 2))[:, None] * picks, axis=0)
    vec_ref = jnp.sum(jnp.sum(wmask * miss_ref * miss_ref, axis=(1, 2))[:, None] * picks, axis=0)
    owned = (jnp.arange(samples, dtype=jnp.int32) // 2 == here).astype(jnp.float32) * jnp.tile(
        own_counts, n_dp
    )
    tot_pol, tot_ref, tot_rows = lax.psum((vec_pol, vec_ref, owned), "dp")
    scale_rows = 1.0 / (width * tot_rows)
    pair_gap = ((tot_pol - tot_ref) * scale_rows).reshape(n_dp, 2)
    inside = -BETA * (pair_gap[:, 0] - pair_gap[:, 1])
    losses = lax.dynamic_slice_in_dim(jax.nn.softplus(-inside), here, 1)
    weight = BETA * LOSS_SCALE * jax.nn.sigmoid(-inside)
    coef = jnp.stack([weight, -weight], axis=1).reshape(samples) * scale_rows
    slot_coef = jnp.sum(picks * coef[None, :], axis=1)
    out_grad = slot_coef[:, None, None] * 2.0 * wmask * miss_pol
    dy_part = (output_gate * out_grad).astype(jnp.bfloat16).reshape(count_rows, width)
    dh = jnp.dot(dy_part, w_down, preferred_element_type=jnp.float32)
    preactivation_gradient = (dh * policy_activation_slope).astype(jnp.bfloat16)
    grad_b = contract_first(low_rank_hidden, preactivation_gradient)
    low_rank_gradient_piece = settle_gradients(
        contract_trailing(preactivation_gradient, adapter_output_factor)
    )
    dm_part = settle_gradients(contract_trailing(preactivation_gradient, w_up))
    modulation_gradient_sum, dlow_sum = (
        lax.psum(dm_part.astype(jnp.bfloat16), "tensor").astype(jnp.float32),
        lax.psum(low_rank_gradient_piece.astype(jnp.bfloat16), "tensor").astype(jnp.float32),
    )
    low_rank_gradient = dlow_sum.astype(jnp.bfloat16)
    modulation_gradient = modulation_gradient_sum + contract_trailing(
        low_rank_gradient, adapter_input_factor
    )
    dn = modulation_gradient.reshape(spots, BLK, width) * modulation_scale
    first_sum = jnp.sum(dn, axis=-1, keepdims=True)
    second_sum = jnp.sum(dn * normalized_input, axis=-1, keepdims=True)
    back_part = inverse_deviation * (dn - first_sum / width - normalized_input * second_sum / width)
    grad_part = (out_grad + back_part).astype(jnp.bfloat16)
    grad_a = contract_first(modulated_input, low_rank_gradient)
    sum_a, sum_b = lax.psum((grad_a, grad_b), "dp")
    return (losses, grad_part.reshape(CAP * BLK, width), sum_a / n_dp, sum_b / n_dp)


MESH = pl.DeviceIdType.MESH
F32 = jnp.float32
BF16 = jnp.bfloat16
SIDE = 32
TILE = 384
PAD = 128
GELU_ROOT = 0.7978845608028654
GELU_CUBE = 0.044715


def activation(pre, want_slope):
    square = pre * pre
    bend = jnp.tanh(GELU_ROOT * pre * (1.0 + GELU_CUBE * square))
    half = 0.5 * (1.0 + bend)
    if not want_slope:
        return pre * half
    slope = half + 0.5 * pre * (1.0 - bend * bend) * GELU_ROOT * (1.0 + 3.0 * GELU_CUBE * square)
    return pre * half, slope


def step_kernel(
    live_ref, wins_ref, tail_ref, x_hbm, t_hbm, mod_hbm, up_ref, dn_ref, a_hbm, b_hbm,
    loss_ref, grad_out, ga_out, gb_out,
    x_ref, t_ref, mod_in, a_in, b_ref, at_ref, mod_ref, mask_ref, flag_ref,
    grad_ref, ga_ref, gb_ref, gat_wide, local,
    w_ref, modded, low_ref, lowt_ref, slope_ref, hid_ref,
    ypart, crecv, ysend, yrecv, ysum, miss_ref, vbuf, ebuf, cf_ref,
    dpre_ref, dmpart, dmc, dmsend, dmrecv, dmsum,
    dlpart, dlc, dlsend, dlrecv, dlsum,
    gat, gatr, gap, gapr, gbp, gbr,
    z_send, z_recv, x_send, x_recv, c_send, c_recv, y_send, y_recv, v_send, v_recv,
    e_send, e_recv, dc_send, dc_recv, dy_send, dy_recv, g_send, g_recv,
    at_send, at_recv, rs_send, rs_recv, ag_send, ag_recv, tg_send, tg_recv,
):
    d = lax.axis_index("dp")
    t = lax.axis_index("tensor")
    z, x = d // 2, d % 2
    y, core = t // 2, t % 2
    high = z // 2
    middle = (z + high) % 2
    base = [middle, 1 - middle, 2, 3]
    place = [p + high * (3 - 2 * p) for p in base]
    inner = ((z + 1 - 2 * high) * 2 + x, t)
    edge_z = z - 1 + 2 * high
    edge = ((edge_z * middle + (1 - middle) * (z + 1 - 2 * high)) * 2 + x, t)
    across = (z * 2 + 1 - x, t)
    t_core = y * 2 + 1 - core
    t_y = (1 - y) * 2 + core
    t_far = (1 - y) * 2 + 1 - core
    mate = (d, t_core)
    over = (d, t_y)
    far = (d, t_far)
    peers = [mate, over, far]
    is_middle = middle == 1

    barrier = pltpu.get_barrier_semaphore()
    for k in range(1, 8):
        pl.semaphore_signal(barrier, inc=1, device_id=((d + k) % 8, t), device_id_type=MESH)
    for peer in peers:
        pl.semaphore_signal(barrier, inc=1, device_id=peer, device_id_type=MESH)

    shard = up_ref.shape[0]
    main = shard - SIDE
    half = main // 2
    here = pl.ds(d * shard, shard)
    loads = [
        pltpu.make_async_copy(src, dst, local.at[k]) for k, (src, dst) in enumerate((
            (up_ref, w_ref.at[0, here, :]), (dn_ref, w_ref.at[1, here, :]),
            (x_hbm, x_ref), (mod_hbm, mod_in), (a_hbm, a_in),
            (b_hbm, b_ref.at[pl.ds(0, b_hbm.shape[0]), :]), (t_hbm, t_ref)))]
    for load in loads:
        load.start()
    loads[0].wait()
    loads[1].wait()
    pl.semaphore_wait(barrier, 10)

    def copy(src, dst, send, recv, device):
        return pltpu.make_async_remote_copy(
            src_ref=src, dst_ref=dst, send_sem=send, recv_sem=recv,
            device_id=device, device_id_type=MESH)

    def rows(m, kind, slot):
        column = 1 - x if kind == 2 else x
        start = (0, half, main)[kind]
        size = (half, shard - half, SIDE)[kind]
        return w_ref.at[m, pl.ds((place[slot] * 2 + column) * shard + start, size), :]

    def x_rows(m, piece, column):
        slot, part = (0, 2) if piece == 8 else (piece // 2, piece % 2)
        size = SIDE if part == 2 else half
        return w_ref.at[m, pl.ds((place[slot] * 2 + column) * shard + part * half, size), :]

    def z_copy(m, kind, which):
        slot = [0, 0, 1, 2, 3][which]
        target = [1 + middle, 1, 3, 2, 3][which]
        device = inner if which in (0, 2) else edge
        ref = rows(m, kind, slot)
        return copy(ref, ref, z_send.at[m, kind, which], z_recv.at[m, kind, target], device)

    def z_arrive(m, kind, slot):
        ref = rows(m, kind, slot)
        copy(ref, ref, z_send.at[m, kind, 0], z_recv.at[m, kind, slot], inner).wait_recv()

    def x_copy(m, piece):
        ref = x_rows(m, piece, x)
        return copy(ref, ref, x_send.at[m, piece], x_recv.at[m, piece], across)

    def x_arrive(m, piece):
        ref = x_rows(m, piece, 1 - x)
        copy(ref, ref, x_send.at[m, piece], x_recv.at[m, piece], across).wait_recv()

    def begin_inner(m):
        x_copy(m, 8).start()
        for part in range(2):
            z_copy(m, part, 0).start()
            x_copy(m, part).start()

    def begin_edge(m):
        @pl.when(is_middle)
        def _():
            for part in range(2):
                z_copy(m, part, 1).start()

    def side_begin(m):
        x_arrive(m, 8)
        z_copy(m, 2, 0).start()

        @pl.when(is_middle)
        def _():
            z_copy(m, 2, 1).start()

    def relay(m, slot):
        for part in range(2):
            z_arrive(m, part, slot)

            @pl.when(is_middle)
            def _():
                z_copy(m, part, slot + 1).start()

            x_copy(m, slot * 2 + part).start()

    def side_relay(m, slot):
        z_arrive(m, 2, slot)

        @pl.when(is_middle)
        def _():
            z_copy(m, 2, slot + 1).start()

    begin_edge(0)
    begin_inner(0)

    count, wins = live_ref[0], wins_ref[0]
    tail_w, tail_l = tail_ref[0, 0], tail_ref[0, 1]
    loser_here = t >= wins
    last = jnp.where(loser_here, count - 1, wins - 1)
    tail = jnp.where(loser_here, tail_l, tail_w)
    live = jnp.where(t < count, jnp.where(t == last, tail, BLK), 0)
    spot = lax.broadcasted_iota(jnp.int32, (BLK, 1), 0)
    mask_ref[...] = jnp.where(spot < live, 1.0, 0.0)
    line = lax.broadcasted_iota(jnp.int32, (8, PAD), 0)
    flag_ref[...] = jnp.where(line >= wins, 1.0, 0.0)
    width = x_ref.shape[1]
    rows_w = jnp.broadcast_to(((wins - 1) * BLK + tail_w).astype(F32), (1, PAD))
    rows_l = jnp.broadcast_to(((count - wins - 1) * BLK + tail_l).astype(F32), (1, PAD))
    for load in loads[2:]:
        load.wait()
    rank = a_in.shape[1]
    b_ref[rank:PAD, :] = jnp.zeros((PAD - rank, b_ref.shape[1]), BF16)
    a_wide = jnp.concatenate(
        [a_in[...].astype(F32), jnp.zeros((width, PAD - rank), F32)], axis=1)
    at_ref[...] = a_wide.T.astype(BF16)
    for b in range(CAP):
        loser = flag_ref[b:b + 1, 0:1]
        mod_ref[b] = (1.0 - loser) * mod_in[0].astype(F32) + loser * mod_in[1].astype(F32)

    def norm(block, b):
        wide = x_ref[block, :].astype(F32)
        center = wide - jnp.mean(wide, axis=-1, keepdims=True)
        inverse = lax.rsqrt(jnp.mean(center * center, axis=-1, keepdims=True) + EPS)
        vectors = mod_ref[b]
        return wide, center * inverse, inverse, vectors[0:1], 1.0 + vectors[1:2], vectors[2:3]

    @pl.loop(0, CAP)
    def _(b):
        block = pl.ds(b * BLK, BLK)
        _, normed, _, shift, scale, _ = norm(block, b)
        modded[block, :] = (normed * scale + shift).astype(BF16)

    low_ref[...] = contract_trailing(modded[...], at_ref[...]).astype(BF16)
    lowt_ref[...] = contract_trailing(at_ref[...], modded[...]).astype(BF16)

    side_begin(0)
    relay(0, 1)
    begin_inner(1)
    side_relay(0, 1)
    relay(0, 2)
    side_relay(0, 2)
    relay(0, 3)
    side_relay(0, 3)
    begin_edge(1)
    side_begin(1)

    @pl.when(is_middle)
    def _():
        for slot in range(1, 4):
            relay(1, slot)
            side_relay(1, slot)

    def edge_relay(slot):
        @pl.when(middle == 0)
        def _():
            relay(1, slot)

    edge_relay(1)
    for piece in range(8):
        x_arrive(0, piece)

    @pl.loop(0, 4)
    def _(n):
        cols = pl.ds(pl.multiple_of(n * TILE, TILE), TILE)
        pre = jnp.dot(modded[...], w_ref[0, :, cols], preferred_element_type=F32)
        hid_ref[1, :, cols] = activation(pre, False).astype(BF16)
        pol = pre + jnp.dot(low_ref[...], b_ref[:, cols], preferred_element_type=F32)
        act, slope = activation(pol, True)
        hid_ref[0, :, cols] = act.astype(BF16)
        slope_ref[:, cols] = slope

    def y_core(j):
        src = ypart.at[j, 1 - core]
        return copy(src, crecv.at[j], c_send.at[j], c_recv.at[j], mate)

    def y_over(j):
        return copy(ysend.at[j], yrecv.at[j], y_send.at[j], y_recv.at[j], over)

    def v_copy(j, which):
        if which == 2:
            ref = vbuf.at[j, t_y]
        else:
            ref = vbuf.at[j, t]
        device = over if which == 1 else mate
        return copy(ref, ref, v_send.at[j, which], v_recv.at[j, which], device)

    def v_arrive(j, which):
        ref = vbuf.at[j, [t_core, t_y, t_far][which]]
        copy(ref, ref, v_send.at[j, which], v_recv.at[j, which], mate).wait_recv()

    def columns(j):
        return pl.ds(pl.multiple_of(place[j] * TILE, TILE), TILE)

    def stage_product(j):
        @pl.loop(0, 2)
        def _(p):
            part = contract_trailing(hid_ref[p], w_ref[1, pl.ds(place[j] * TILE, TILE), :])
            part = part.astype(BF16)
            for b in range(CAP):
                ypart[j, b % 2, b // 2, p] = part[b * BLK:(b + 1) * BLK, :]
        y_core(j).start()

    def stage_pair(j):
        y_core(j).wait_recv()
        ysend[j] = (ypart[j, core, 1 - y].astype(F32) + crecv[j, 1 - y].astype(F32)).astype(BF16)
        y_over(j).start()
        ysum[j] = ypart[j, core, y].astype(F32) + crecv[j, y].astype(F32)

    own = pl.ds(t * BLK, BLK)

    def stage_total(j):
        y_over(j).wait_recv()
        cols = columns(j)
        total = ysum[j] + yrecv[j].astype(F32)
        gate = mod_ref[t, 2:3, cols]
        residual = x_ref[own, cols].astype(F32) - t_ref[own, cols].astype(F32)
        mask = mask_ref[...]
        miss = residual + gate * total[0]
        miss_ref2 = residual + gate * total[1]
        slope = 2.0 * mask * miss
        miss_ref[:, cols] = slope
        vbuf[j, t] = (gate * slope).astype(BF16)
        v_copy(j, 0).start()
        v_copy(j, 1).start()
        err = jnp.concatenate([
            jnp.sum(mask * miss * miss, axis=(0, 1), keepdims=True),
            jnp.sum(mask * miss_ref2 * miss_ref2, axis=(0, 1), keepdims=True)], axis=0)
        return jnp.broadcast_to(err, (2, PAD))

    def stage_share(j):
        v_arrive(j, 1)
        v_copy(j, 2).start()

    def ready(j):
        x_arrive(1, 2 * j)
        x_arrive(1, 2 * j + 1)
        if j > 0:
            @pl.when(middle == 0)
            def _():
                side_relay(1, j)

    ready(0)
    stage_product(0)
    stage_pair(0)
    edge_relay(2)
    ready(1)
    stage_product(1)
    stage_pair(1)
    edge_relay(3)
    err = stage_total(0)
    ready(2)
    stage_product(2)
    stage_pair(2)
    err = err + stage_total(1)
    stage_share(0)
    ready(3)
    stage_product(3)
    stage_pair(3)
    err = err + stage_total(2)
    stage_share(1)
    err = err + stage_total(3)
    ebuf[t, 0:2, :] = err
    ebuf[t, 2:8, :] = jnp.zeros((6, PAD), F32)

    def e_copy(k):
        ref = ebuf.at[t]
        return copy(ref, ref, e_send.at[k], e_recv.at[k], peers[k])

    for k in range(3):
        e_copy(k).start()
    stage_share(2)
    stage_share(3)
    for k, peer in enumerate(peers):
        ref = ebuf.at[peer[1]]
        copy(ref, ref, e_send.at[k], e_recv.at[k], peer).wait_recv()
    gains = jnp.zeros((1, PAD), F32)
    loses = jnp.zeros((1, PAD), F32)
    for b in range(CAP):
        drop = ebuf[b, 0:1, :] - ebuf[b, 1:2, :]
        loser = flag_ref[b:b + 1, :]
        gains = gains + (1.0 - loser) * drop
        loses = loses + loser * drop
    inv_w, inv_l = 1.0 / (width * rows_w), 1.0 / (width * rows_l)
    outside = BETA * (gains * inv_w - loses * inv_l)
    loss = jnp.maximum(outside, 0.0) + jnp.log1p(jnp.exp(-jnp.abs(outside)))
    loss_ref[0] = loss[0, 0]
    weight = BETA * LOSS_SCALE / (1.0 + jnp.exp(-outside))
    loser = flag_ref[...]
    cf_ref[...] = weight * ((1.0 - loser) * inv_w - loser * inv_l)

    for j in range(4):
        v_arrive(j, 0)
        v_arrive(j, 2)

    @pl.loop(0, 4)
    def _(n):
        cols = pl.ds(pl.multiple_of(n * TILE, TILE), TILE)
        dh = jnp.zeros((CAP * BLK, TILE), F32)
        for j in range(4):
            dy = vbuf[j].reshape(CAP * BLK, TILE)
            dh = dh + jnp.dot(dy, w_ref[1, pl.ds(place[j] * TILE, TILE), cols],
                              preferred_element_type=F32)
        for b in range(CAP):
            block = slice(b * BLK, (b + 1) * BLK)
            dpre_ref[block, cols] = (
                dh[block] * (cf_ref[b:b + 1, 0:1] * slope_ref[block, cols])).astype(BF16)

    def dl_core():
        return copy(dlpart.at[1 - core], dlc, dc_send.at[4], dc_recv.at[4], mate)

    def dl_over():
        return copy(dlsend, dlrecv, dy_send.at[4], dy_recv.at[4], over)

    def dm_core(n):
        return copy(dmpart.at[n, 1 - core], dmc.at[n], dc_send.at[n], dc_recv.at[n], mate)

    def dm_over(n):
        return copy(dmsend.at[n], dmrecv.at[n], dy_send.at[n], dy_recv.at[n], over)

    def at_copy(k):
        return copy(gat.at[peers[k][1]], gatr.at[k], at_send.at[k], at_recv.at[k], peers[k])

    def rs_copy(which, k):
        to = (d + k) % 8
        part, land = ((gap, gapr), (gbp, gbr))[which]
        return copy(part.at[to], land.at[k], rs_send.at[which, k], rs_recv.at[which, k], (to, t))

    def ag_copy(which, k):
        to = (d + k) % 8
        ref = ga_ref.at[t, d] if which == 0 else gb_ref.at[d]
        return copy(ref, ref, ag_send.at[which, k], ag_recv.at[which, k], (to, t))

    def ag_arrive(which, k):
        source = (d + 8 - k) % 8
        ref = ga_ref.at[t, source] if which == 0 else gb_ref.at[source]
        copy(ref, ref, ag_send.at[which, k], ag_recv.at[which, k], (source, t)).wait_recv()

    dlowt = contract_trailing(b_ref[...], dpre_ref[...]).astype(BF16)
    ga = jnp.dot(dlowt, modded[...], preferred_element_type=F32).astype(BF16)
    for k in range(4):
        gat[k] = ga[k * 16:(k + 1) * 16, :]
    for k in range(3):
        at_copy(k).start()

    dlow = contract_trailing(dpre_ref[...], b_ref[...]).astype(BF16)
    for b in range(CAP):
        dlpart[b % 2, b // 2] = dlow[b * BLK:(b + 1) * BLK, :]
    dl_core().start()

    def dm_product(n):
        part = contract_trailing(
            dpre_ref[...], w_ref[0, n * TILE:(n + 1) * TILE, :]).astype(BF16)
        for b in range(CAP):
            dmpart[n, b % 2, b // 2] = part[b * BLK:(b + 1) * BLK, :]
        dm_core(n).start()

    def dm_pair(n):
        dm_core(n).wait_recv()
        dmsend[n] = (dmpart[n, core, 1 - y].astype(F32) + dmc[n, 1 - y].astype(F32)).astype(BF16)
        dm_over(n).start()
        dmsum[n] = dmpart[n, core, y].astype(F32) + dmc[n, y].astype(F32)

    dm_product(0)
    gb = jnp.dot(lowt_ref[...], dpre_ref[...], preferred_element_type=F32).astype(BF16)
    half_b = gb.shape[1] // 2
    for k in range(8):
        gbp[k] = gb[(k // 2) * 16:(k // 2 + 1) * 16, (k % 2) * half_b:(k % 2 + 1) * half_b]
    for k in range(1, 8):
        rs_copy(1, k).start()
    dm_pair(0)
    dl_core().wait_recv()
    dlsend[...] = (dlpart[core, 1 - y].astype(F32) + dlc[1 - y].astype(F32)).astype(BF16)
    dl_over().start()
    dlsum[...] = dlpart[core, y].astype(F32) + dlc[y].astype(F32)
    dm_product(1)
    total = gat[t].astype(F32)
    for k in range(3):
        at_copy(k).wait_recv()
        total = total + gatr[k].astype(F32)
    total = total.astype(BF16)
    wide = total.shape[1] // 8
    for k in range(8):
        gap[k] = total[:, k * wide:(k + 1) * wide]
    for k in range(1, 8):
        rs_copy(0, k).start()
    dm_pair(1)
    dm_product(2)
    dm_pair(2)
    dm_product(3)
    dm_pair(3)

    _, normed, inverse, _, scale, _ = norm(own, t)
    dl_over().wait_recv()
    dlow = (dlsum[...] + dlrecv[...].astype(F32)).astype(BF16)
    for n in range(4):
        dm_over(n).wait_recv()
    dm = jnp.concatenate([dmsum[n] + dmrecv[n].astype(F32) for n in range(4)], axis=1)
    dm = dm + jnp.dot(dlow, at_ref[...], preferred_element_type=F32)
    dn = dm * scale
    first = jnp.mean(dn, axis=-1, keepdims=True)
    second = jnp.mean(dn * normed, axis=-1, keepdims=True)
    out_grad = cf_ref[pl.ds(t, 1), 0:1] * miss_ref[...]
    grad_ref[t] = (out_grad + inverse * (dn - first - normed * second)).astype(BF16)

    def g_copy(which):
        ref = grad_ref.at[t_y] if which == 2 else grad_ref.at[t]
        return copy(ref, ref, g_send.at[which], g_recv.at[which], over if which == 1 else mate)

    def g_arrive(which):
        ref = grad_ref.at[[t_core, t_y, t_far][which]]
        copy(ref, ref, g_send.at[which], g_recv.at[which], mate).wait_recv()

    def g_store(k, block):
        return pltpu.make_async_copy(
            grad_ref.at[block], grad_out.at[pl.ds(block * BLK, BLK), :], local.at[7 + k])

    g_copy(1).start()
    g_copy(0).start()
    g_store(0, t).start()

    for which, (part, land) in ((1, (gbp, gbr)), (0, (gap, gapr))):
        total = part[d].astype(F32)
        for k in range(1, 8):
            rs_copy(which, k).wait_recv()
            total = total + land[k].astype(F32)
        if which == 1:
            gb_ref[d] = total.astype(BF16)
        else:
            ga_ref[t, d] = total.astype(BF16)
        for k in range(1, 8):
            ag_copy(which, k).start()

    g_arrive(1)
    g_copy(2).start()
    g_store(2, t_y).start()
    for k in range(1, 8):
        ag_arrive(0, k)

    def tg_copy(k):
        ref = ga_ref.at[t]
        return copy(ref, ref, tg_send.at[k], tg_recv.at[k], peers[k])

    for k in range(3):
        tg_copy(k).start()
    for k in range(1, 8):
        ag_arrive(1, k)
    for k in range(8):
        gb_out[(k // 2) * 16:(k // 2 + 1) * 16, (k % 2) * half_b:(k % 2 + 1) * half_b] = (
            gb_ref[k].astype(F32) * 0.125)
    g_arrive(0)
    g_store(1, t_core).start()
    g_arrive(2)
    g_store(3, t_far).start()
    for k, peer in enumerate(peers):
        ref = ga_ref.at[peer[1]]
        copy(ref, ref, tg_send.at[k], tg_recv.at[k], peer).wait_recv()
    for r in range(4):
        for k in range(8):
            gat_wide[r * 16:(r + 1) * 16, k * wide:(k + 1) * wide] = (
                ga_ref[r, k].astype(F32) * 0.125)
    gat_wide[rank:PAD, :] = jnp.zeros((PAD - rank, width), F32)
    ga_out[...] = gat_wide[...].T[:, 0:rank]
    for k, block in enumerate((t, t_core, t_y, t_far)):
        g_store(k, block).wait()

    for m in range(2):
        for piece in range(9):
            x_copy(m, piece).wait_send()
        for kind in range(3):
            z_copy(m, kind, 0).wait_send()

            @pl.when(is_middle)
            def _():
                for which in range(1, 5):
                    z_copy(m, kind, which).wait_send()
    for j in range(4):
        y_core(j).wait_send()
        y_over(j).wait_send()
        dm_core(j).wait_send()
        dm_over(j).wait_send()
        for which in range(3):
            v_copy(j, which).wait_send()
    dl_core().wait_send()
    dl_over().wait_send()
    for k in range(3):
        e_copy(k).wait_send()
        at_copy(k).wait_send()
        g_copy(k).wait_send()
        tg_copy(k).wait_send()
    for which in range(2):
        for k in range(1, 8):
            rs_copy(which, k).wait_send()
            ag_copy(which, k).wait_send()


def fused_device(
    tokens, targets, modulation, live_block_count, preferred_blocks, last_block_rows,
    up_projection_weight, down_weight_transposed, adapter_input_factor, adapter_output_factor,
):
    width = tokens.shape[1]
    rank = adapter_input_factor.shape[1]
    hidden = adapter_output_factor.shape[1]
    dma = pltpu.SemaphoreType.DMA
    vm = pltpu.VMEM
    rows = CAP * BLK
    smem = pl.BlockSpec(memory_space=pltpu.SMEM)
    anywhere = pl.BlockSpec(memory_space=pl.ANY)
    whole = pl.BlockSpec(memory_space=pltpu.VMEM)
    return pl.pallas_call(
        step_kernel,
        out_shape=(
            jax.ShapeDtypeStruct((1,), F32),
            jax.ShapeDtypeStruct((rows, width), BF16),
            jax.ShapeDtypeStruct((width, rank), F32),
            jax.ShapeDtypeStruct((rank, hidden), F32),
        ),
        in_specs=[smem] * 3 + [anywhere] * 7,
        out_specs=(smem, anywhere, whole, whole),
        scratch_shapes=[
            vm((rows, width), BF16),
            vm((rows, width), BF16),
            vm((2, 3, width), BF16),
            vm((width, rank), BF16),
            vm((PAD, hidden), BF16),
            vm((PAD, width), BF16),
            vm((CAP, 3, width), F32),
            vm((BLK, 1), F32),
            vm((8, PAD), F32),
            vm((CAP, BLK, width), BF16),
            vm((4, 8, 16, width // 8), BF16),
            vm((8, 16, hidden // 2), BF16),
            vm((PAD, width), F32),
            dma((11,)),
            vm((2, width, hidden), BF16),
            vm((rows, width), BF16),
            vm((rows, PAD), BF16),
            vm((PAD, rows), BF16),
            vm((rows, hidden), F32),
            vm((2, rows, hidden), BF16),
            vm((4, 2, 2, 2, BLK, TILE), BF16),
            vm((4, 2, 2, BLK, TILE), BF16),
            vm((4, 2, BLK, TILE), BF16),
            vm((4, 2, BLK, TILE), BF16),
            vm((4, 2, BLK, TILE), F32),
            vm((BLK, width), F32),
            vm((4, CAP, BLK, TILE), BF16),
            vm((CAP, 8, PAD), F32),
            vm((8, PAD), F32),
            vm((rows, hidden), BF16),
            vm((4, 2, 2, BLK, TILE), BF16),
            vm((4, 2, BLK, TILE), BF16),
            vm((4, BLK, TILE), BF16),
            vm((4, BLK, TILE), BF16),
            vm((4, BLK, TILE), F32),
            vm((2, 2, BLK, PAD), BF16),
            vm((2, BLK, PAD), BF16),
            vm((BLK, PAD), BF16),
            vm((BLK, PAD), BF16),
            vm((BLK, PAD), F32),
            vm((4, 16, width), BF16),
            vm((3, 16, width), BF16),
            vm((8, 16, width // 8), BF16),
            vm((8, 16, width // 8), BF16),
            vm((8, 16, hidden // 2), BF16),
            vm((8, 16, hidden // 2), BF16),
            dma((2, 3, 5)), dma((2, 3, 4)), dma((2, 9)), dma((2, 9)),
            dma((4,)), dma((4,)), dma((4,)), dma((4,)), dma((4, 3)), dma((4, 3)),
            dma((3,)), dma((3,)), dma((5,)), dma((5,)), dma((5,)), dma((5,)),
            dma((3,)), dma((3,)), dma((3,)), dma((3,)),
            dma((2, 8)), dma((2, 8)), dma((2, 8)), dma((2, 8)), dma((3,)), dma((3,)),
        ],
        compiler_params=pltpu.CompilerParams(
            collective_id=0, has_side_effects=True, vmem_limit_bytes=48 * 1024 * 1024),
    )(live_block_count, preferred_blocks, last_block_rows, tokens, targets, modulation,
      up_projection_weight, down_weight_transposed, adapter_input_factor, adapter_output_factor)


def fits_fused(mesh):
    return dict(mesh.shape) == {"dp": 8, "tensor": 4}


def solution(mesh):
    return jax.shard_map(
        fused_device if fits_fused(mesh) else per_device,
        mesh=mesh,
        in_specs=(
            P("dp", None),
            P("dp", None),
            P("dp", None, None),
            P("dp"),
            P("dp"),
            P("dp", None),
            P("dp", "tensor"),
            P("dp", "tensor"),
            P(),
            P(None, "tensor"),
        ),
        out_specs=(P("dp"), P("dp", None), P(), P(None, "tensor")),
        check_vma=False,
    )
```

```python
import jax
import jax.numpy as jnp
from jax import lax
from jax.experimental import pallas as pl
from jax.experimental.pallas import tpu as pltpu
from jax.sharding import PartitionSpec as P

BLK = 64
CAP = 4


EPS = 1e-06
BETA = 20.0
LOSS_SCALE = 4096.0


def settle_gradients(value):
    return lax.optimization_barrier(value.astype(jnp.bfloat16)).astype(jnp.float32)


def layer_norm(image_blocks):
    wide = image_blocks.astype(jnp.float32)
    center = wide - jnp.mean(wide, axis=-1, keepdims=True)
    inverse_deviation = lax.rsqrt(jnp.mean(center * center, axis=-1, keepdims=True) + EPS)
    return (center * inverse_deviation, inverse_deviation)


def gelu_and_slope(pre):

    def act(value):
        return jax.nn.gelu(value, approximate=True)

    value, back = jax.vjp(act, pre)
    return (value, back(jnp.ones_like(pre))[0])


def contract_trailing(left, right):
    return lax.dot_general(
        left, right, (((1,), (1,)), ((), ())), preferred_element_type=jnp.float32
    )


def contract_first(left, right):
    return lax.dot_general(
        left, right, (((0,), (0,)), ((), ())), preferred_element_type=jnp.float32
    )


def slot_state(live_block_count, preferred_blocks, last_block_rows):
    count = live_block_count[0]
    wins = preferred_blocks[0]
    slots = jnp.arange(CAP, dtype=jnp.int32)
    flags = (slots >= wins).astype(jnp.int32)
    last = jnp.where(flags == 0, wins - 1, count - 1)
    tail = jnp.where(flags == 0, last_block_rows[0, 0], last_block_rows[0, 1])
    live = jnp.where(slots < count, jnp.where(slots == last, tail, BLK), 0)
    masks = (jnp.arange(BLK, dtype=jnp.int32)[None, :] < live[:, None]).astype(jnp.float32)
    own_counts = jnp.stack(
        [jnp.sum(jnp.where(flags == 0, live, 0)), jnp.sum(jnp.where(flags == 1, live, 0))]
    ).astype(jnp.float32)
    return flags, masks, own_counts


def per_device(
    tokens,
    targets,
    modulation,
    live_block_count,
    preferred_blocks,
    last_block_rows,
    up_projection_weight,
    down_weight_transposed,
    adapter_input_factor,
    adapter_output_factor,
):
    width = tokens.shape[1]
    n_dp = lax.axis_size("dp")
    here = lax.axis_index("dp")
    flags, masks, own_counts = slot_state(live_block_count, preferred_blocks, last_block_rows)
    blocks_x = tokens.reshape(CAP, BLK, width)
    blocks_t = targets.reshape(CAP, BLK, width)
    blocks_mod = jnp.where(flags[:, None, None] == 0, modulation[0][None], modulation[1][None])
    homes = jnp.full((CAP,), here, jnp.int32)
    work_x, work_t, work_mod = (blocks_x, blocks_t, blocks_mod)
    work_mask, work_flag, work_home = (masks, flags, homes)
    spots = work_x.shape[0]
    count_rows = spots * BLK
    samples = 2 * n_dp
    ids = work_home * 2 + work_flag
    picks = (ids[:, None] == jnp.arange(samples, dtype=jnp.int32)[None, :]).astype(jnp.float32)
    modulation_vectors = work_mod.astype(jnp.float32)
    shift = modulation_vectors[:, None, 0]
    modulation_scale = 1.0 + modulation_vectors[:, None, 1]
    output_gate = modulation_vectors[:, None, 2]
    normalized_input, inverse_deviation = layer_norm(work_x)
    modulated_input = (
        (normalized_input * modulation_scale + shift)
        .astype(jnp.bfloat16)
        .reshape(count_rows, width)
    )
    w_up, w_down = (
        lax.all_gather(up_projection_weight, "dp", axis=0, tiled=True),
        lax.all_gather(down_weight_transposed, "dp", axis=0, tiled=True),
    )
    low_rank_hidden = jnp.dot(
        modulated_input, adapter_input_factor, preferred_element_type=jnp.float32
    ).astype(jnp.bfloat16)
    reference_preactivation = jnp.dot(modulated_input, w_up, preferred_element_type=jnp.float32)
    policy_preactivation = reference_preactivation + jnp.dot(
        low_rank_hidden, adapter_output_factor, preferred_element_type=jnp.float32
    )
    act_pol, policy_activation_slope = gelu_and_slope(policy_preactivation)
    hid_pol = act_pol.astype(jnp.bfloat16)
    hid_ref = jax.nn.gelu(reference_preactivation, approximate=True).astype(jnp.bfloat16)
    part_pol = settle_gradients(contract_trailing(hid_pol, w_down))
    part_ref = settle_gradients(contract_trailing(hid_ref, w_down))
    sum_pol, sum_ref = (
        lax.psum(part_pol.astype(jnp.bfloat16), "tensor").astype(jnp.float32),
        lax.psum(part_ref.astype(jnp.bfloat16), "tensor").astype(jnp.float32),
    )
    x_part = work_x.astype(jnp.float32)
    t_part = work_t.astype(jnp.float32)
    wmask = work_mask[:, :, None]
    miss_pol = x_part + output_gate * sum_pol.reshape(spots, BLK, width) - t_part
    miss_ref = x_part + output_gate * sum_ref.reshape(spots, BLK, width) - t_part
    vec_pol = jnp.sum(jnp.sum(wmask * miss_pol * miss_pol, axis=(1, 2))[:, None] * picks, axis=0)
    vec_ref = jnp.sum(jnp.sum(wmask * miss_ref * miss_ref, axis=(1, 2))[:, None] * picks, axis=0)
    owned = (jnp.arange(samples, dtype=jnp.int32) // 2 == here).astype(jnp.float32) * jnp.tile(
        own_counts, n_dp
    )
    tot_pol, tot_ref, tot_rows = lax.psum((vec_pol, vec_ref, owned), "dp")
    scale_rows = 1.0 / (width * tot_rows)
    pair_gap = ((tot_pol - tot_ref) * scale_rows).reshape(n_dp, 2)
    inside = -BETA * (pair_gap[:, 0] - pair_gap[:, 1])
    losses = lax.dynamic_slice_in_dim(jax.nn.softplus(-inside), here, 1)
    weight = BETA * LOSS_SCALE * jax.nn.sigmoid(-inside)
    coef = jnp.stack([weight, -weight], axis=1).reshape(samples) * scale_rows
    slot_coef = jnp.sum(picks * coef[None, :], axis=1)
    out_grad = slot_coef[:, None, None] * 2.0 * wmask * miss_pol
    dy_part = (output_gate * out_grad).astype(jnp.bfloat16).reshape(count_rows, width)
    dh = jnp.dot(dy_part, w_down, preferred_element_type=jnp.float32)
    preactivation_gradient = (dh * policy_activation_slope).astype(jnp.bfloat16)
    grad_b = contract_first(low_rank_hidden, preactivation_gradient)
    low_rank_gradient_piece = settle_gradients(
        contract_trailing(preactivation_gradient, adapter_output_factor)
    )
    dm_part = settle_gradients(contract_trailing(preactivation_gradient, w_up))
    modulation_gradient_sum, dlow_sum = (
        lax.psum(dm_part.astype(jnp.bfloat16), "tensor").astype(jnp.float32),
        lax.psum(low_rank_gradient_piece.astype(jnp.bfloat16), "tensor").astype(jnp.float32),
    )
    low_rank_gradient = dlow_sum.astype(jnp.bfloat16)
    modulation_gradient = modulation_gradient_sum + contract_trailing(
        low_rank_gradient, adapter_input_factor
    )
    dn = modulation_gradient.reshape(spots, BLK, width) * modulation_scale
    first_sum = jnp.sum(dn, axis=-1, keepdims=True)
    second_sum = jnp.sum(dn * normalized_input, axis=-1, keepdims=True)
    back_part = inverse_deviation * (dn - first_sum / width - normalized_input * second_sum / width)
    grad_part = (out_grad + back_part).astype(jnp.bfloat16)
    grad_a = contract_first(modulated_input, low_rank_gradient)
    sum_a, sum_b = lax.psum((grad_a, grad_b), "dp")
    return (losses, grad_part.reshape(CAP * BLK, width), sum_a / n_dp, sum_b / n_dp)


MESH = pl.DeviceIdType.MESH
F32 = jnp.float32
BF16 = jnp.bfloat16
SIDE = 32
TILE = 384
PAD = 128
GELU_ROOT = 0.7978845608028654
GELU_CUBE = 0.044715


def activation(pre, want_slope):
    square = pre * pre
    bend = jnp.tanh(GELU_ROOT * pre * (1.0 + GELU_CUBE * square))
    half = 0.5 * (1.0 + bend)
    if not want_slope:
        return pre * half
    slope = half + 0.5 * pre * (1.0 - bend * bend) * GELU_ROOT * (1.0 + 3.0 * GELU_CUBE * square)
    return pre * half, slope


def step_kernel(
    live_ref, wins_ref, tail_ref, x_hbm, t_hbm, mod_hbm, up_ref, dn_ref, a_hbm, b_hbm,
    loss_ref, grad_out, ga_out, gb_out,
    x_ref, t_ref, mod_in, b_ref, at_ref, mod_ref, mask_ref, flag_ref,
    grad_ref, ga_ref, gb_ref, local,
    w_ref, modded, low_ref, lowt_ref, slope_ref, hid_ref,
    ypart, crecv, ysend, yrecv, ysum, miss_ref, vbuf, ebuf, cf_ref,
    dpre_ref, dmpart, dmc, dmsend, dmrecv, dmsum,
    dlpart, dlc, dlsend, dlrecv, dlsum,
    gat, gatr, gap, gapr, gbp, gbr,
    z_send, z_recv, x_send, x_recv, c_send, c_recv, y_send, y_recv, v_send, v_recv,
    e_send, e_recv, dc_send, dc_recv, dy_send, dy_recv, g_send, g_recv,
    at_send, at_recv, rs_send, rs_recv, ag_send, ag_recv, tg_send, tg_recv,
):
    d = lax.axis_index("dp")
    t = lax.axis_index("tensor")
    z, x = d // 2, d % 2
    y, core = t // 2, t % 2
    high = z // 2
    middle = (z + high) % 2
    base = [middle, 1 - middle, 2, 3]
    place = [p + high * (3 - 2 * p) for p in base]
    inner = ((z + 1 - 2 * high) * 2 + x, t)
    edge_z = z - 1 + 2 * high
    edge = ((edge_z * middle + (1 - middle) * (z + 1 - 2 * high)) * 2 + x, t)
    across = (z * 2 + 1 - x, t)
    t_core = y * 2 + 1 - core
    t_y = (1 - y) * 2 + core
    t_far = (1 - y) * 2 + 1 - core
    mate = (d, t_core)
    over = (d, t_y)
    far = (d, t_far)
    peers = [mate, over, far]
    is_middle = middle == 1

    barrier = pltpu.get_barrier_semaphore()
    for k in range(1, 8):
        pl.semaphore_signal(barrier, inc=1, device_id=((d + k) % 8, t), device_id_type=MESH)
    for peer in peers:
        pl.semaphore_signal(barrier, inc=1, device_id=peer, device_id_type=MESH)

    shard = up_ref.shape[0]
    main = shard - SIDE
    half = main // 2
    here = pl.ds(d * shard, shard)
    loads = [
        pltpu.make_async_copy(src, dst, local.at[k]) for k, (src, dst) in enumerate((
            (up_ref, w_ref.at[0, here, :]), (dn_ref, w_ref.at[1, here, :]),
            (x_hbm, x_ref), (mod_hbm, mod_in),
            (a_hbm, at_ref.at[pl.ds(0, a_hbm.shape[0]), :]),
            (b_hbm, b_ref.at[pl.ds(0, b_hbm.shape[0]), :]), (t_hbm, t_ref)))]
    for load in loads:
        load.start()
    loads[0].wait()
    loads[1].wait()
    pl.semaphore_wait(barrier, 10)

    def copy(src, dst, send, recv, device):
        return pltpu.make_async_remote_copy(
            src_ref=src, dst_ref=dst, send_sem=send, recv_sem=recv,
            device_id=device, device_id_type=MESH)

    def rows(m, kind, slot):
        column = 1 - x if kind == 2 else x
        start = (0, half, main)[kind]
        size = (half, shard - half, SIDE)[kind]
        return w_ref.at[m, pl.ds((place[slot] * 2 + column) * shard + start, size), :]

    def x_rows(m, piece, column):
        slot, part = (0, 2) if piece == 8 else (piece // 2, piece % 2)
        size = SIDE if part == 2 else half
        return w_ref.at[m, pl.ds((place[slot] * 2 + column) * shard + part * half, size), :]

    def z_copy(m, kind, which):
        slot = [0, 0, 1, 2, 3][which]
        target = [1 + middle, 1, 3, 2, 3][which]
        device = inner if which in (0, 2) else edge
        ref = rows(m, kind, slot)
        return copy(ref, ref, z_send.at[m, kind, which], z_recv.at[m, kind, target], device)

    def z_arrive(m, kind, slot):
        ref = rows(m, kind, slot)
        copy(ref, ref, z_send.at[m, kind, 0], z_recv.at[m, kind, slot], inner).wait_recv()

    def x_copy(m, piece):
        ref = x_rows(m, piece, x)
        return copy(ref, ref, x_send.at[m, piece], x_recv.at[m, piece], across)

    def x_arrive(m, piece):
        ref = x_rows(m, piece, 1 - x)
        copy(ref, ref, x_send.at[m, piece], x_recv.at[m, piece], across).wait_recv()

    def begin_inner(m):
        for part in range(2):
            z_copy(m, part, 0).start()

    def begin_x(m):
        x_copy(m, 8).start()
        for part in range(2):
            x_copy(m, part).start()

    def begin_edge(m):
        @pl.when(is_middle)
        def _():
            for part in range(2):
                z_copy(m, part, 1).start()

    def side_begin(m):
        x_arrive(m, 8)
        z_copy(m, 2, 0).start()

        @pl.when(is_middle)
        def _():
            z_copy(m, 2, 1).start()

    def relay_part(m, slot, part):
        z_arrive(m, part, slot)

        @pl.when(is_middle)
        def _():
            z_copy(m, part, slot + 1).start()

        x_copy(m, slot * 2 + part).start()

    def relay(m, slot):
        for part in range(2):
            relay_part(m, slot, part)

    def side_relay(m, slot):
        z_arrive(m, 2, slot)

        @pl.when(is_middle)
        def _():
            z_copy(m, 2, slot + 1).start()

    begin_edge(0)
    begin_inner(0)
    begin_x(0)

    count, wins = live_ref[0], wins_ref[0]
    tail_w, tail_l = tail_ref[0, 0], tail_ref[0, 1]
    loser_here = t >= wins
    last = jnp.where(loser_here, count - 1, wins - 1)
    tail = jnp.where(loser_here, tail_l, tail_w)
    live = jnp.where(t < count, jnp.where(t == last, tail, BLK), 0)
    spot = lax.broadcasted_iota(jnp.int32, (BLK, 1), 0)
    mask_ref[...] = jnp.where(spot < live, 1.0, 0.0)
    line = lax.broadcasted_iota(jnp.int32, (8, PAD), 0)
    flag_ref[...] = jnp.where(line >= wins, 1.0, 0.0)
    width = x_ref.shape[1]
    rows_w = jnp.broadcast_to(((wins - 1) * BLK + tail_w).astype(F32), (1, PAD))
    rows_l = jnp.broadcast_to(((count - wins - 1) * BLK + tail_l).astype(F32), (1, PAD))
    for load in loads[2:]:
        load.wait()
    rank = a_hbm.shape[0]
    b_ref[rank:PAD, :] = jnp.zeros((PAD - rank, b_ref.shape[1]), BF16)
    at_ref[rank:PAD, :] = jnp.zeros((PAD - rank, width), BF16)
    for b in range(CAP):
        loser = flag_ref[b:b + 1, 0:1]
        mod_ref[b] = ((1.0 - loser) * mod_in[:, 0, :].astype(F32)
                      + loser * mod_in[:, 1, :].astype(F32))

    def norm(block, b):
        wide = x_ref[block, :].astype(F32)
        center = wide - jnp.mean(wide, axis=-1, keepdims=True)
        inverse = lax.rsqrt(jnp.mean(center * center, axis=-1, keepdims=True) + EPS)
        vectors = mod_ref[b]
        return wide, center * inverse, inverse, vectors[0:1], 1.0 + vectors[1:2], vectors[2:3]

    @pl.loop(0, CAP)
    def _(b):
        block = pl.ds(b * BLK, BLK)
        _, normed, _, shift, scale, _ = norm(block, b)
        modded[block, :] = (normed * scale + shift).astype(BF16)

    low_ref[...] = contract_trailing(modded[...], at_ref[...]).astype(BF16)
    lowt_ref[...] = contract_trailing(at_ref[...], modded[...]).astype(BF16)

    side_begin(0)
    relay(0, 1)

    @pl.when(middle == 0)
    def _():
        begin_inner(1)

    begin_x(1)
    side_relay(0, 1)
    relay(0, 2)
    side_relay(0, 2)
    relay(0, 3)
    side_relay(0, 3)

    @pl.when(is_middle)
    def _():
        begin_inner(1)

    begin_edge(1)
    side_begin(1)

    @pl.when(is_middle)
    def _():
        for slot in range(1, 4):
            relay(1, slot)
            side_relay(1, slot)

    def edge_relay(slot, parts=(0, 1)):
        @pl.when(middle == 0)
        def _():
            for part in parts:
                relay_part(1, slot, part)

    edge_relay(1)
    for piece in range(8):
        x_arrive(0, piece)

    @pl.loop(0, 4)
    def _(n):
        cols = pl.ds(pl.multiple_of(n * TILE, TILE), TILE)
        pre = jnp.dot(modded[...], w_ref[0, :, cols], preferred_element_type=F32)
        hid_ref[1, :, cols] = activation(pre, False).astype(BF16)
        pol = pre + jnp.dot(low_ref[...], b_ref[:, cols], preferred_element_type=F32)
        act, slope = activation(pol, True)
        hid_ref[0, :, cols] = act.astype(BF16)
        slope_ref[:, cols] = slope

    def y_core(j):
        src = ypart.at[j, 1 - core]
        return copy(src, crecv.at[j], c_send.at[j], c_recv.at[j], mate)

    def y_over(j):
        return copy(ysend.at[j], yrecv.at[j], y_send.at[j], y_recv.at[j], over)

    def v_copy(j, which):
        if which == 2:
            ref = vbuf.at[j, t_y]
        else:
            ref = vbuf.at[j, t]
        device = over if which == 1 else mate
        return copy(ref, ref, v_send.at[j, which], v_recv.at[j, which], device)

    def v_arrive(j, which):
        ref = vbuf.at[j, [t_core, t_y, t_far][which]]
        copy(ref, ref, v_send.at[j, which], v_recv.at[j, which], mate).wait_recv()

    def columns(j):
        return pl.ds(pl.multiple_of(place[j] * TILE, TILE), TILE)

    def stage_product(j):
        @pl.loop(0, 2)
        def _(p):
            part = contract_trailing(hid_ref[p], w_ref[1, pl.ds(place[j] * TILE, TILE), :])
            part = part.astype(BF16)
            for b in range(CAP):
                ypart[j, b % 2, b // 2, p] = part[b * BLK:(b + 1) * BLK, :]
        y_core(j).start()

    def stage_pair(j):
        y_core(j).wait_recv()
        ysend[j] = (ypart[j, core, 1 - y].astype(F32) + crecv[j, 1 - y].astype(F32)).astype(BF16)
        y_over(j).start()
        ysum[j] = ypart[j, core, y].astype(F32) + crecv[j, y].astype(F32)

    own = pl.ds(t * BLK, BLK)

    def stage_total(j):
        y_over(j).wait_recv()
        cols = columns(j)
        total = ysum[j] + yrecv[j].astype(F32)
        gate = mod_ref[t, 2:3, cols]
        residual = x_ref[own, cols].astype(F32) - t_ref[own, cols].astype(F32)
        mask = mask_ref[...]
        miss = residual + gate * total[0]
        miss_ref2 = residual + gate * total[1]
        slope = 2.0 * mask * miss
        miss_ref[:, cols] = slope
        vbuf[j, t] = (gate * slope).astype(BF16)
        v_copy(j, 0).start()
        v_copy(j, 1).start()
        err = jnp.concatenate([
            jnp.sum(mask * miss * miss, axis=(0, 1), keepdims=True),
            jnp.sum(mask * miss_ref2 * miss_ref2, axis=(0, 1), keepdims=True)], axis=0)
        return jnp.broadcast_to(err, (2, PAD))

    def stage_share(j):
        v_arrive(j, 1)
        v_copy(j, 2).start()

    def ready(j):
        x_arrive(1, 2 * j)
        x_arrive(1, 2 * j + 1)
        if j > 0:
            @pl.when(middle == 0)
            def _():
                side_relay(1, j)

    ready(0)
    stage_product(0)
    stage_pair(0)
    edge_relay(2)
    ready(1)
    stage_product(1)
    stage_pair(1)
    err = stage_total(0)
    edge_relay(3, (0,))
    ready(2)
    stage_product(2)
    stage_pair(2)
    edge_relay(3, (1,))
    err = err + stage_total(1)
    stage_share(0)
    err = err + stage_total(2)
    stage_share(1)
    ready(3)
    stage_product(3)
    stage_pair(3)
    err = err + stage_total(3)
    ebuf[t, 0:2, :] = err
    ebuf[t, 2:8, :] = jnp.zeros((6, PAD), F32)

    def e_copy(k):
        ref = ebuf.at[t]
        return copy(ref, ref, e_send.at[k], e_recv.at[k], peers[k])

    for k in range(3):
        e_copy(k).start()
    stage_share(2)
    stage_share(3)
    for k, peer in enumerate(peers):
        ref = ebuf.at[peer[1]]
        copy(ref, ref, e_send.at[k], e_recv.at[k], peer).wait_recv()
    gains = jnp.zeros((1, PAD), F32)
    loses = jnp.zeros((1, PAD), F32)
    for b in range(CAP):
        drop = ebuf[b, 0:1, :] - ebuf[b, 1:2, :]
        loser = flag_ref[b:b + 1, :]
        gains = gains + (1.0 - loser) * drop
        loses = loses + loser * drop
    inv_w, inv_l = 1.0 / (width * rows_w), 1.0 / (width * rows_l)
    outside = BETA * (gains * inv_w - loses * inv_l)
    loss = jnp.maximum(outside, 0.0) + jnp.log1p(jnp.exp(-jnp.abs(outside)))
    loss_ref[0] = loss[0, 0]
    weight = BETA * LOSS_SCALE / (1.0 + jnp.exp(-outside))
    loser = flag_ref[...]
    cf_ref[...] = weight * ((1.0 - loser) * inv_w - loser * inv_l)

    for j in range(4):
        v_arrive(j, 0)
        v_arrive(j, 2)

    @pl.loop(0, 4)
    def _(n):
        cols = pl.ds(pl.multiple_of(n * TILE, TILE), TILE)
        dh = jnp.zeros((CAP * BLK, TILE), F32)
        for j in range(4):
            dy = vbuf[j].reshape(CAP * BLK, TILE)
            dh = dh + jnp.dot(dy, w_ref[1, pl.ds(place[j] * TILE, TILE), cols],
                              preferred_element_type=F32)
        for b in range(CAP):
            block = slice(b * BLK, (b + 1) * BLK)
            dpre_ref[block, cols] = (
                dh[block] * (cf_ref[b:b + 1, 0:1] * slope_ref[block, cols])).astype(BF16)

    def dl_core():
        return copy(dlpart.at[1 - core], dlc, dc_send.at[4], dc_recv.at[4], mate)

    def dl_over():
        return copy(dlsend, dlrecv, dy_send.at[4], dy_recv.at[4], over)

    def dm_core(n):
        return copy(dmpart.at[n, 1 - core], dmc.at[n], dc_send.at[n], dc_recv.at[n], mate)

    def dm_over(n):
        return copy(dmsend.at[n], dmrecv.at[n], dy_send.at[n], dy_recv.at[n], over)

    def at_copy(k):
        return copy(gat.at[peers[k][1]], gatr.at[k], at_send.at[k], at_recv.at[k], peers[k])

    def rs_copy(which, k):
        to = (d + k) % 8
        part, land = ((gap, gapr), (gbp, gbr))[which]
        return copy(part.at[to], land.at[k], rs_send.at[which, k], rs_recv.at[which, k], (to, t))

    def ag_copy(which, k):
        to = (d + k) % 8
        ref = ga_ref.at[t, d] if which == 0 else gb_ref.at[d]
        return copy(ref, ref, ag_send.at[which, k], ag_recv.at[which, k], (to, t))

    def ag_arrive(which, k):
        source = (d + 8 - k) % 8
        ref = ga_ref.at[t, source] if which == 0 else gb_ref.at[source]
        copy(ref, ref, ag_send.at[which, k], ag_recv.at[which, k], (source, t)).wait_recv()

    dlowt = contract_trailing(b_ref[...], dpre_ref[...]).astype(BF16)
    ga = jnp.dot(dlowt, modded[...], preferred_element_type=F32).astype(BF16)
    for k in range(4):
        gat[k] = ga[k * 16:(k + 1) * 16, :]
    for k in range(3):
        at_copy(k).start()

    dlow = contract_trailing(dpre_ref[...], b_ref[...]).astype(BF16)
    for b in range(CAP):
        dlpart[b % 2, b // 2] = dlow[b * BLK:(b + 1) * BLK, :]
    dl_core().start()

    def dm_product(n):
        part = contract_trailing(
            dpre_ref[...], w_ref[0, n * TILE:(n + 1) * TILE, :]).astype(BF16)
        for b in range(CAP):
            dmpart[n, b % 2, b // 2] = part[b * BLK:(b + 1) * BLK, :]
        dm_core(n).start()

    def dm_pair(n):
        dm_core(n).wait_recv()
        dmsend[n] = (dmpart[n, core, 1 - y].astype(F32) + dmc[n, 1 - y].astype(F32)).astype(BF16)
        dm_over(n).start()
        dmsum[n] = dmpart[n, core, y].astype(F32) + dmc[n, y].astype(F32)

    dm_product(0)
    gb = jnp.dot(lowt_ref[...], dpre_ref[...], preferred_element_type=F32).astype(BF16)
    half_b = gb.shape[1] // 2
    for k in range(8):
        gbp[k] = gb[(k // 2) * 16:(k // 2 + 1) * 16, (k % 2) * half_b:(k % 2 + 1) * half_b]
    for k in range(1, 8):
        rs_copy(1, k).start()
    dm_pair(0)
    dl_core().wait_recv()
    dlsend[...] = (dlpart[core, 1 - y].astype(F32) + dlc[1 - y].astype(F32)).astype(BF16)
    dl_over().start()
    dlsum[...] = dlpart[core, y].astype(F32) + dlc[y].astype(F32)
    dm_product(1)
    total = gat[t].astype(F32)
    for k in range(3):
        at_copy(k).wait_recv()
        total = total + gatr[k].astype(F32)
    total = total.astype(BF16)
    wide = total.shape[1] // 8
    for k in range(8):
        gap[k] = total[:, k * wide:(k + 1) * wide]
    for k in range(1, 8):
        rs_copy(0, k).start()
    dm_pair(1)
    dm_product(2)
    dm_pair(2)
    dm_product(3)
    dm_pair(3)

    _, normed, inverse, _, scale, _ = norm(own, t)
    dl_over().wait_recv()
    dlow = (dlsum[...] + dlrecv[...].astype(F32)).astype(BF16)
    for n in range(4):
        dm_over(n).wait_recv()
    dm = jnp.concatenate([dmsum[n] + dmrecv[n].astype(F32) for n in range(4)], axis=1)
    dm = dm + jnp.dot(dlow, at_ref[...], preferred_element_type=F32)
    dn = dm * scale
    first = jnp.mean(dn, axis=-1, keepdims=True)
    second = jnp.mean(dn * normed, axis=-1, keepdims=True)
    out_grad = cf_ref[pl.ds(t, 1), 0:1] * miss_ref[...]
    grad_ref[t] = (out_grad + inverse * (dn - first - normed * second)).astype(BF16)

    def g_copy(which):
        ref = grad_ref.at[t_y] if which == 2 else grad_ref.at[t]
        return copy(ref, ref, g_send.at[which], g_recv.at[which], over if which == 1 else mate)

    def g_arrive(which):
        ref = grad_ref.at[[t_core, t_y, t_far][which]]
        copy(ref, ref, g_send.at[which], g_recv.at[which], mate).wait_recv()

    def g_store(k, block):
        return pltpu.make_async_copy(
            grad_ref.at[block], grad_out.at[pl.ds(block * BLK, BLK), :], local.at[7 + k])

    g_copy(1).start()
    g_copy(0).start()
    g_store(0, t).start()

    for which, (part, land) in ((1, (gbp, gbr)), (0, (gap, gapr))):
        total = part[d].astype(F32)
        for k in range(1, 8):
            rs_copy(which, k).wait_recv()
            total = total + land[k].astype(F32)
        if which == 1:
            gb_ref[d] = total.astype(BF16)
        else:
            ga_ref[t, d] = total.astype(BF16)
        for k in range(1, 8):
            ag_copy(which, k).start()

    g_arrive(1)
    g_copy(2).start()
    g_store(2, t_y).start()
    for k in range(1, 8):
        ag_arrive(0, k)

    def tg_copy(k):
        ref = ga_ref.at[t]
        return copy(ref, ref, tg_send.at[k], tg_recv.at[k], peers[k])

    for k in range(3):
        tg_copy(k).start()
    for k in range(1, 8):
        ag_arrive(1, k)
    for k in range(8):
        gb_out[(k // 2) * 16:(k // 2 + 1) * 16, (k % 2) * half_b:(k % 2 + 1) * half_b] = (
            gb_ref[k].astype(F32) * 0.125)
    g_arrive(0)
    g_store(1, t_core).start()
    g_arrive(2)
    g_store(3, t_far).start()
    for k, peer in enumerate(peers):
        ref = ga_ref.at[peer[1]]
        copy(ref, ref, tg_send.at[k], tg_recv.at[k], peer).wait_recv()
    for r in range(4):
        for k in range(8):
            ga_out[r * 16:(r + 1) * 16, k * wide:(k + 1) * wide] = (
                ga_ref[r, k].astype(F32) * 0.125)
    for k, block in enumerate((t, t_core, t_y, t_far)):
        g_store(k, block).wait()

    for m in range(2):
        for piece in range(9):
            x_copy(m, piece).wait_send()
        for kind in range(3):
            z_copy(m, kind, 0).wait_send()

            @pl.when(is_middle)
            def _():
                for which in range(1, 5):
                    z_copy(m, kind, which).wait_send()
    for j in range(4):
        y_core(j).wait_send()
        y_over(j).wait_send()
        dm_core(j).wait_send()
        dm_over(j).wait_send()
        for which in range(3):
            v_copy(j, which).wait_send()
    dl_core().wait_send()
    dl_over().wait_send()
    for k in range(3):
        e_copy(k).wait_send()
        at_copy(k).wait_send()
        g_copy(k).wait_send()
        tg_copy(k).wait_send()
    for which in range(2):
        for k in range(1, 8):
            rs_copy(which, k).wait_send()
            ag_copy(which, k).wait_send()


def fused_device(
    tokens, targets, modulation, live_block_count, preferred_blocks, last_block_rows,
    up_projection_weight, down_weight_transposed, adapter_input_factor, adapter_output_factor,
):
    width = tokens.shape[1]
    rank = adapter_input_factor.shape[1]
    hidden = adapter_output_factor.shape[1]
    dma = pltpu.SemaphoreType.DMA
    vm = pltpu.VMEM
    rows = CAP * BLK
    smem = pl.BlockSpec(memory_space=pltpu.SMEM)
    anywhere = pl.BlockSpec(memory_space=pl.ANY)
    whole = pl.BlockSpec(memory_space=pltpu.VMEM)
    losses, grad, grad_a, grad_b = pl.pallas_call(
        step_kernel,
        out_shape=(
            jax.ShapeDtypeStruct((1,), F32),
            jax.ShapeDtypeStruct((rows, width), BF16),
            jax.ShapeDtypeStruct((rank, width), F32),
            jax.ShapeDtypeStruct((rank, hidden), F32),
        ),
        in_specs=[smem] * 3 + [anywhere] * 7,
        out_specs=(smem, anywhere, whole, whole),
        scratch_shapes=[
            vm((rows, width), BF16),
            vm((rows, width), BF16),
            vm((3, 2, width), BF16),
            vm((PAD, hidden), BF16),
            vm((PAD, width), BF16),
            vm((CAP, 3, width), F32),
            vm((BLK, 1), F32),
            vm((8, PAD), F32),
            vm((CAP, BLK, width), BF16),
            vm((4, 8, 16, width // 8), BF16),
            vm((8, 16, hidden // 2), BF16),
            dma((11,)),
            vm((2, width, hidden), BF16),
            vm((rows, width), BF16),
            vm((rows, PAD), BF16),
            vm((PAD, rows), BF16),
            vm((rows, hidden), F32),
            vm((2, rows, hidden), BF16),
            vm((4, 2, 2, 2, BLK, TILE), BF16),
            vm((4, 2, 2, BLK, TILE), BF16),
            vm((4, 2, BLK, TILE), BF16),
            vm((4, 2, BLK, TILE), BF16),
            vm((4, 2, BLK, TILE), F32),
            vm((BLK, width), F32),
            vm((4, CAP, BLK, TILE), BF16),
            vm((CAP, 8, PAD), F32),
            vm((8, PAD), F32),
            vm((rows, hidden), BF16),
            vm((4, 2, 2, BLK, TILE), BF16),
            vm((4, 2, BLK, TILE), BF16),
            vm((4, BLK, TILE), BF16),
            vm((4, BLK, TILE), BF16),
            vm((4, BLK, TILE), F32),
            vm((2, 2, BLK, PAD), BF16),
            vm((2, BLK, PAD), BF16),
            vm((BLK, PAD), BF16),
            vm((BLK, PAD), BF16),
            vm((BLK, PAD), F32),
            vm((4, 16, width), BF16),
            vm((3, 16, width), BF16),
            vm((8, 16, width // 8), BF16),
            vm((8, 16, width // 8), BF16),
            vm((8, 16, hidden // 2), BF16),
            vm((8, 16, hidden // 2), BF16),
            dma((2, 3, 5)), dma((2, 3, 4)), dma((2, 9)), dma((2, 9)),
            dma((4,)), dma((4,)), dma((4,)), dma((4,)), dma((4, 3)), dma((4, 3)),
            dma((3,)), dma((3,)), dma((5,)), dma((5,)), dma((5,)), dma((5,)),
            dma((3,)), dma((3,)), dma((3,)), dma((3,)),
            dma((2, 8)), dma((2, 8)), dma((2, 8)), dma((2, 8)), dma((3,)), dma((3,)),
        ],
        compiler_params=pltpu.CompilerParams(
            collective_id=0, has_side_effects=True, vmem_limit_bytes=60 * 1024 * 1024),
    )(live_block_count, preferred_blocks, last_block_rows, tokens, targets,
      modulation.transpose(1, 0, 2), up_projection_weight, down_weight_transposed,
      adapter_input_factor.T, adapter_output_factor)
    return losses, grad, grad_a.T, grad_b


def fits_fused(mesh):
    return dict(mesh.shape) == {"dp": 8, "tensor": 4}


def solution(mesh):
    return jax.shard_map(
        fused_device if fits_fused(mesh) else per_device,
        mesh=mesh,
        in_specs=(
            P("dp", None),
            P("dp", None),
            P("dp", None, None),
            P("dp"),
            P("dp"),
            P("dp", None),
            P("dp", "tensor"),
            P("dp", "tensor"),
            P(),
            P(None, "tensor"),
        ),
        out_specs=(P("dp"), P("dp", None), P(), P(None, "tensor")),
        check_vma=False,
    )
```

```python
import jax
import jax.numpy as jnp
from jax import lax
from jax.experimental import pallas as pl
from jax.experimental.pallas import tpu as pltpu
from jax.sharding import PartitionSpec as P

BLK = 64
CAP = 4


EPS = 1e-06
BETA = 20.0
LOSS_SCALE = 4096.0


def settle_gradients(value):
    return lax.optimization_barrier(value.astype(jnp.bfloat16)).astype(jnp.float32)


def layer_norm(image_blocks):
    wide = image_blocks.astype(jnp.float32)
    center = wide - jnp.mean(wide, axis=-1, keepdims=True)
    inverse_deviation = lax.rsqrt(jnp.mean(center * center, axis=-1, keepdims=True) + EPS)
    return (center * inverse_deviation, inverse_deviation)


def gelu_and_slope(pre):

    def act(value):
        return jax.nn.gelu(value, approximate=True)

    value, back = jax.vjp(act, pre)
    return (value, back(jnp.ones_like(pre))[0])


def contract_trailing(left, right):
    return lax.dot_general(
        left, right, (((1,), (1,)), ((), ())), preferred_element_type=jnp.float32
    )


def contract_first(left, right):
    return lax.dot_general(
        left, right, (((0,), (0,)), ((), ())), preferred_element_type=jnp.float32
    )


def slot_state(live_block_count, preferred_blocks, last_block_rows):
    count = live_block_count[0]
    wins = preferred_blocks[0]
    slots = jnp.arange(CAP, dtype=jnp.int32)
    flags = (slots >= wins).astype(jnp.int32)
    last = jnp.where(flags == 0, wins - 1, count - 1)
    tail = jnp.where(flags == 0, last_block_rows[0, 0], last_block_rows[0, 1])
    live = jnp.where(slots < count, jnp.where(slots == last, tail, BLK), 0)
    masks = (jnp.arange(BLK, dtype=jnp.int32)[None, :] < live[:, None]).astype(jnp.float32)
    own_counts = jnp.stack(
        [jnp.sum(jnp.where(flags == 0, live, 0)), jnp.sum(jnp.where(flags == 1, live, 0))]
    ).astype(jnp.float32)
    return flags, masks, own_counts


def per_device(
    tokens,
    targets,
    modulation,
    live_block_count,
    preferred_blocks,
    last_block_rows,
    up_projection_weight,
    down_weight_transposed,
    adapter_input_factor,
    adapter_output_factor,
):
    width = tokens.shape[1]
    n_dp = lax.axis_size("dp")
    here = lax.axis_index("dp")
    flags, masks, own_counts = slot_state(live_block_count, preferred_blocks, last_block_rows)
    blocks_x = tokens.reshape(CAP, BLK, width)
    blocks_t = targets.reshape(CAP, BLK, width)
    blocks_mod = jnp.where(flags[:, None, None] == 0, modulation[0][None], modulation[1][None])
    homes = jnp.full((CAP,), here, jnp.int32)
    work_x, work_t, work_mod = (blocks_x, blocks_t, blocks_mod)
    work_mask, work_flag, work_home = (masks, flags, homes)
    spots = work_x.shape[0]
    count_rows = spots * BLK
    samples = 2 * n_dp
    ids = work_home * 2 + work_flag
    picks = (ids[:, None] == jnp.arange(samples, dtype=jnp.int32)[None, :]).astype(jnp.float32)
    modulation_vectors = work_mod.astype(jnp.float32)
    shift = modulation_vectors[:, None, 0]
    modulation_scale = 1.0 + modulation_vectors[:, None, 1]
    output_gate = modulation_vectors[:, None, 2]
    normalized_input, inverse_deviation = layer_norm(work_x)
    modulated_input = (
        (normalized_input * modulation_scale + shift)
        .astype(jnp.bfloat16)
        .reshape(count_rows, width)
    )
    w_up, w_down = (
        lax.all_gather(up_projection_weight, "dp", axis=0, tiled=True),
        lax.all_gather(down_weight_transposed, "dp", axis=0, tiled=True),
    )
    low_rank_hidden = jnp.dot(
        modulated_input, adapter_input_factor, preferred_element_type=jnp.float32
    ).astype(jnp.bfloat16)
    reference_preactivation = jnp.dot(modulated_input, w_up, preferred_element_type=jnp.float32)
    policy_preactivation = reference_preactivation + jnp.dot(
        low_rank_hidden, adapter_output_factor, preferred_element_type=jnp.float32
    )
    act_pol, policy_activation_slope = gelu_and_slope(policy_preactivation)
    hid_pol = act_pol.astype(jnp.bfloat16)
    hid_ref = jax.nn.gelu(reference_preactivation, approximate=True).astype(jnp.bfloat16)
    part_pol = settle_gradients(contract_trailing(hid_pol, w_down))
    part_ref = settle_gradients(contract_trailing(hid_ref, w_down))
    sum_pol, sum_ref = (
        lax.psum(part_pol.astype(jnp.bfloat16), "tensor").astype(jnp.float32),
        lax.psum(part_ref.astype(jnp.bfloat16), "tensor").astype(jnp.float32),
    )
    x_part = work_x.astype(jnp.float32)
    t_part = work_t.astype(jnp.float32)
    wmask = work_mask[:, :, None]
    miss_pol = x_part + output_gate * sum_pol.reshape(spots, BLK, width) - t_part
    miss_ref = x_part + output_gate * sum_ref.reshape(spots, BLK, width) - t_part
    vec_pol = jnp.sum(jnp.sum(wmask * miss_pol * miss_pol, axis=(1, 2))[:, None] * picks, axis=0)
    vec_ref = jnp.sum(jnp.sum(wmask * miss_ref * miss_ref, axis=(1, 2))[:, None] * picks, axis=0)
    owned = (jnp.arange(samples, dtype=jnp.int32) // 2 == here).astype(jnp.float32) * jnp.tile(
        own_counts, n_dp
    )
    tot_pol, tot_ref, tot_rows = lax.psum((vec_pol, vec_ref, owned), "dp")
    scale_rows = 1.0 / (width * tot_rows)
    pair_gap = ((tot_pol - tot_ref) * scale_rows).reshape(n_dp, 2)
    inside = -BETA * (pair_gap[:, 0] - pair_gap[:, 1])
    losses = lax.dynamic_slice_in_dim(jax.nn.softplus(-inside), here, 1)
    weight = BETA * LOSS_SCALE * jax.nn.sigmoid(-inside)
    coef = jnp.stack([weight, -weight], axis=1).reshape(samples) * scale_rows
    slot_coef = jnp.sum(picks * coef[None, :], axis=1)
    out_grad = slot_coef[:, None, None] * 2.0 * wmask * miss_pol
    dy_part = (output_gate * out_grad).astype(jnp.bfloat16).reshape(count_rows, width)
    dh = jnp.dot(dy_part, w_down, preferred_element_type=jnp.float32)
    preactivation_gradient = (dh * policy_activation_slope).astype(jnp.bfloat16)
    grad_b = contract_first(low_rank_hidden, preactivation_gradient)
    low_rank_gradient_piece = settle_gradients(
        contract_trailing(preactivation_gradient, adapter_output_factor)
    )
    dm_part = settle_gradients(contract_trailing(preactivation_gradient, w_up))
    modulation_gradient_sum, dlow_sum = (
        lax.psum(dm_part.astype(jnp.bfloat16), "tensor").astype(jnp.float32),
        lax.psum(low_rank_gradient_piece.astype(jnp.bfloat16), "tensor").astype(jnp.float32),
    )
    low_rank_gradient = dlow_sum.astype(jnp.bfloat16)
    modulation_gradient = modulation_gradient_sum + contract_trailing(
        low_rank_gradient, adapter_input_factor
    )
    dn = modulation_gradient.reshape(spots, BLK, width) * modulation_scale
    first_sum = jnp.sum(dn, axis=-1, keepdims=True)
    second_sum = jnp.sum(dn * normalized_input, axis=-1, keepdims=True)
    back_part = inverse_deviation * (dn - first_sum / width - normalized_input * second_sum / width)
    grad_part = (out_grad + back_part).astype(jnp.bfloat16)
    grad_a = contract_first(modulated_input, low_rank_gradient)
    sum_a, sum_b = lax.psum((grad_a, grad_b), "dp")
    return (losses, grad_part.reshape(CAP * BLK, width), sum_a / n_dp, sum_b / n_dp)


MESH = pl.DeviceIdType.MESH
F32 = jnp.float32
BF16 = jnp.bfloat16
SIDE = 32
TILE = 384
PAD = 128
GELU_ROOT = 0.7978845608028654
GELU_CUBE = 0.044715


def activation(pre, want_slope):
    square = pre * pre
    bend = jnp.tanh(GELU_ROOT * pre * (1.0 + GELU_CUBE * square))
    half = 0.5 * (1.0 + bend)
    if not want_slope:
        return pre * half
    slope = half + 0.5 * pre * (1.0 - bend * bend) * GELU_ROOT * (1.0 + 3.0 * GELU_CUBE * square)
    return pre * half, slope


def step_kernel(
    live_ref, wins_ref, tail_ref, x_hbm, t_hbm, mod_hbm, up_ref, dn_ref, a_hbm, b_hbm,
    loss_ref, grad_out, ga_out, gb_out,
    x_ref, t_ref, mod_in, b_ref, at_ref, mod_ref, mask_ref, flag_ref,
    grad_ref, ga_ref, gb_ref, local,
    w_ref, modded, low_ref, lowt_ref, slope_ref, hid_ref,
    ypart, crecv, ysend, yrecv, ysum, miss_ref, vbuf, ebuf, cf_ref,
    dpre_ref, dmpart, dmc, dmsend, dmrecv, dmsum,
    dlpart, dlc, dlsend, dlrecv, dlsum,
    gat, gatr, gap, gapr, gbp, gbr,
    z_send, z_recv, x_send, x_recv, c_send, c_recv, y_send, y_recv, v_send, v_recv,
    e_send, e_recv, dc_send, dc_recv, dy_send, dy_recv, g_send, g_recv,
    at_send, at_recv, rs_send, rs_recv, ag_send, ag_recv, tg_send, tg_recv,
):
    d = lax.axis_index("dp")
    t = lax.axis_index("tensor")
    z, x = d // 2, d % 2
    y, core = t // 2, t % 2
    high = z // 2
    middle = (z + high) % 2
    base = [middle, 1 - middle, 2, 3]
    place = [p + high * (3 - 2 * p) for p in base]
    inner = ((z + 1 - 2 * high) * 2 + x, t)
    edge_z = z - 1 + 2 * high
    edge = ((edge_z * middle + (1 - middle) * (z + 1 - 2 * high)) * 2 + x, t)
    across = (z * 2 + 1 - x, t)
    t_core = y * 2 + 1 - core
    t_y = (1 - y) * 2 + core
    t_far = (1 - y) * 2 + 1 - core
    mate = (d, t_core)
    over = (d, t_y)
    far = (d, t_far)
    peers = [mate, over, far]
    is_middle = middle == 1

    barrier = pltpu.get_barrier_semaphore()
    for k in range(1, 8):
        pl.semaphore_signal(barrier, inc=1, device_id=((d + k) % 8, t), device_id_type=MESH)
    for peer in peers:
        pl.semaphore_signal(barrier, inc=1, device_id=peer, device_id_type=MESH)

    shard = up_ref.shape[0]
    main = shard - SIDE
    half = main // 2
    here = pl.ds(d * shard, shard)
    loads = [
        pltpu.make_async_copy(src, dst, local.at[k]) for k, (src, dst) in enumerate((
            (up_ref, w_ref.at[0, here, :]), (dn_ref, w_ref.at[1, here, :]),
            (x_hbm, x_ref), (mod_hbm, mod_in),
            (a_hbm, at_ref.at[pl.ds(0, a_hbm.shape[0]), :]),
            (b_hbm, b_ref.at[pl.ds(0, b_hbm.shape[0]), :]), (t_hbm, t_ref)))]
    for load in loads:
        load.start()
    loads[0].wait()
    loads[1].wait()
    pl.semaphore_wait(barrier, 10)

    def copy(src, dst, send, recv, device):
        return pltpu.make_async_remote_copy(
            src_ref=src, dst_ref=dst, send_sem=send, recv_sem=recv,
            device_id=device, device_id_type=MESH)

    def rows(m, kind, slot):
        column = 1 - x if kind == 2 else x
        start = (0, half, main)[kind]
        size = (half, shard - half, SIDE)[kind]
        return w_ref.at[m, pl.ds((place[slot] * 2 + column) * shard + start, size), :]

    def x_rows(m, piece, column):
        slot, part = (0, 2) if piece == 8 else (piece // 2, piece % 2)
        size = SIDE if part == 2 else half
        return w_ref.at[m, pl.ds((place[slot] * 2 + column) * shard + part * half, size), :]

    def z_copy(m, kind, which):
        slot = [0, 0, 1, 2, 3][which]
        target = [1 + middle, 1, 3, 2, 3][which]
        device = inner if which in (0, 2) else edge
        ref = rows(m, kind, slot)
        return copy(ref, ref, z_send.at[m, kind, which], z_recv.at[m, kind, target], device)

    def z_arrive(m, kind, slot):
        ref = rows(m, kind, slot)
        copy(ref, ref, z_send.at[m, kind, 0], z_recv.at[m, kind, slot], inner).wait_recv()

    def x_copy(m, piece):
        ref = x_rows(m, piece, x)
        return copy(ref, ref, x_send.at[m, piece], x_recv.at[m, piece], across)

    def x_arrive(m, piece):
        ref = x_rows(m, piece, 1 - x)
        copy(ref, ref, x_send.at[m, piece], x_recv.at[m, piece], across).wait_recv()

    def begin_inner(m):
        for part in range(2):
            z_copy(m, part, 0).start()

    def begin_x(m):
        x_copy(m, 8).start()
        for part in range(2):
            x_copy(m, part).start()

    def outward(i):
        return z_copy(i // 9, i % 3, (1, 3, 4)[i % 9 // 3])

    def push(*items):
        @pl.when(is_middle)
        def _():
            for i in items:
                m, kind, slot = i // 9, i % 3, (0, 2, 3)[i % 9 // 3]
                if slot > 0:
                    z_arrive(m, kind, slot)
                    if kind < 2:
                        x_copy(m, slot * 2 + kind).start()
                if i > 1:
                    outward(i - 2).wait_send()
                outward(i).start()

    def edge_relay(m, slot, parts=(0, 1)):
        @pl.when(middle == 0)
        def _():
            for part in parts:
                z_arrive(m, part, slot)
                x_copy(m, slot * 2 + part).start()

    def edge_side(m, slot):
        @pl.when(middle == 0)
        def _():
            z_arrive(m, 2, slot)

    def first_relay(m):
        for part in range(2):
            z_arrive(m, part, 1)

            @pl.when(is_middle)
            def _():
                z_copy(m, part, 2).start()

            x_copy(m, 2 + part).start()

    def first_side(m):
        z_arrive(m, 2, 1)

        @pl.when(is_middle)
        def _():
            z_copy(m, 2, 2).start()

    def side_begin(m):
        x_arrive(m, 8)
        z_copy(m, 2, 0).start()

    push(0, 1)
    begin_inner(0)
    begin_x(0)

    count, wins = live_ref[0], wins_ref[0]
    tail_w, tail_l = tail_ref[0, 0], tail_ref[0, 1]
    loser_here = t >= wins
    last = jnp.where(loser_here, count - 1, wins - 1)
    tail = jnp.where(loser_here, tail_l, tail_w)
    live = jnp.where(t < count, jnp.where(t == last, tail, BLK), 0)
    spot = lax.broadcasted_iota(jnp.int32, (BLK, 1), 0)
    mask_ref[...] = jnp.where(spot < live, 1.0, 0.0)
    line = lax.broadcasted_iota(jnp.int32, (8, PAD), 0)
    flag_ref[...] = jnp.where(line >= wins, 1.0, 0.0)
    width = x_ref.shape[1]
    rows_w = jnp.broadcast_to(((wins - 1) * BLK + tail_w).astype(F32), (1, PAD))
    rows_l = jnp.broadcast_to(((count - wins - 1) * BLK + tail_l).astype(F32), (1, PAD))
    for load in loads[2:]:
        load.wait()
    rank = a_hbm.shape[0]
    b_ref[rank:PAD, :] = jnp.zeros((PAD - rank, b_ref.shape[1]), BF16)
    at_ref[rank:PAD, :] = jnp.zeros((PAD - rank, width), BF16)
    for b in range(CAP):
        loser = flag_ref[b:b + 1, 0:1]
        mod_ref[b] = ((1.0 - loser) * mod_in[:, 0, :].astype(F32)
                      + loser * mod_in[:, 1, :].astype(F32))

    def norm(block, b):
        wide = x_ref[block, :].astype(F32)
        center = wide - jnp.mean(wide, axis=-1, keepdims=True)
        inverse = lax.rsqrt(jnp.mean(center * center, axis=-1, keepdims=True) + EPS)
        vectors = mod_ref[b]
        return wide, center * inverse, inverse, vectors[0:1], 1.0 + vectors[1:2], vectors[2:3]

    @pl.loop(0, CAP)
    def _(b):
        block = pl.ds(b * BLK, BLK)
        _, normed, _, shift, scale, _ = norm(block, b)
        modded[block, :] = (normed * scale + shift).astype(BF16)

    low_ref[...] = contract_trailing(modded[...], at_ref[...]).astype(BF16)
    lowt_ref[...] = contract_trailing(at_ref[...], modded[...]).astype(BF16)

    side_begin(0)
    push(2)
    first_relay(0)

    @pl.when(middle == 0)
    def _():
        begin_inner(1)

    first_side(0)
    edge_relay(0, 2)
    push(3, 4)
    begin_x(1)
    edge_side(0, 2)
    push(5)

    @pl.when(is_middle)
    def _():
        begin_inner(1)

    edge_relay(0, 3)
    push(6, 7)
    edge_side(0, 3)
    push(8, 9, 10)
    side_begin(1)
    push(11)
    first_relay(1)

    @pl.when(is_middle)
    def _():
        z_arrive(1, 2, 1)
        z_copy(1, 2, 2).start()

    for piece in range(8):
        x_arrive(0, piece)

    @pl.loop(0, 4)
    def _(n):
        cols = pl.ds(pl.multiple_of(n * TILE, TILE), TILE)
        pre = jnp.dot(modded[...], w_ref[0, :, cols], preferred_element_type=F32)
        hid_ref[1, :, cols] = activation(pre, False).astype(BF16)
        pol = pre + jnp.dot(low_ref[...], b_ref[:, cols], preferred_element_type=F32)
        act, slope = activation(pol, True)
        hid_ref[0, :, cols] = act.astype(BF16)
        slope_ref[:, cols] = slope

    def y_core(j):
        src = ypart.at[j, 1 - core]
        return copy(src, crecv.at[j], c_send.at[j], c_recv.at[j], mate)

    def y_over(j):
        return copy(ysend.at[j], yrecv.at[j], y_send.at[j], y_recv.at[j], over)

    def v_copy(j, which):
        if which == 2:
            ref = vbuf.at[j, t_y]
        else:
            ref = vbuf.at[j, t]
        device = over if which == 1 else mate
        return copy(ref, ref, v_send.at[j, which], v_recv.at[j, which], device)

    def v_arrive(j, which):
        ref = vbuf.at[j, [t_core, t_y, t_far][which]]
        copy(ref, ref, v_send.at[j, which], v_recv.at[j, which], mate).wait_recv()

    def columns(j):
        return pl.ds(pl.multiple_of(place[j] * TILE, TILE), TILE)

    def stage_product(j):
        @pl.loop(0, 2)
        def _(p):
            part = contract_trailing(hid_ref[p], w_ref[1, pl.ds(place[j] * TILE, TILE), :])
            part = part.astype(BF16)
            for b in range(CAP):
                ypart[j, b % 2, b // 2, p] = part[b * BLK:(b + 1) * BLK, :]
        y_core(j).start()

    def stage_pair(j):
        y_core(j).wait_recv()
        ysend[j] = (ypart[j, core, 1 - y].astype(F32) + crecv[j, 1 - y].astype(F32)).astype(BF16)
        y_over(j).start()
        ysum[j] = ypart[j, core, y].astype(F32) + crecv[j, y].astype(F32)

    own = pl.ds(t * BLK, BLK)

    def stage_total(j):
        y_over(j).wait_recv()
        cols = columns(j)
        total = ysum[j] + yrecv[j].astype(F32)
        gate = mod_ref[t, 2:3, cols]
        residual = x_ref[own, cols].astype(F32) - t_ref[own, cols].astype(F32)
        mask = mask_ref[...]
        miss = residual + gate * total[0]
        miss_ref2 = residual + gate * total[1]
        slope = 2.0 * mask * miss
        miss_ref[:, cols] = slope
        vbuf[j, t] = (gate * slope).astype(BF16)
        v_copy(j, 0).start()
        v_copy(j, 1).start()
        err = jnp.concatenate([
            jnp.sum(mask * miss * miss, axis=(0, 1), keepdims=True),
            jnp.sum(mask * miss_ref2 * miss_ref2, axis=(0, 1), keepdims=True)], axis=0)
        return jnp.broadcast_to(err, (2, PAD))

    def stage_share(j):
        v_arrive(j, 1)
        v_copy(j, 2).start()

    def ready(j):
        x_arrive(1, 2 * j)
        x_arrive(1, 2 * j + 1)
        if j > 0:
            edge_side(1, j)

    push(12)
    ready(0)
    stage_product(0)
    push(13)
    stage_pair(0)
    push(14)
    edge_relay(1, 2)
    ready(1)
    stage_product(1)
    stage_pair(1)
    push(15, 16)
    err = stage_total(0)
    edge_relay(1, 3, (0,))
    ready(2)
    stage_product(2)
    push(17)
    stage_pair(2)
    edge_relay(1, 3, (1,))
    err = err + stage_total(1)
    stage_share(0)
    err = err + stage_total(2)
    stage_share(1)
    ready(3)
    stage_product(3)
    stage_pair(3)
    err = err + stage_total(3)
    ebuf[t, 0:2, :] = err
    ebuf[t, 2:8, :] = jnp.zeros((6, PAD), F32)

    def e_copy(k):
        ref = ebuf.at[t]
        return copy(ref, ref, e_send.at[k], e_recv.at[k], peers[k])

    for k in range(3):
        e_copy(k).start()
    stage_share(2)
    stage_share(3)
    for k, peer in enumerate(peers):
        ref = ebuf.at[peer[1]]
        copy(ref, ref, e_send.at[k], e_recv.at[k], peer).wait_recv()
    gains = jnp.zeros((1, PAD), F32)
    loses = jnp.zeros((1, PAD), F32)
    for b in range(CAP):
        drop = ebuf[b, 0:1, :] - ebuf[b, 1:2, :]
        loser = flag_ref[b:b + 1, :]
        gains = gains + (1.0 - loser) * drop
        loses = loses + loser * drop
    inv_w, inv_l = 1.0 / (width * rows_w), 1.0 / (width * rows_l)
    outside = BETA * (gains * inv_w - loses * inv_l)
    loss = jnp.maximum(outside, 0.0) + jnp.log1p(jnp.exp(-jnp.abs(outside)))
    loss_ref[0] = loss[0, 0]
    weight = BETA * LOSS_SCALE / (1.0 + jnp.exp(-outside))
    loser = flag_ref[...]
    cf_ref[...] = weight * ((1.0 - loser) * inv_w - loser * inv_l)

    for j in range(4):
        v_arrive(j, 0)
        v_arrive(j, 2)

    @pl.loop(0, 4)
    def _(n):
        cols = pl.ds(pl.multiple_of(n * TILE, TILE), TILE)
        dh = jnp.zeros((CAP * BLK, TILE), F32)
        for j in range(4):
            dy = vbuf[j].reshape(CAP * BLK, TILE)
            dh = dh + jnp.dot(dy, w_ref[1, pl.ds(place[j] * TILE, TILE), cols],
                              preferred_element_type=F32)
        for b in range(CAP):
            block = slice(b * BLK, (b + 1) * BLK)
            dpre_ref[block, cols] = (
                dh[block] * (cf_ref[b:b + 1, 0:1] * slope_ref[block, cols])).astype(BF16)

    def dl_core():
        return copy(dlpart.at[1 - core], dlc, dc_send.at[4], dc_recv.at[4], mate)

    def dl_over():
        return copy(dlsend, dlrecv, dy_send.at[4], dy_recv.at[4], over)

    def dm_core(n):
        return copy(dmpart.at[n, 1 - core], dmc.at[n], dc_send.at[n], dc_recv.at[n], mate)

    def dm_over(n):
        return copy(dmsend.at[n], dmrecv.at[n], dy_send.at[n], dy_recv.at[n], over)

    def at_copy(k):
        return copy(gat.at[peers[k][1]], gatr.at[k], at_send.at[k], at_recv.at[k], peers[k])

    def rs_copy(which, k):
        to = (d + k) % 8
        part, land = ((gap, gapr), (gbp, gbr))[which]
        return copy(part.at[to], land.at[k], rs_send.at[which, k], rs_recv.at[which, k], (to, t))

    def ag_copy(which, k):
        to = (d + k) % 8
        ref = ga_ref.at[t, d] if which == 0 else gb_ref.at[d]
        return copy(ref, ref, ag_send.at[which, k], ag_recv.at[which, k], (to, t))

    def ag_arrive(which, k):
        source = (d + 8 - k) % 8
        ref = ga_ref.at[t, source] if which == 0 else gb_ref.at[source]
        copy(ref, ref, ag_send.at[which, k], ag_recv.at[which, k], (source, t)).wait_recv()

    dlowt = contract_trailing(b_ref[...], dpre_ref[...]).astype(BF16)
    ga = jnp.dot(dlowt, modded[...], preferred_element_type=F32).astype(BF16)
    for k in range(4):
        gat[k] = ga[k * 16:(k + 1) * 16, :]
    for k in range(3):
        at_copy(k).start()

    dlow = contract_trailing(dpre_ref[...], b_ref[...]).astype(BF16)
    for b in range(CAP):
        dlpart[b % 2, b // 2] = dlow[b * BLK:(b + 1) * BLK, :]
    dl_core().start()

    def dm_product(n):
        part = contract_trailing(
            dpre_ref[...], w_ref[0, n * TILE:(n + 1) * TILE, :]).astype(BF16)
        for b in range(CAP):
            dmpart[n, b % 2, b // 2] = part[b * BLK:(b + 1) * BLK, :]
        dm_core(n).start()

    def dm_pair(n):
        dm_core(n).wait_recv()
        dmsend[n] = (dmpart[n, core, 1 - y].astype(F32) + dmc[n, 1 - y].astype(F32)).astype(BF16)
        dm_over(n).start()
        dmsum[n] = dmpart[n, core, y].astype(F32) + dmc[n, y].astype(F32)

    dm_product(0)
    gb = jnp.dot(lowt_ref[...], dpre_ref[...], preferred_element_type=F32).astype(BF16)
    half_b = gb.shape[1] // 2
    for k in range(8):
        gbp[k] = gb[(k // 2) * 16:(k // 2 + 1) * 16, (k % 2) * half_b:(k % 2 + 1) * half_b]
    for k in range(1, 8):
        rs_copy(1, k).start()
    dm_pair(0)
    dl_core().wait_recv()
    dlsend[...] = (dlpart[core, 1 - y].astype(F32) + dlc[1 - y].astype(F32)).astype(BF16)
    dl_over().start()
    dlsum[...] = dlpart[core, y].astype(F32) + dlc[y].astype(F32)
    dm_product(1)
    total = gat[t].astype(F32)
    for k in range(3):
        at_copy(k).wait_recv()
        total = total + gatr[k].astype(F32)
    total = total.astype(BF16)
    wide = total.shape[1] // 8
    for k in range(8):
        gap[k] = total[:, k * wide:(k + 1) * wide]
    for k in range(1, 8):
        rs_copy(0, k).start()
    dm_pair(1)
    dm_product(2)
    dm_pair(2)
    dm_product(3)
    dm_pair(3)

    _, normed, inverse, _, scale, _ = norm(own, t)
    dl_over().wait_recv()
    dlow = (dlsum[...] + dlrecv[...].astype(F32)).astype(BF16)
    for n in range(4):
        dm_over(n).wait_recv()
    dm = jnp.concatenate([dmsum[n] + dmrecv[n].astype(F32) for n in range(4)], axis=1)
    dm = dm + jnp.dot(dlow, at_ref[...], preferred_element_type=F32)
    dn = dm * scale
    first = jnp.mean(dn, axis=-1, keepdims=True)
    second = jnp.mean(dn * normed, axis=-1, keepdims=True)
    out_grad = cf_ref[pl.ds(t, 1), 0:1] * miss_ref[...]
    grad_ref[t] = (out_grad + inverse * (dn - first - normed * second)).astype(BF16)

    def g_copy(which):
        ref = grad_ref.at[t_y] if which == 2 else grad_ref.at[t]
        return copy(ref, ref, g_send.at[which], g_recv.at[which], over if which == 1 else mate)

    def g_arrive(which):
        ref = grad_ref.at[[t_core, t_y, t_far][which]]
        copy(ref, ref, g_send.at[which], g_recv.at[which], mate).wait_recv()

    def g_store(k, block):
        return pltpu.make_async_copy(
            grad_ref.at[block], grad_out.at[pl.ds(block * BLK, BLK), :], local.at[7 + k])

    g_copy(1).start()
    g_copy(0).start()
    g_store(0, t).start()

    for which, (part, land) in ((1, (gbp, gbr)), (0, (gap, gapr))):
        total = part[d].astype(F32)
        for k in range(1, 8):
            rs_copy(which, k).wait_recv()
            total = total + land[k].astype(F32)
        if which == 1:
            gb_ref[d] = total.astype(BF16)
        else:
            ga_ref[t, d] = total.astype(BF16)
        for k in range(1, 8):
            ag_copy(which, k).start()

    g_arrive(1)
    g_copy(2).start()
    g_store(2, t_y).start()
    for k in range(1, 8):
        ag_arrive(0, k)

    def tg_copy(k):
        ref = ga_ref.at[t]
        return copy(ref, ref, tg_send.at[k], tg_recv.at[k], peers[k])

    for k in range(3):
        tg_copy(k).start()
    for k in range(1, 8):
        ag_arrive(1, k)
    for k in range(8):
        gb_out[(k // 2) * 16:(k // 2 + 1) * 16, (k % 2) * half_b:(k % 2 + 1) * half_b] = (
            gb_ref[k].astype(F32) * 0.125)
    g_arrive(0)
    g_store(1, t_core).start()
    g_arrive(2)
    g_store(3, t_far).start()
    for k, peer in enumerate(peers):
        ref = ga_ref.at[peer[1]]
        copy(ref, ref, tg_send.at[k], tg_recv.at[k], peer).wait_recv()
    for r in range(4):
        for k in range(8):
            ga_out[r * 16:(r + 1) * 16, k * wide:(k + 1) * wide] = (
                ga_ref[r, k].astype(F32) * 0.125)
    for k, block in enumerate((t, t_core, t_y, t_far)):
        g_store(k, block).wait()

    for m in range(2):
        for piece in range(9):
            x_copy(m, piece).wait_send()
        for kind in range(3):
            z_copy(m, kind, 0).wait_send()

            @pl.when(is_middle)
            def _():
                z_copy(m, kind, 2).wait_send()

    @pl.when(is_middle)
    def _():
        outward(16).wait_send()
        outward(17).wait_send()
    for j in range(4):
        y_core(j).wait_send()
        y_over(j).wait_send()
        dm_core(j).wait_send()
        dm_over(j).wait_send()
        for which in range(3):
            v_copy(j, which).wait_send()
    dl_core().wait_send()
    dl_over().wait_send()
    for k in range(3):
        e_copy(k).wait_send()
        at_copy(k).wait_send()
        g_copy(k).wait_send()
        tg_copy(k).wait_send()
    for which in range(2):
        for k in range(1, 8):
            rs_copy(which, k).wait_send()
            ag_copy(which, k).wait_send()


def fused_device(
    tokens, targets, modulation, live_block_count, preferred_blocks, last_block_rows,
    up_projection_weight, down_weight_transposed, adapter_input_factor, adapter_output_factor,
):
    width = tokens.shape[1]
    rank = adapter_input_factor.shape[1]
    hidden = adapter_output_factor.shape[1]
    dma = pltpu.SemaphoreType.DMA
    vm = pltpu.VMEM
    rows = CAP * BLK
    smem = pl.BlockSpec(memory_space=pltpu.SMEM)
    anywhere = pl.BlockSpec(memory_space=pl.ANY)
    whole = pl.BlockSpec(memory_space=pltpu.VMEM)
    losses, grad, grad_a, grad_b = pl.pallas_call(
        step_kernel,
        out_shape=(
            jax.ShapeDtypeStruct((1,), F32),
            jax.ShapeDtypeStruct((rows, width), BF16),
            jax.ShapeDtypeStruct((rank, width), F32),
            jax.ShapeDtypeStruct((rank, hidden), F32),
        ),
        in_specs=[smem] * 3 + [anywhere] * 7,
        out_specs=(smem, anywhere, whole, whole),
        scratch_shapes=[
            vm((rows, width), BF16),
            vm((rows, width), BF16),
            vm((3, 2, width), BF16),
            vm((PAD, hidden), BF16),
            vm((PAD, width), BF16),
            vm((CAP, 3, width), F32),
            vm((BLK, 1), F32),
            vm((8, PAD), F32),
            vm((CAP, BLK, width), BF16),
            vm((4, 8, 16, width // 8), BF16),
            vm((8, 16, hidden // 2), BF16),
            dma((11,)),
            vm((2, width, hidden), BF16),
            vm((rows, width), BF16),
            vm((rows, PAD), BF16),
            vm((PAD, rows), BF16),
            vm((rows, hidden), F32),
            vm((2, rows, hidden), BF16),
            vm((4, 2, 2, 2, BLK, TILE), BF16),
            vm((4, 2, 2, BLK, TILE), BF16),
            vm((4, 2, BLK, TILE), BF16),
            vm((4, 2, BLK, TILE), BF16),
            vm((4, 2, BLK, TILE), F32),
            vm((BLK, width), F32),
            vm((4, CAP, BLK, TILE), BF16),
            vm((CAP, 8, PAD), F32),
            vm((8, PAD), F32),
            vm((rows, hidden), BF16),
            vm((4, 2, 2, BLK, TILE), BF16),
            vm((4, 2, BLK, TILE), BF16),
            vm((4, BLK, TILE), BF16),
            vm((4, BLK, TILE), BF16),
            vm((4, BLK, TILE), F32),
            vm((2, 2, BLK, PAD), BF16),
            vm((2, BLK, PAD), BF16),
            vm((BLK, PAD), BF16),
            vm((BLK, PAD), BF16),
            vm((BLK, PAD), F32),
            vm((4, 16, width), BF16),
            vm((3, 16, width), BF16),
            vm((8, 16, width // 8), BF16),
            vm((8, 16, width // 8), BF16),
            vm((8, 16, hidden // 2), BF16),
            vm((8, 16, hidden // 2), BF16),
            dma((2, 3, 5)), dma((2, 3, 4)), dma((2, 9)), dma((2, 9)),
            dma((4,)), dma((4,)), dma((4,)), dma((4,)), dma((4, 3)), dma((4, 3)),
            dma((3,)), dma((3,)), dma((5,)), dma((5,)), dma((5,)), dma((5,)),
            dma((3,)), dma((3,)), dma((3,)), dma((3,)),
            dma((2, 8)), dma((2, 8)), dma((2, 8)), dma((2, 8)), dma((3,)), dma((3,)),
        ],
        compiler_params=pltpu.CompilerParams(
            collective_id=0, has_side_effects=True, vmem_limit_bytes=60 * 1024 * 1024),
    )(live_block_count, preferred_blocks, last_block_rows, tokens, targets,
      modulation.transpose(1, 0, 2), up_projection_weight, down_weight_transposed,
      adapter_input_factor.T, adapter_output_factor)
    return losses, grad, grad_a.T, grad_b


def fits_fused(mesh):
    return dict(mesh.shape) == {"dp": 8, "tensor": 4}


def solution(mesh):
    return jax.shard_map(
        fused_device if fits_fused(mesh) else per_device,
        mesh=mesh,
        in_specs=(
            P("dp", None),
            P("dp", None),
            P("dp", None, None),
            P("dp"),
            P("dp"),
            P("dp", None),
            P("dp", "tensor"),
            P("dp", "tensor"),
            P(),
            P(None, "tensor"),
        ),
        out_specs=(P("dp"), P("dp", None), P(), P(None, "tensor")),
        check_vma=False,
    )
```

```python
import jax
import jax.numpy as jnp
from jax import lax
from jax.experimental import pallas as pl
from jax.experimental.pallas import tpu as pltpu
from jax.sharding import PartitionSpec as P

BLK = 64
CAP = 4


EPS = 1e-06
BETA = 20.0
LOSS_SCALE = 4096.0


def settle_gradients(value):
    return lax.optimization_barrier(value.astype(jnp.bfloat16)).astype(jnp.float32)


def layer_norm(image_blocks):
    wide = image_blocks.astype(jnp.float32)
    center = wide - jnp.mean(wide, axis=-1, keepdims=True)
    inverse_deviation = lax.rsqrt(jnp.mean(center * center, axis=-1, keepdims=True) + EPS)
    return (center * inverse_deviation, inverse_deviation)


def gelu_and_slope(pre):

    def act(value):
        return jax.nn.gelu(value, approximate=True)

    value, back = jax.vjp(act, pre)
    return (value, back(jnp.ones_like(pre))[0])


def contract_trailing(left, right):
    return lax.dot_general(
        left, right, (((1,), (1,)), ((), ())), preferred_element_type=jnp.float32
    )


def contract_first(left, right):
    return lax.dot_general(
        left, right, (((0,), (0,)), ((), ())), preferred_element_type=jnp.float32
    )


def slot_state(live_block_count, preferred_blocks, last_block_rows):
    count = live_block_count[0]
    wins = preferred_blocks[0]
    slots = jnp.arange(CAP, dtype=jnp.int32)
    flags = (slots >= wins).astype(jnp.int32)
    last = jnp.where(flags == 0, wins - 1, count - 1)
    tail = jnp.where(flags == 0, last_block_rows[0, 0], last_block_rows[0, 1])
    live = jnp.where(slots < count, jnp.where(slots == last, tail, BLK), 0)
    masks = (jnp.arange(BLK, dtype=jnp.int32)[None, :] < live[:, None]).astype(jnp.float32)
    own_counts = jnp.stack(
        [jnp.sum(jnp.where(flags == 0, live, 0)), jnp.sum(jnp.where(flags == 1, live, 0))]
    ).astype(jnp.float32)
    return flags, masks, own_counts


def per_device(
    tokens,
    targets,
    modulation,
    live_block_count,
    preferred_blocks,
    last_block_rows,
    up_projection_weight,
    down_weight_transposed,
    adapter_input_factor,
    adapter_output_factor,
):
    width = tokens.shape[1]
    n_dp = lax.axis_size("dp")
    here = lax.axis_index("dp")
    flags, masks, own_counts = slot_state(live_block_count, preferred_blocks, last_block_rows)
    blocks_x = tokens.reshape(CAP, BLK, width)
    blocks_t = targets.reshape(CAP, BLK, width)
    blocks_mod = jnp.where(flags[:, None, None] == 0, modulation[0][None], modulation[1][None])
    homes = jnp.full((CAP,), here, jnp.int32)
    work_x, work_t, work_mod = (blocks_x, blocks_t, blocks_mod)
    work_mask, work_flag, work_home = (masks, flags, homes)
    spots = work_x.shape[0]
    count_rows = spots * BLK
    samples = 2 * n_dp
    ids = work_home * 2 + work_flag
    picks = (ids[:, None] == jnp.arange(samples, dtype=jnp.int32)[None, :]).astype(jnp.float32)
    modulation_vectors = work_mod.astype(jnp.float32)
    shift = modulation_vectors[:, None, 0]
    modulation_scale = 1.0 + modulation_vectors[:, None, 1]
    output_gate = modulation_vectors[:, None, 2]
    normalized_input, inverse_deviation = layer_norm(work_x)
    modulated_input = (
        (normalized_input * modulation_scale + shift)
        .astype(jnp.bfloat16)
        .reshape(count_rows, width)
    )
    w_up, w_down = (
        lax.all_gather(up_projection_weight, "dp", axis=0, tiled=True),
        lax.all_gather(down_weight_transposed, "dp", axis=0, tiled=True),
    )
    low_rank_hidden = jnp.dot(
        modulated_input, adapter_input_factor, preferred_element_type=jnp.float32
    ).astype(jnp.bfloat16)
    reference_preactivation = jnp.dot(modulated_input, w_up, preferred_element_type=jnp.float32)
    policy_preactivation = reference_preactivation + jnp.dot(
        low_rank_hidden, adapter_output_factor, preferred_element_type=jnp.float32
    )
    act_pol, policy_activation_slope = gelu_and_slope(policy_preactivation)
    hid_pol = act_pol.astype(jnp.bfloat16)
    hid_ref = jax.nn.gelu(reference_preactivation, approximate=True).astype(jnp.bfloat16)
    part_pol = settle_gradients(contract_trailing(hid_pol, w_down))
    part_ref = settle_gradients(contract_trailing(hid_ref, w_down))
    sum_pol, sum_ref = (
        lax.psum(part_pol.astype(jnp.bfloat16), "tensor").astype(jnp.float32),
        lax.psum(part_ref.astype(jnp.bfloat16), "tensor").astype(jnp.float32),
    )
    x_part = work_x.astype(jnp.float32)
    t_part = work_t.astype(jnp.float32)
    wmask = work_mask[:, :, None]
    miss_pol = x_part + output_gate * sum_pol.reshape(spots, BLK, width) - t_part
    miss_ref = x_part + output_gate * sum_ref.reshape(spots, BLK, width) - t_part
    vec_pol = jnp.sum(jnp.sum(wmask * miss_pol * miss_pol, axis=(1, 2))[:, None] * picks, axis=0)
    vec_ref = jnp.sum(jnp.sum(wmask * miss_ref * miss_ref, axis=(1, 2))[:, None] * picks, axis=0)
    owned = (jnp.arange(samples, dtype=jnp.int32) // 2 == here).astype(jnp.float32) * jnp.tile(
        own_counts, n_dp
    )
    tot_pol, tot_ref, tot_rows = lax.psum((vec_pol, vec_ref, owned), "dp")
    scale_rows = 1.0 / (width * tot_rows)
    pair_gap = ((tot_pol - tot_ref) * scale_rows).reshape(n_dp, 2)
    inside = -BETA * (pair_gap[:, 0] - pair_gap[:, 1])
    losses = lax.dynamic_slice_in_dim(jax.nn.softplus(-inside), here, 1)
    weight = BETA * LOSS_SCALE * jax.nn.sigmoid(-inside)
    coef = jnp.stack([weight, -weight], axis=1).reshape(samples) * scale_rows
    slot_coef = jnp.sum(picks * coef[None, :], axis=1)
    out_grad = slot_coef[:, None, None] * 2.0 * wmask * miss_pol
    dy_part = (output_gate * out_grad).astype(jnp.bfloat16).reshape(count_rows, width)
    dh = jnp.dot(dy_part, w_down, preferred_element_type=jnp.float32)
    preactivation_gradient = (dh * policy_activation_slope).astype(jnp.bfloat16)
    grad_b = contract_first(low_rank_hidden, preactivation_gradient)
    low_rank_gradient_piece = settle_gradients(
        contract_trailing(preactivation_gradient, adapter_output_factor)
    )
    dm_part = settle_gradients(contract_trailing(preactivation_gradient, w_up))
    modulation_gradient_sum, dlow_sum = (
        lax.psum(dm_part.astype(jnp.bfloat16), "tensor").astype(jnp.float32),
        lax.psum(low_rank_gradient_piece.astype(jnp.bfloat16), "tensor").astype(jnp.float32),
    )
    low_rank_gradient = dlow_sum.astype(jnp.bfloat16)
    modulation_gradient = modulation_gradient_sum + contract_trailing(
        low_rank_gradient, adapter_input_factor
    )
    dn = modulation_gradient.reshape(spots, BLK, width) * modulation_scale
    first_sum = jnp.sum(dn, axis=-1, keepdims=True)
    second_sum = jnp.sum(dn * normalized_input, axis=-1, keepdims=True)
    back_part = inverse_deviation * (dn - first_sum / width - normalized_input * second_sum / width)
    grad_part = (out_grad + back_part).astype(jnp.bfloat16)
    grad_a = contract_first(modulated_input, low_rank_gradient)
    sum_a, sum_b = lax.psum((grad_a, grad_b), "dp")
    return (losses, grad_part.reshape(CAP * BLK, width), sum_a / n_dp, sum_b / n_dp)


MESH = pl.DeviceIdType.MESH
F32 = jnp.float32
BF16 = jnp.bfloat16
SIDE = 32
TILE = 384
PAD = 128
GELU_ROOT = 0.7978845608028654
GELU_CUBE = 0.044715


def activation(pre, want_slope):
    square = pre * pre
    bend = jnp.tanh(GELU_ROOT * pre * (1.0 + GELU_CUBE * square))
    half = 0.5 * (1.0 + bend)
    if not want_slope:
        return pre * half
    slope = half + 0.5 * pre * (1.0 - bend * bend) * GELU_ROOT * (1.0 + 3.0 * GELU_CUBE * square)
    return pre * half, slope


def step_kernel(
    live_ref, wins_ref, tail_ref, x_hbm, t_hbm, mod_hbm, up_ref, dn_ref, a_hbm, b_hbm,
    loss_ref, grad_out, ga_out, gb_out,
    x_ref, t_ref, mod_in, b_ref, at_ref, mod_ref, mask_ref, flag_ref,
    grad_ref, ga_ref, gb_ref, ga_rows, local,
    w_ref, modded, low_ref, lowt_ref, slope_ref, hid_ref,
    ypart, crecv, ysend, yrecv, ysum, miss_ref, vbuf, ebuf, cf_ref,
    dpre_ref, dmpart, dmc, dmsend, dmrecv, dmsum,
    dlpart, dlc, dlsend, dlrecv, dlsum,
    gat, gatr, gap, gapr, gbp, gbr,
    z_send, z_recv, x_send, x_recv, c_send, c_recv, y_send, y_recv, v_send, v_recv,
    e_send, e_recv, dc_send, dc_recv, dy_send, dy_recv, g_send, g_recv,
    at_send, at_recv, rs_send, rs_recv, ag_send, ag_recv, tg_send, tg_recv,
):
    d = lax.axis_index("dp")
    t = lax.axis_index("tensor")
    z, x = d // 2, d % 2
    y, core = t // 2, t % 2
    high = z // 2
    middle = (z + high) % 2
    base = [middle, 1 - middle, 2, 3]
    place = [p + high * (3 - 2 * p) for p in base]
    inner = ((z + 1 - 2 * high) * 2 + x, t)
    edge_z = z - 1 + 2 * high
    edge = ((edge_z * middle + (1 - middle) * (z + 1 - 2 * high)) * 2 + x, t)
    across = (z * 2 + 1 - x, t)
    t_core = y * 2 + 1 - core
    t_y = (1 - y) * 2 + core
    t_far = (1 - y) * 2 + 1 - core
    mate = (d, t_core)
    over = (d, t_y)
    far = (d, t_far)
    peers = [mate, over, far]
    is_middle = middle == 1

    barrier = pltpu.get_barrier_semaphore()
    for k in range(1, 8):
        pl.semaphore_signal(barrier, inc=1, device_id=((d + k) % 8, t), device_id_type=MESH)
    for peer in peers:
        pl.semaphore_signal(barrier, inc=1, device_id=peer, device_id_type=MESH)

    shard = up_ref.shape[0]
    main = shard - SIDE
    half = main // 2
    here = pl.ds(d * shard, shard)
    loads = [
        pltpu.make_async_copy(src, dst, local.at[k]) for k, (src, dst) in enumerate((
            (up_ref, w_ref.at[0, here, :]), (dn_ref, w_ref.at[1, here, :]),
            (x_hbm, x_ref), (mod_hbm, mod_in),
            (a_hbm, at_ref.at[pl.ds(0, a_hbm.shape[0]), :]),
            (b_hbm, b_ref.at[pl.ds(0, b_hbm.shape[0]), :]), (t_hbm, t_ref)))]
    for load in loads:
        load.start()
    pl.semaphore_wait(barrier, 10)

    def copy(src, dst, send, recv, device):
        return pltpu.make_async_remote_copy(
            src_ref=src, dst_ref=dst, send_sem=send, recv_sem=recv,
            device_id=device, device_id_type=MESH)

    def rows(m, kind, slot):
        column = 1 - x if kind == 2 else x
        start = (0, half, main)[kind]
        size = (half, shard - half, SIDE)[kind]
        return w_ref.at[m, pl.ds((place[slot] * 2 + column) * shard + start, size), :]

    def x_rows(m, piece, column):
        slot, part = (0, 2) if piece == 8 else (piece // 2, piece % 2)
        size = SIDE if part == 2 else half
        return w_ref.at[m, pl.ds((place[slot] * 2 + column) * shard + part * half, size), :]

    def z_copy(m, kind, which):
        slot = [0, 0, 1, 2, 3][which]
        target = [1 + middle, 1, 3, 2, 3][which]
        device = inner if which in (0, 2) else edge
        ref = rows(m, kind, slot)
        src = ref
        if slot == 0 and kind < 2:
            start = (0, half)[kind]
            src = (up_ref, dn_ref)[m].at[pl.ds(start, (half, shard - half)[kind]), :]
        return copy(src, ref, z_send.at[m, kind, which], z_recv.at[m, kind, target], device)

    def z_arrive(m, kind, slot):
        ref = rows(m, kind, slot)
        copy(ref, ref, z_send.at[m, kind, 0], z_recv.at[m, kind, slot], inner).wait_recv()

    def x_copy(m, piece):
        ref = x_rows(m, piece, x)
        src = ref
        if piece in (0, 1, 8):
            start, size = {0: (0, half), 1: (half, half), 8: (main, SIDE)}[piece]
            src = (up_ref, dn_ref)[m].at[pl.ds(start, size), :]
        return copy(src, ref, x_send.at[m, piece], x_recv.at[m, piece], across)

    def x_arrive(m, piece):
        ref = x_rows(m, piece, 1 - x)
        copy(ref, ref, x_send.at[m, piece], x_recv.at[m, piece], across).wait_recv()

    def begin_inner(m):
        for part in range(2):
            z_copy(m, part, 0).start()

    def begin_x(m):
        x_copy(m, 8).start()
        for part in range(2):
            x_copy(m, part).start()

    def begin_edge(m):
        @pl.when(is_middle)
        def _():
            for part in range(2):
                z_copy(m, part, 1).start()

    def side_begin(m):
        x_arrive(m, 8)
        z_copy(m, 2, 0).start()

        @pl.when(is_middle)
        def _():
            z_copy(m, 2, 1).start()

    def relay_part(m, slot, part):
        z_arrive(m, part, slot)

        @pl.when(is_middle)
        def _():
            z_copy(m, part, slot + 1).start()

        x_copy(m, slot * 2 + part).start()

    def relay(m, slot):
        for part in range(2):
            relay_part(m, slot, part)

    def side_relay(m, slot):
        z_arrive(m, 2, slot)

        @pl.when(is_middle)
        def _():
            z_copy(m, 2, slot + 1).start()

    begin_edge(0)
    begin_inner(0)
    begin_x(0)

    count, wins = live_ref[0], wins_ref[0]
    tail_w, tail_l = tail_ref[0, 0], tail_ref[0, 1]
    loser_here = t >= wins
    last = jnp.where(loser_here, count - 1, wins - 1)
    tail = jnp.where(loser_here, tail_l, tail_w)
    live = jnp.where(t < count, jnp.where(t == last, tail, BLK), 0)
    spot = lax.broadcasted_iota(jnp.int32, (BLK, 1), 0)
    mask_ref[...] = jnp.where(spot < live, 1.0, 0.0)
    line = lax.broadcasted_iota(jnp.int32, (8, PAD), 0)
    flag_ref[...] = jnp.where(line >= wins, 1.0, 0.0)
    width = x_ref.shape[1]
    rows_w = jnp.broadcast_to(((wins - 1) * BLK + tail_w).astype(F32), (1, PAD))
    rows_l = jnp.broadcast_to(((count - wins - 1) * BLK + tail_l).astype(F32), (1, PAD))
    for load in loads:
        load.wait()
    rank = a_hbm.shape[0]
    b_ref[rank:PAD, :] = jnp.zeros((PAD - rank, b_ref.shape[1]), BF16)
    at_ref[rank:PAD, :] = jnp.zeros((PAD - rank, width), BF16)
    for b in range(CAP):
        loser = flag_ref[b:b + 1, 0:1]
        mod_ref[b] = ((1.0 - loser) * mod_in[:, 0, :].astype(F32)
                      + loser * mod_in[:, 1, :].astype(F32))

    def norm(block, b):
        wide = x_ref[block, :].astype(F32)
        center = wide - jnp.mean(wide, axis=-1, keepdims=True)
        inverse = lax.rsqrt(jnp.mean(center * center, axis=-1, keepdims=True) + EPS)
        vectors = mod_ref[b]
        return wide, center * inverse, inverse, vectors[0:1], 1.0 + vectors[1:2], vectors[2:3]

    @pl.loop(0, CAP)
    def _(b):
        block = pl.ds(b * BLK, BLK)
        _, normed, _, shift, scale, _ = norm(block, b)
        modded[block, :] = (normed * scale + shift).astype(BF16)

    low_ref[...] = contract_trailing(modded[...], at_ref[...]).astype(BF16)
    lowt_ref[...] = contract_trailing(at_ref[...], modded[...]).astype(BF16)

    side_begin(0)
    relay(0, 1)

    @pl.when(middle == 0)
    def _():
        begin_inner(1)

    begin_x(1)
    side_relay(0, 1)
    relay(0, 2)
    side_relay(0, 2)
    relay(0, 3)
    side_relay(0, 3)

    @pl.when(is_middle)
    def _():
        begin_inner(1)

    begin_edge(1)
    side_begin(1)

    @pl.when(is_middle)
    def _():
        for slot in range(1, 4):
            relay(1, slot)
            side_relay(1, slot)

    def edge_relay(slot, parts=(0, 1)):
        @pl.when(middle == 0)
        def _():
            for part in parts:
                relay_part(1, slot, part)

    edge_relay(1)
    for piece in range(8):
        x_arrive(0, piece)

    @pl.loop(0, 4)
    def _(n):
        cols = pl.ds(pl.multiple_of(n * TILE, TILE), TILE)
        pre = jnp.dot(modded[...], w_ref[0, :, cols], preferred_element_type=F32)
        hid_ref[1, :, cols] = activation(pre, False).astype(BF16)
        pol = pre + jnp.dot(low_ref[...], b_ref[:, cols], preferred_element_type=F32)
        act, slope = activation(pol, True)
        hid_ref[0, :, cols] = act.astype(BF16)
        slope_ref[:, cols] = slope

    def y_core(j):
        src = ypart.at[j, 1 - core]
        return copy(src, crecv.at[j], c_send.at[j], c_recv.at[j], mate)

    def y_over(j):
        return copy(ysend.at[j], yrecv.at[j], y_send.at[j], y_recv.at[j], over)

    def v_copy(j, which):
        ref = vbuf.at[t_y if which == 2 else t, :, columns(j)]
        device = over if which == 1 else mate
        return copy(ref, ref, v_send.at[j, which], v_recv.at[j, which], device)

    def v_arrive(j, which):
        ref = vbuf.at[[t_core, t_y, t_far][which], :, columns(j)]
        copy(ref, ref, v_send.at[j, which], v_recv.at[j, which], mate).wait_recv()

    def columns(j):
        return pl.ds(pl.multiple_of(place[j] * TILE, TILE), TILE)

    def stage_product(j):
        @pl.loop(0, 2)
        def _(p):
            part = contract_trailing(hid_ref[p], w_ref[1, pl.ds(place[j] * TILE, TILE), :])
            part = part.astype(BF16)
            for b in range(CAP):
                ypart[j, b % 2, b // 2, p] = part[b * BLK:(b + 1) * BLK, :]
        y_core(j).start()

    def stage_pair(j):
        y_core(j).wait_recv()
        ysend[j] = (ypart[j, core, 1 - y].astype(F32) + crecv[j, 1 - y].astype(F32)).astype(BF16)
        y_over(j).start()
        ysum[j] = ypart[j, core, y].astype(F32) + crecv[j, y].astype(F32)

    own = pl.ds(t * BLK, BLK)

    def stage_total(j):
        y_over(j).wait_recv()
        cols = columns(j)
        total = ysum[j] + yrecv[j].astype(F32)
        gate = mod_ref[t, 2:3, cols]
        residual = x_ref[own, cols].astype(F32) - t_ref[own, cols].astype(F32)
        mask = mask_ref[...]
        miss = residual + gate * total[0]
        miss_ref2 = residual + gate * total[1]
        slope = 2.0 * mask * miss
        miss_ref[:, cols] = slope
        vbuf[t, :, cols] = (gate * slope).astype(BF16)
        v_copy(j, 0).start()
        v_copy(j, 1).start()
        err = jnp.concatenate([
            jnp.sum(mask * miss * miss, axis=(0, 1), keepdims=True),
            jnp.sum(mask * miss_ref2 * miss_ref2, axis=(0, 1), keepdims=True)], axis=0)
        return jnp.broadcast_to(err, (2, PAD))

    def stage_share(j):
        v_arrive(j, 1)
        v_copy(j, 2).start()

    def ready(j):
        x_arrive(1, 2 * j)
        x_arrive(1, 2 * j + 1)
        if j > 0:
            @pl.when(middle == 0)
            def _():
                side_relay(1, j)

    ready(0)
    stage_product(0)
    stage_pair(0)
    edge_relay(2)
    ready(1)
    stage_product(1)
    stage_pair(1)
    err = stage_total(0)
    edge_relay(3, (0,))
    ready(2)
    stage_product(2)
    stage_pair(2)
    edge_relay(3, (1,))
    err = err + stage_total(1)
    stage_share(0)
    err = err + stage_total(2)
    stage_share(1)
    ready(3)
    stage_product(3)
    stage_pair(3)
    err = err + stage_total(3)
    ebuf[t, 0:2, :] = err
    ebuf[t, 2:8, :] = jnp.zeros((6, PAD), F32)

    def e_copy(k):
        ref = ebuf.at[t]
        return copy(ref, ref, e_send.at[k], e_recv.at[k], peers[k])

    for k in range(3):
        e_copy(k).start()
    stage_share(2)
    stage_share(3)
    for k, peer in enumerate(peers):
        ref = ebuf.at[peer[1]]
        copy(ref, ref, e_send.at[k], e_recv.at[k], peer).wait_recv()
    gains = jnp.zeros((1, PAD), F32)
    loses = jnp.zeros((1, PAD), F32)
    for b in range(CAP):
        drop = ebuf[b, 0:1, :] - ebuf[b, 1:2, :]
        loser = flag_ref[b:b + 1, :]
        gains = gains + (1.0 - loser) * drop
        loses = loses + loser * drop
    inv_w, inv_l = 1.0 / (width * rows_w), 1.0 / (width * rows_l)
    outside = BETA * (gains * inv_w - loses * inv_l)
    loss = jnp.maximum(outside, 0.0) + jnp.log1p(jnp.exp(-jnp.abs(outside)))
    loss_ref[0] = loss[0, 0]
    weight = BETA * LOSS_SCALE / (1.0 + jnp.exp(-outside))
    loser = flag_ref[...]
    cf_ref[...] = weight * ((1.0 - loser) * inv_w - loser * inv_l)

    for j in range(4):
        v_arrive(j, 0)
        v_arrive(j, 2)

    @pl.loop(0, 4)
    def _(n):
        cols = pl.ds(pl.multiple_of(n * TILE, TILE), TILE)
        dy = vbuf[...].reshape(CAP * BLK, vbuf.shape[2])
        dh = jnp.dot(dy, w_ref[1, :, cols], preferred_element_type=F32)
        for b in range(CAP):
            block = slice(b * BLK, (b + 1) * BLK)
            dpre_ref[block, cols] = (
                dh[block] * (cf_ref[b:b + 1, 0:1] * slope_ref[block, cols])).astype(BF16)

    def dl_core():
        return copy(dlpart.at[1 - core], dlc, dc_send.at[4], dc_recv.at[4], mate)

    def dl_over():
        return copy(dlsend, dlrecv, dy_send.at[4], dy_recv.at[4], over)

    def dm_core(n):
        return copy(dmpart.at[n, 1 - core], dmc.at[n], dc_send.at[n], dc_recv.at[n], mate)

    def dm_over(n):
        return copy(dmsend.at[n], dmrecv.at[n], dy_send.at[n], dy_recv.at[n], over)

    def at_copy(k):
        return copy(gat.at[peers[k][1]], gatr.at[k], at_send.at[k], at_recv.at[k], peers[k])

    def rs_copy(which, k):
        to = (d + k) % 8
        part, land = ((gap, gapr), (gbp, gbr))[which]
        return copy(part.at[to], land.at[k], rs_send.at[which, k], rs_recv.at[which, k], (to, t))

    def ag_copy(which, k):
        to = (d + k) % 8
        ref = ga_ref.at[t, d] if which == 0 else gb_ref.at[d]
        return copy(ref, ref, ag_send.at[which, k], ag_recv.at[which, k], (to, t))

    def ag_arrive(which, k):
        source = (d + 8 - k) % 8
        ref = ga_ref.at[t, source] if which == 0 else gb_ref.at[source]
        copy(ref, ref, ag_send.at[which, k], ag_recv.at[which, k], (source, t)).wait_recv()

    dlowt = contract_trailing(b_ref[...], dpre_ref[...]).astype(BF16)
    ga = jnp.dot(dlowt, modded[...], preferred_element_type=F32).astype(BF16)
    for k in range(4):
        gat[k] = ga[k * 16:(k + 1) * 16, :]
    for k in range(3):
        at_copy(k).start()

    dlow = contract_trailing(dpre_ref[...], b_ref[...]).astype(BF16)
    for b in range(CAP):
        dlpart[b % 2, b // 2] = dlow[b * BLK:(b + 1) * BLK, :]
    dl_core().start()

    def dm_product(n):
        part = contract_trailing(
            dpre_ref[...], w_ref[0, n * TILE:(n + 1) * TILE, :]).astype(BF16)
        for b in range(CAP):
            dmpart[n, b % 2, b // 2] = part[b * BLK:(b + 1) * BLK, :]
        dm_core(n).start()

    def dm_pair(n):
        dm_core(n).wait_recv()
        dmsend[n] = (dmpart[n, core, 1 - y].astype(F32) + dmc[n, 1 - y].astype(F32)).astype(BF16)
        dm_over(n).start()
        dmsum[n] = dmpart[n, core, y].astype(F32) + dmc[n, y].astype(F32)

    dm_product(0)
    gb = jnp.dot(lowt_ref[...], dpre_ref[...], preferred_element_type=F32).astype(BF16)
    half_b = gb.shape[1] // 2
    for k in range(8):
        gbp[k] = gb[(k // 2) * 16:(k // 2 + 1) * 16, (k % 2) * half_b:(k % 2 + 1) * half_b]
    for k in range(1, 8):
        rs_copy(1, k).start()
    dm_pair(0)
    dl_core().wait_recv()
    dlsend[...] = (dlpart[core, 1 - y].astype(F32) + dlc[1 - y].astype(F32)).astype(BF16)
    dl_over().start()
    dlsum[...] = dlpart[core, y].astype(F32) + dlc[y].astype(F32)
    dm_product(1)
    total = gat[t].astype(F32)
    for k in range(3):
        at_copy(k).wait_recv()
        total = total + gatr[k].astype(F32)
    total = total.astype(BF16)
    wide = total.shape[1] // 8
    for k in range(8):
        gap[k] = total[:, k * wide:(k + 1) * wide]
    for k in range(1, 8):
        rs_copy(0, k).start()
    dm_pair(1)
    dm_product(2)
    dm_pair(2)
    dm_product(3)
    dm_pair(3)

    for which, (part, land) in ((0, (gap, gapr)), (1, (gbp, gbr))):
        total = part[d].astype(F32)
        for k in range(1, 8):
            rs_copy(which, k).wait_recv()
            total = total + land[k].astype(F32)
        if which == 1:
            gb_ref[d] = total.astype(BF16)
        else:
            ga_ref[t, d] = total.astype(BF16)
        for k in range(1, 8):
            ag_copy(which, k).start()

    _, normed, inverse, _, scale, _ = norm(own, t)
    dl_over().wait_recv()
    dlow = (dlsum[...] + dlrecv[...].astype(F32)).astype(BF16)
    for n in range(4):
        dm_over(n).wait_recv()
    dm = jnp.concatenate([dmsum[n] + dmrecv[n].astype(F32) for n in range(4)], axis=1)
    dm = dm + jnp.dot(dlow, at_ref[...], preferred_element_type=F32)
    dn = dm * scale
    first = jnp.mean(dn, axis=-1, keepdims=True)
    second = jnp.mean(dn * normed, axis=-1, keepdims=True)
    out_grad = cf_ref[pl.ds(t, 1), 0:1] * miss_ref[...]
    for k in range(1, 8):
        ag_arrive(0, k)
    for k in range(8):
        ga_rows[t, :, k * wide:(k + 1) * wide] = ga_ref[t, k]

    def tg_copy(which):
        ref = ga_rows.at[t_y if which == 2 else t]
        return copy(ref, ref, tg_send.at[which], tg_recv.at[which],
                    over if which == 1 else mate)

    def tg_arrive(which):
        ref = ga_rows.at[[t_core, t_y, t_far][which]]
        copy(ref, ref, tg_send.at[which], tg_recv.at[which], mate).wait_recv()

    grad_ref[t] = (out_grad + inverse * (dn - first - normed * second)).astype(BF16)

    def g_copy(which):
        ref = grad_ref.at[t_y] if which == 2 else grad_ref.at[t]
        return copy(ref, ref, g_send.at[which], g_recv.at[which], over if which == 1 else mate)

    def g_arrive(which):
        ref = grad_ref.at[[t_core, t_y, t_far][which]]
        copy(ref, ref, g_send.at[which], g_recv.at[which], mate).wait_recv()

    def g_store(k, block):
        return pltpu.make_async_copy(
            grad_ref.at[block], grad_out.at[pl.ds(block * BLK, BLK), :], local.at[7 + k])

    g_copy(1).start()
    g_copy(0).start()
    tg_copy(1).start()
    tg_copy(0).start()
    g_store(0, t).start()

    g_arrive(1)
    g_copy(2).start()
    g_store(2, t_y).start()
    tg_arrive(1)
    tg_copy(2).start()
    for k in range(1, 8):
        ag_arrive(1, k)
    for k in range(8):
        gb_out[(k // 2) * 16:(k // 2 + 1) * 16, (k % 2) * half_b:(k % 2 + 1) * half_b] = (
            gb_ref[k])
    g_arrive(0)
    g_store(1, t_core).start()
    g_arrive(2)
    g_store(3, t_far).start()
    tg_arrive(0)
    tg_arrive(2)
    ga_out[...] = ga_rows[...].reshape(ga_out.shape)
    for k, block in enumerate((t, t_core, t_y, t_far)):
        g_store(k, block).wait()

    for m in range(2):
        for piece in range(9):
            x_copy(m, piece).wait_send()
        for kind in range(3):
            z_copy(m, kind, 0).wait_send()

            @pl.when(is_middle)
            def _():
                for which in range(1, 5):
                    z_copy(m, kind, which).wait_send()
    for j in range(4):
        y_core(j).wait_send()
        y_over(j).wait_send()
        dm_core(j).wait_send()
        dm_over(j).wait_send()
        for which in range(3):
            v_copy(j, which).wait_send()
    dl_core().wait_send()
    dl_over().wait_send()
    for k in range(3):
        e_copy(k).wait_send()
        at_copy(k).wait_send()
        g_copy(k).wait_send()
        tg_copy(k).wait_send()
    for which in range(2):
        for k in range(1, 8):
            rs_copy(which, k).wait_send()
            ag_copy(which, k).wait_send()


def fused_device(
    tokens, targets, modulation, live_block_count, preferred_blocks, last_block_rows,
    up_projection_weight, down_weight_transposed, adapter_input_factor, adapter_output_factor,
):
    width = tokens.shape[1]
    rank = adapter_input_factor.shape[1]
    hidden = adapter_output_factor.shape[1]
    dma = pltpu.SemaphoreType.DMA
    vm = pltpu.VMEM
    rows = CAP * BLK
    smem = pl.BlockSpec(memory_space=pltpu.SMEM)
    anywhere = pl.BlockSpec(memory_space=pl.ANY)
    whole = pl.BlockSpec(memory_space=pltpu.VMEM)
    losses, grad, grad_a, grad_b = pl.pallas_call(
        step_kernel,
        out_shape=(
            jax.ShapeDtypeStruct((1,), F32),
            jax.ShapeDtypeStruct((rows, width), BF16),
            jax.ShapeDtypeStruct((rank, width), BF16),
            jax.ShapeDtypeStruct((rank, hidden), BF16),
        ),
        in_specs=[smem] * 3 + [anywhere] * 7,
        out_specs=(smem, anywhere, whole, whole),
        scratch_shapes=[
            vm((rows, width), BF16),
            vm((rows, width), BF16),
            vm((3, 2, width), BF16),
            vm((PAD, hidden), BF16),
            vm((PAD, width), BF16),
            vm((CAP, 3, width), F32),
            vm((BLK, 1), F32),
            vm((8, PAD), F32),
            vm((CAP, BLK, width), BF16),
            vm((4, 8, 16, width // 8), BF16),
            vm((8, 16, hidden // 2), BF16),
            vm((4, 16, width), BF16),
            dma((11,)),
            vm((2, width, hidden), BF16),
            vm((rows, width), BF16),
            vm((rows, PAD), BF16),
            vm((PAD, rows), BF16),
            vm((rows, hidden), F32),
            vm((2, rows, hidden), BF16),
            vm((4, 2, 2, 2, BLK, TILE), BF16),
            vm((4, 2, 2, BLK, TILE), BF16),
            vm((4, 2, BLK, TILE), BF16),
            vm((4, 2, BLK, TILE), BF16),
            vm((4, 2, BLK, TILE), F32),
            vm((BLK, width), F32),
            vm((CAP, BLK, width), BF16),
            vm((CAP, 8, PAD), F32),
            vm((8, PAD), F32),
            vm((rows, hidden), BF16),
            vm((4, 2, 2, BLK, TILE), BF16),
            vm((4, 2, BLK, TILE), BF16),
            vm((4, BLK, TILE), BF16),
            vm((4, BLK, TILE), BF16),
            vm((4, BLK, TILE), F32),
            vm((2, 2, BLK, PAD), BF16),
            vm((2, BLK, PAD), BF16),
            vm((BLK, PAD), BF16),
            vm((BLK, PAD), BF16),
            vm((BLK, PAD), F32),
            vm((4, 16, width), BF16),
            vm((3, 16, width), BF16),
            vm((8, 16, width // 8), BF16),
            vm((8, 16, width // 8), BF16),
            vm((8, 16, hidden // 2), BF16),
            vm((8, 16, hidden // 2), BF16),
            dma((2, 3, 5)), dma((2, 3, 4)), dma((2, 9)), dma((2, 9)),
            dma((4,)), dma((4,)), dma((4,)), dma((4,)), dma((4, 3)), dma((4, 3)),
            dma((3,)), dma((3,)), dma((5,)), dma((5,)), dma((5,)), dma((5,)),
            dma((3,)), dma((3,)), dma((3,)), dma((3,)),
            dma((2, 8)), dma((2, 8)), dma((2, 8)), dma((2, 8)), dma((3,)), dma((3,)),
        ],
        compiler_params=pltpu.CompilerParams(
            collective_id=0, has_side_effects=True, vmem_limit_bytes=60 * 1024 * 1024),
    )(live_block_count, preferred_blocks, last_block_rows, tokens, targets,
      modulation.transpose(1, 0, 2), up_projection_weight, down_weight_transposed,
      adapter_input_factor.T, adapter_output_factor)
    n_dp = lax.axis_size("dp")
    return losses, grad, grad_a.T.astype(F32) / n_dp, grad_b.astype(F32) / n_dp


def fits_fused(mesh):
    return dict(mesh.shape) == {"dp": 8, "tensor": 4}


def solution(mesh):
    return jax.shard_map(
        fused_device if fits_fused(mesh) else per_device,
        mesh=mesh,
        in_specs=(
            P("dp", None),
            P("dp", None),
            P("dp", None, None),
            P("dp"),
            P("dp"),
            P("dp", None),
            P("dp", "tensor"),
            P("dp", "tensor"),
            P(),
            P(None, "tensor"),
        ),
        out_specs=(P("dp"), P("dp", None), P(), P(None, "tensor")),
        check_vma=False,
    )
```

```python
import jax
import jax.numpy as jnp
from jax import lax
from jax.experimental import pallas as pl
from jax.experimental.pallas import tpu as pltpu
from jax.sharding import PartitionSpec as P

BLK = 64
CAP = 4


EPS = 1e-06
BETA = 20.0
LOSS_SCALE = 4096.0


def settle_gradients(value):
    return lax.optimization_barrier(value.astype(jnp.bfloat16)).astype(jnp.float32)


def layer_norm(image_blocks):
    wide = image_blocks.astype(jnp.float32)
    center = wide - jnp.mean(wide, axis=-1, keepdims=True)
    inverse_deviation = lax.rsqrt(jnp.mean(center * center, axis=-1, keepdims=True) + EPS)
    return (center * inverse_deviation, inverse_deviation)


def gelu_and_slope(pre):

    def act(value):
        return jax.nn.gelu(value, approximate=True)

    value, back = jax.vjp(act, pre)
    return (value, back(jnp.ones_like(pre))[0])


def contract_trailing(left, right):
    return lax.dot_general(
        left, right, (((1,), (1,)), ((), ())), preferred_element_type=jnp.float32
    )


def contract_first(left, right):
    return lax.dot_general(
        left, right, (((0,), (0,)), ((), ())), preferred_element_type=jnp.float32
    )


def slot_state(live_block_count, preferred_blocks, last_block_rows):
    count = live_block_count[0]
    wins = preferred_blocks[0]
    slots = jnp.arange(CAP, dtype=jnp.int32)
    flags = (slots >= wins).astype(jnp.int32)
    last = jnp.where(flags == 0, wins - 1, count - 1)
    tail = jnp.where(flags == 0, last_block_rows[0, 0], last_block_rows[0, 1])
    live = jnp.where(slots < count, jnp.where(slots == last, tail, BLK), 0)
    masks = (jnp.arange(BLK, dtype=jnp.int32)[None, :] < live[:, None]).astype(jnp.float32)
    own_counts = jnp.stack(
        [jnp.sum(jnp.where(flags == 0, live, 0)), jnp.sum(jnp.where(flags == 1, live, 0))]
    ).astype(jnp.float32)
    return flags, masks, own_counts


def per_device(
    tokens,
    targets,
    modulation,
    live_block_count,
    preferred_blocks,
    last_block_rows,
    up_projection_weight,
    down_weight_transposed,
    adapter_input_factor,
    adapter_output_factor,
):
    width = tokens.shape[1]
    n_dp = lax.axis_size("dp")
    here = lax.axis_index("dp")
    flags, masks, own_counts = slot_state(live_block_count, preferred_blocks, last_block_rows)
    blocks_x = tokens.reshape(CAP, BLK, width)
    blocks_t = targets.reshape(CAP, BLK, width)
    blocks_mod = jnp.where(flags[:, None, None] == 0, modulation[0][None], modulation[1][None])
    homes = jnp.full((CAP,), here, jnp.int32)
    work_x, work_t, work_mod = (blocks_x, blocks_t, blocks_mod)
    work_mask, work_flag, work_home = (masks, flags, homes)
    spots = work_x.shape[0]
    count_rows = spots * BLK
    samples = 2 * n_dp
    ids = work_home * 2 + work_flag
    picks = (ids[:, None] == jnp.arange(samples, dtype=jnp.int32)[None, :]).astype(jnp.float32)
    modulation_vectors = work_mod.astype(jnp.float32)
    shift = modulation_vectors[:, None, 0]
    modulation_scale = 1.0 + modulation_vectors[:, None, 1]
    output_gate = modulation_vectors[:, None, 2]
    normalized_input, inverse_deviation = layer_norm(work_x)
    modulated_input = (
        (normalized_input * modulation_scale + shift)
        .astype(jnp.bfloat16)
        .reshape(count_rows, width)
    )
    w_up, w_down = (
        lax.all_gather(up_projection_weight, "dp", axis=0, tiled=True),
        lax.all_gather(down_weight_transposed, "dp", axis=0, tiled=True),
    )
    low_rank_hidden = jnp.dot(
        modulated_input, adapter_input_factor, preferred_element_type=jnp.float32
    ).astype(jnp.bfloat16)
    reference_preactivation = jnp.dot(modulated_input, w_up, preferred_element_type=jnp.float32)
    policy_preactivation = reference_preactivation + jnp.dot(
        low_rank_hidden, adapter_output_factor, preferred_element_type=jnp.float32
    )
    act_pol, policy_activation_slope = gelu_and_slope(policy_preactivation)
    hid_pol = act_pol.astype(jnp.bfloat16)
    hid_ref = jax.nn.gelu(reference_preactivation, approximate=True).astype(jnp.bfloat16)
    part_pol = settle_gradients(contract_trailing(hid_pol, w_down))
    part_ref = settle_gradients(contract_trailing(hid_ref, w_down))
    sum_pol, sum_ref = (
        lax.psum(part_pol.astype(jnp.bfloat16), "tensor").astype(jnp.float32),
        lax.psum(part_ref.astype(jnp.bfloat16), "tensor").astype(jnp.float32),
    )
    x_part = work_x.astype(jnp.float32)
    t_part = work_t.astype(jnp.float32)
    wmask = work_mask[:, :, None]
    miss_pol = x_part + output_gate * sum_pol.reshape(spots, BLK, width) - t_part
    miss_ref = x_part + output_gate * sum_ref.reshape(spots, BLK, width) - t_part
    vec_pol = jnp.sum(jnp.sum(wmask * miss_pol * miss_pol, axis=(1, 2))[:, None] * picks, axis=0)
    vec_ref = jnp.sum(jnp.sum(wmask * miss_ref * miss_ref, axis=(1, 2))[:, None] * picks, axis=0)
    owned = (jnp.arange(samples, dtype=jnp.int32) // 2 == here).astype(jnp.float32) * jnp.tile(
        own_counts, n_dp
    )
    tot_pol, tot_ref, tot_rows = lax.psum((vec_pol, vec_ref, owned), "dp")
    scale_rows = 1.0 / (width * tot_rows)
    pair_gap = ((tot_pol - tot_ref) * scale_rows).reshape(n_dp, 2)
    inside = -BETA * (pair_gap[:, 0] - pair_gap[:, 1])
    losses = lax.dynamic_slice_in_dim(jax.nn.softplus(-inside), here, 1)
    weight = BETA * LOSS_SCALE * jax.nn.sigmoid(-inside)
    coef = jnp.stack([weight, -weight], axis=1).reshape(samples) * scale_rows
    slot_coef = jnp.sum(picks * coef[None, :], axis=1)
    out_grad = slot_coef[:, None, None] * 2.0 * wmask * miss_pol
    dy_part = (output_gate * out_grad).astype(jnp.bfloat16).reshape(count_rows, width)
    dh = jnp.dot(dy_part, w_down, preferred_element_type=jnp.float32)
    preactivation_gradient = (dh * policy_activation_slope).astype(jnp.bfloat16)
    grad_b = contract_first(low_rank_hidden, preactivation_gradient)
    low_rank_gradient_piece = settle_gradients(
        contract_trailing(preactivation_gradient, adapter_output_factor)
    )
    dm_part = settle_gradients(contract_trailing(preactivation_gradient, w_up))
    modulation_gradient_sum, dlow_sum = (
        lax.psum(dm_part.astype(jnp.bfloat16), "tensor").astype(jnp.float32),
        lax.psum(low_rank_gradient_piece.astype(jnp.bfloat16), "tensor").astype(jnp.float32),
    )
    low_rank_gradient = dlow_sum.astype(jnp.bfloat16)
    modulation_gradient = modulation_gradient_sum + contract_trailing(
        low_rank_gradient, adapter_input_factor
    )
    dn = modulation_gradient.reshape(spots, BLK, width) * modulation_scale
    first_sum = jnp.sum(dn, axis=-1, keepdims=True)
    second_sum = jnp.sum(dn * normalized_input, axis=-1, keepdims=True)
    back_part = inverse_deviation * (dn - first_sum / width - normalized_input * second_sum / width)
    grad_part = (out_grad + back_part).astype(jnp.bfloat16)
    grad_a = contract_first(modulated_input, low_rank_gradient)
    sum_a, sum_b = lax.psum((grad_a, grad_b), "dp")
    return (losses, grad_part.reshape(CAP * BLK, width), sum_a / n_dp, sum_b / n_dp)


MESH = pl.DeviceIdType.MESH
F32 = jnp.float32
BF16 = jnp.bfloat16
SIDE = 32
TILE = 384
PAD = 128
STRIP = 16
GELU_ROOT = 0.7978845608028654
GELU_CUBE = 0.044715


def activation(pre, want_slope):
    square = pre * pre
    bend = jnp.tanh(GELU_ROOT * pre * (1.0 + GELU_CUBE * square))
    half = 0.5 * (1.0 + bend)
    if not want_slope:
        return pre * half
    slope = half + 0.5 * pre * (1.0 - bend * bend) * GELU_ROOT * (1.0 + 3.0 * GELU_CUBE * square)
    return pre * half, slope


def step_kernel(
    live_ref, wins_ref, tail_ref, x_hbm, t_hbm, mod_hbm, up_ref, dn_ref, a_hbm, b_hbm,
    loss_ref, grad_out, ga_out, gb_out,
    x_ref, t_ref, mod_in, b_ref, at_ref, mod_ref, mask_ref, flag_ref,
    grad_ref, ga_ref, gb_ref, ga_rows, pre_ref, back_ref, local,
    w_ref, modded, low_ref, lowt_ref, slope_ref, hid_ref,
    ypart, crecv, ysend, yrecv, ysum, miss_ref, vbuf, ebuf, cf_ref,
    dpre_ref, dmpart, dmc, dmsend, dmrecv, dmsum,
    dlpart, dlc, dlsend, dlrecv, dlsum,
    gat, gatr, gap, gapr, gbp, gbr,
    z_send, z_recv, x_send, x_recv, c_send, c_recv, y_send, y_recv, v_send, v_recv,
    e_send, e_recv, dc_send, dc_recv, dy_send, dy_recv, g_send, g_recv,
    at_send, at_recv, rs_send, rs_recv, ag_send, ag_recv, tg_send, tg_recv,
):
    d = lax.axis_index("dp")
    t = lax.axis_index("tensor")
    z, x = d // 2, d % 2
    y, core = t // 2, t % 2
    high = z // 2
    middle = (z + high) % 2
    base = [middle, 1 - middle, 2, 3]
    place = [p + high * (3 - 2 * p) for p in base]
    inner = ((z + 1 - 2 * high) * 2 + x, t)
    edge_z = z - 1 + 2 * high
    edge = ((edge_z * middle + (1 - middle) * (z + 1 - 2 * high)) * 2 + x, t)
    across = (z * 2 + 1 - x, t)
    t_core = y * 2 + 1 - core
    t_y = (1 - y) * 2 + core
    t_far = (1 - y) * 2 + 1 - core
    mate = (d, t_core)
    over = (d, t_y)
    far = (d, t_far)
    peers = [mate, over, far]
    is_middle = middle == 1

    barrier = pltpu.get_barrier_semaphore()
    for k in range(1, 8):
        pl.semaphore_signal(barrier, inc=1, device_id=((d + k) % 8, t), device_id_type=MESH)
    for peer in peers:
        pl.semaphore_signal(barrier, inc=1, device_id=peer, device_id_type=MESH)

    shard = up_ref.shape[0]
    main = shard - SIDE
    half = main // 2
    here = pl.ds(d * shard, shard)
    loads = [
        pltpu.make_async_copy(src, dst, local.at[k]) for k, (src, dst) in enumerate((
            (up_ref, w_ref.at[0, here, :]), (dn_ref, w_ref.at[1, here, :]),
            (x_hbm, x_ref), (mod_hbm, mod_in),
            (a_hbm, at_ref.at[pl.ds(0, a_hbm.shape[0]), :]),
            (b_hbm, b_ref.at[pl.ds(0, b_hbm.shape[0]), :]), (t_hbm, t_ref)))]
    for load in loads:
        load.start()
    pl.semaphore_wait(barrier, 10)

    def copy(src, dst, send, recv, device):
        return pltpu.make_async_remote_copy(
            src_ref=src, dst_ref=dst, send_sem=send, recv_sem=recv,
            device_id=device, device_id_type=MESH)

    def rows(m, kind, slot):
        column = 1 - x if kind == 2 else x
        start = (0, half, main)[kind]
        size = (half, shard - half, SIDE)[kind]
        return w_ref.at[m, pl.ds((place[slot] * 2 + column) * shard + start, size), :]

    def x_rows(m, piece, column):
        slot, part = (0, 2) if piece == 8 else (piece // 2, piece % 2)
        size = SIDE if part == 2 else half
        return w_ref.at[m, pl.ds((place[slot] * 2 + column) * shard + part * half, size), :]

    def z_copy(m, kind, which):
        slot = [0, 0, 1, 2, 3][which]
        target = [1 + middle, 1, 3, 2, 3][which]
        device = inner if which in (0, 2) else edge
        ref = rows(m, kind, slot)
        src = ref
        if slot == 0 and kind < 2:
            start = (0, half)[kind]
            src = (up_ref, dn_ref)[m].at[pl.ds(start, (half, shard - half)[kind]), :]
        return copy(src, ref, z_send.at[m, kind, which], z_recv.at[m, kind, target], device)

    def z_arrive(m, kind, slot):
        ref = rows(m, kind, slot)
        copy(ref, ref, z_send.at[m, kind, 0], z_recv.at[m, kind, slot], inner).wait_recv()

    def x_copy(m, piece):
        ref = x_rows(m, piece, x)
        src = ref
        if piece in (0, 1, 8):
            start, size = {0: (0, half), 1: (half, half), 8: (main, SIDE)}[piece]
            src = (up_ref, dn_ref)[m].at[pl.ds(start, size), :]
        return copy(src, ref, x_send.at[m, piece], x_recv.at[m, piece], across)

    def x_arrive(m, piece):
        ref = x_rows(m, piece, 1 - x)
        copy(ref, ref, x_send.at[m, piece], x_recv.at[m, piece], across).wait_recv()

    def begin_inner(m):
        for part in range(2):
            z_copy(m, part, 0).start()

    def begin_x(m):
        x_copy(m, 8).start()
        for part in range(2):
            x_copy(m, part).start()

    def begin_edge(m):
        @pl.when(is_middle)
        def _():
            for part in range(2):
                z_copy(m, part, 1).start()

    def side_begin(m):
        x_arrive(m, 8)
        z_copy(m, 2, 0).start()

        @pl.when(is_middle)
        def _():
            z_copy(m, 2, 1).start()

    def relay_part(m, slot, part):
        z_arrive(m, part, slot)

        @pl.when(is_middle)
        def _():
            z_copy(m, part, slot + 1).start()

        x_copy(m, slot * 2 + part).start()

    def relay(m, slot):
        for part in range(2):
            relay_part(m, slot, part)

    def side_relay(m, slot):
        z_arrive(m, 2, slot)

        @pl.when(is_middle)
        def _():
            z_copy(m, 2, slot + 1).start()

    begin_edge(0)
    begin_inner(0)
    begin_x(0)

    count, wins = live_ref[0], wins_ref[0]
    tail_w, tail_l = tail_ref[0, 0], tail_ref[0, 1]
    loser_here = t >= wins
    last = jnp.where(loser_here, count - 1, wins - 1)
    tail = jnp.where(loser_here, tail_l, tail_w)
    live = jnp.where(t < count, jnp.where(t == last, tail, BLK), 0)
    spot = lax.broadcasted_iota(jnp.int32, (BLK, 1), 0)
    mask_ref[...] = jnp.where(spot < live, 1.0, 0.0)
    line = lax.broadcasted_iota(jnp.int32, (8, PAD), 0)
    flag_ref[...] = jnp.where(line >= wins, 1.0, 0.0)
    width = x_ref.shape[1]
    rows_w = jnp.broadcast_to(((wins - 1) * BLK + tail_w).astype(F32), (1, PAD))
    rows_l = jnp.broadcast_to(((count - wins - 1) * BLK + tail_l).astype(F32), (1, PAD))
    for load in loads:
        load.wait()
    rank = a_hbm.shape[0]
    b_ref[rank:PAD, :] = jnp.zeros((PAD - rank, b_ref.shape[1]), BF16)
    at_ref[rank:PAD, :] = jnp.zeros((PAD - rank, width), BF16)
    for b in range(CAP):
        loser = flag_ref[b:b + 1, 0:1]
        mod_ref[b] = ((1.0 - loser) * mod_in[:, 0, :].astype(F32)
                      + loser * mod_in[:, 1, :].astype(F32))

    def norm(block, b):
        wide = x_ref[block, :].astype(F32)
        center = wide - jnp.mean(wide, axis=-1, keepdims=True)
        inverse = lax.rsqrt(jnp.mean(center * center, axis=-1, keepdims=True) + EPS)
        vectors = mod_ref[b]
        return wide, center * inverse, inverse, vectors[0:1], 1.0 + vectors[1:2], vectors[2:3]

    @pl.loop(0, CAP * BLK // STRIP)
    def _(i):
        block = pl.ds(pl.multiple_of(i * STRIP, STRIP), STRIP)
        _, normed, _, shift, scale, _ = norm(block, i // (BLK // STRIP))
        modded[block, :] = (normed * scale + shift).astype(BF16)

    low_ref[...] = contract_trailing(modded[...], at_ref[...]).astype(BF16)
    lowt_ref[...] = contract_trailing(at_ref[...], modded[...]).astype(BF16)

    side_begin(0)
    relay(0, 1)

    @pl.when(middle == 0)
    def _():
        begin_inner(1)

    begin_x(1)
    side_relay(0, 1)
    relay(0, 2)
    side_relay(0, 2)
    relay(0, 3)
    side_relay(0, 3)

    @pl.when(is_middle)
    def _():
        begin_inner(1)

    begin_edge(1)
    side_begin(1)

    @pl.when(is_middle)
    def _():
        for slot in range(1, 4):
            relay(1, slot)
            side_relay(1, slot)

    def edge_relay(slot, parts=(0, 1)):
        @pl.when(middle == 0)
        def _():
            for part in parts:
                relay_part(1, slot, part)

    edge_relay(1)
    for piece in range(8):
        x_arrive(0, piece)

    @pl.loop(0, 4)
    def _(n):
        cols = pl.ds(pl.multiple_of(n * TILE, TILE), TILE)
        pre = jnp.dot(modded[...], w_ref[0, :, cols], preferred_element_type=F32)
        pre_ref[1] = pre
        pre_ref[0] = pre + jnp.dot(low_ref[...], b_ref[:, cols], preferred_element_type=F32)

        @pl.loop(0, CAP * BLK // STRIP)
        def _(i):
            strip = pl.ds(pl.multiple_of(i * STRIP, STRIP), STRIP)
            hid_ref[1, strip, cols] = activation(pre_ref[1, strip, :], False).astype(BF16)
            act, slope = activation(pre_ref[0, strip, :], True)
            hid_ref[0, strip, cols] = act.astype(BF16)
            slope_ref[strip, cols] = slope

    def y_core(j):
        src = ypart.at[j, 1 - core]
        return copy(src, crecv.at[j], c_send.at[j], c_recv.at[j], mate)

    def y_over(j):
        return copy(ysend.at[j], yrecv.at[j], y_send.at[j], y_recv.at[j], over)

    def v_copy(j, which):
        ref = vbuf.at[t_y if which == 2 else t, :, columns(j)]
        device = over if which == 1 else mate
        return copy(ref, ref, v_send.at[j, which], v_recv.at[j, which], device)

    def v_arrive(j, which):
        ref = vbuf.at[[t_core, t_y, t_far][which], :, columns(j)]
        copy(ref, ref, v_send.at[j, which], v_recv.at[j, which], mate).wait_recv()

    def columns(j):
        return pl.ds(pl.multiple_of(place[j] * TILE, TILE), TILE)

    def stage_product(j):
        @pl.loop(0, 2)
        def _(p):
            part = contract_trailing(hid_ref[p], w_ref[1, pl.ds(place[j] * TILE, TILE), :])
            part = part.astype(BF16)
            for b in range(CAP):
                ypart[j, b % 2, b // 2, p] = part[b * BLK:(b + 1) * BLK, :]
        y_core(j).start()

    def stage_pair(j):
        y_core(j).wait_recv()
        ysend[j] = (ypart[j, core, 1 - y].astype(F32) + crecv[j, 1 - y].astype(F32)).astype(BF16)
        y_over(j).start()
        ysum[j] = ypart[j, core, y].astype(F32) + crecv[j, y].astype(F32)

    own = pl.ds(t * BLK, BLK)

    def stage_total(j):
        y_over(j).wait_recv()
        cols = columns(j)
        total = ysum[j] + yrecv[j].astype(F32)
        gate = mod_ref[t, 2:3, cols]
        residual = x_ref[own, cols].astype(F32) - t_ref[own, cols].astype(F32)
        mask = mask_ref[...]
        miss = residual + gate * total[0]
        miss_ref2 = residual + gate * total[1]
        slope = 2.0 * mask * miss
        miss_ref[:, cols] = slope
        vbuf[t, :, cols] = (gate * slope).astype(BF16)
        v_copy(j, 0).start()
        v_copy(j, 1).start()
        err = jnp.concatenate([
            jnp.sum(mask * miss * miss, axis=(0, 1), keepdims=True),
            jnp.sum(mask * miss_ref2 * miss_ref2, axis=(0, 1), keepdims=True)], axis=0)
        return jnp.broadcast_to(err, (2, PAD))

    def stage_share(j):
        v_arrive(j, 1)
        v_copy(j, 2).start()

    def ready(j):
        x_arrive(1, 2 * j)
        x_arrive(1, 2 * j + 1)
        if j > 0:
            @pl.when(middle == 0)
            def _():
                side_relay(1, j)

    ready(0)
    stage_product(0)
    stage_pair(0)
    edge_relay(2)
    ready(1)
    stage_product(1)
    stage_pair(1)
    err = stage_total(0)
    edge_relay(3, (0,))
    ready(2)
    stage_product(2)
    stage_pair(2)
    edge_relay(3, (1,))
    err = err + stage_total(1)
    stage_share(0)
    err = err + stage_total(2)
    stage_share(1)
    ready(3)
    stage_product(3)
    stage_pair(3)
    err = err + stage_total(3)
    ebuf[t, 0:2, :] = err
    ebuf[t, 2:8, :] = jnp.zeros((6, PAD), F32)

    def e_copy(k):
        ref = ebuf.at[t]
        return copy(ref, ref, e_send.at[k], e_recv.at[k], peers[k])

    for k in range(3):
        e_copy(k).start()
    stage_share(2)
    stage_share(3)
    for k, peer in enumerate(peers):
        ref = ebuf.at[peer[1]]
        copy(ref, ref, e_send.at[k], e_recv.at[k], peer).wait_recv()
    gains = jnp.zeros((1, PAD), F32)
    loses = jnp.zeros((1, PAD), F32)
    for b in range(CAP):
        drop = ebuf[b, 0:1, :] - ebuf[b, 1:2, :]
        loser = flag_ref[b:b + 1, :]
        gains = gains + (1.0 - loser) * drop
        loses = loses + loser * drop
    inv_w, inv_l = 1.0 / (width * rows_w), 1.0 / (width * rows_l)
    outside = BETA * (gains * inv_w - loses * inv_l)
    loss = jnp.maximum(outside, 0.0) + jnp.log1p(jnp.exp(-jnp.abs(outside)))
    loss_ref[0] = loss[0, 0]
    weight = BETA * LOSS_SCALE / (1.0 + jnp.exp(-outside))
    loser = flag_ref[...]
    cf_ref[...] = weight * ((1.0 - loser) * inv_w - loser * inv_l)

    for j in range(4):
        v_arrive(j, 0)
        v_arrive(j, 2)

    @pl.loop(0, 4)
    def _(n):
        cols = pl.ds(pl.multiple_of(n * TILE, TILE), TILE)
        dy = vbuf[...].reshape(CAP * BLK, vbuf.shape[2])
        dh = jnp.dot(dy, w_ref[1, :, cols], preferred_element_type=F32)
        for b in range(CAP):
            block = slice(b * BLK, (b + 1) * BLK)
            dpre_ref[block, cols] = (
                dh[block] * (cf_ref[b:b + 1, 0:1] * slope_ref[block, cols])).astype(BF16)

    def dl_core():
        return copy(dlpart.at[1 - core], dlc, dc_send.at[4], dc_recv.at[4], mate)

    def dl_over():
        return copy(dlsend, dlrecv, dy_send.at[4], dy_recv.at[4], over)

    def dm_core(n):
        return copy(dmpart.at[n, 1 - core], dmc.at[n], dc_send.at[n], dc_recv.at[n], mate)

    def dm_over(n):
        return copy(dmsend.at[n], dmrecv.at[n], dy_send.at[n], dy_recv.at[n], over)

    def at_copy(k):
        return copy(gat.at[peers[k][1]], gatr.at[k], at_send.at[k], at_recv.at[k], peers[k])

    def rs_copy(which, k):
        to = (d + k) % 8
        part, land = ((gap, gapr), (gbp, gbr))[which]
        return copy(part.at[to], land.at[k], rs_send.at[which, k], rs_recv.at[which, k], (to, t))

    def ag_copy(which, k):
        to = (d + k) % 8
        ref = ga_ref.at[t, d] if which == 0 else gb_ref.at[d]
        return copy(ref, ref, ag_send.at[which, k], ag_recv.at[which, k], (to, t))

    def ag_arrive(which, k):
        source = (d + 8 - k) % 8
        ref = ga_ref.at[t, source] if which == 0 else gb_ref.at[source]
        copy(ref, ref, ag_send.at[which, k], ag_recv.at[which, k], (source, t)).wait_recv()

    dlowt = contract_trailing(b_ref[...], dpre_ref[...]).astype(BF16)
    ga = jnp.dot(dlowt, modded[...], preferred_element_type=F32).astype(BF16)
    for k in range(4):
        gat[k] = ga[k * 16:(k + 1) * 16, :]
    for k in range(3):
        at_copy(k).start()

    dlow = contract_trailing(dpre_ref[...], b_ref[...]).astype(BF16)
    for b in range(CAP):
        dlpart[b % 2, b // 2] = dlow[b * BLK:(b + 1) * BLK, :]
    dl_core().start()

    def dm_product(n):
        part = contract_trailing(
            dpre_ref[...], w_ref[0, n * TILE:(n + 1) * TILE, :]).astype(BF16)
        for b in range(CAP):
            dmpart[n, b % 2, b // 2] = part[b * BLK:(b + 1) * BLK, :]
        dm_core(n).start()

    def dm_pair(n):
        dm_core(n).wait_recv()
        dmsend[n] = (dmpart[n, core, 1 - y].astype(F32) + dmc[n, 1 - y].astype(F32)).astype(BF16)
        dm_over(n).start()
        dmsum[n] = dmpart[n, core, y].astype(F32) + dmc[n, y].astype(F32)

    dm_product(0)
    gb = jnp.dot(lowt_ref[...], dpre_ref[...], preferred_element_type=F32).astype(BF16)
    half_b = gb.shape[1] // 2
    for k in range(8):
        gbp[k] = gb[(k // 2) * 16:(k // 2 + 1) * 16, (k % 2) * half_b:(k % 2 + 1) * half_b]
    for k in range(1, 8):
        rs_copy(1, k).start()
    dm_pair(0)
    dl_core().wait_recv()
    dlsend[...] = (dlpart[core, 1 - y].astype(F32) + dlc[1 - y].astype(F32)).astype(BF16)
    dl_over().start()
    dlsum[...] = dlpart[core, y].astype(F32) + dlc[y].astype(F32)
    dm_product(1)
    total = gat[t].astype(F32)
    for k in range(3):
        at_copy(k).wait_recv()
        total = total + gatr[k].astype(F32)
    total = total.astype(BF16)
    wide = total.shape[1] // 8
    for k in range(8):
        gap[k] = total[:, k * wide:(k + 1) * wide]
    for k in range(1, 8):
        rs_copy(0, k).start()
    dm_pair(1)
    dm_product(2)
    dm_pair(2)
    dm_product(3)
    dm_pair(3)

    for which, (part, land) in ((0, (gap, gapr)), (1, (gbp, gbr))):
        total = part[d].astype(F32)
        for k in range(1, 8):
            rs_copy(which, k).wait_recv()
            total = total + land[k].astype(F32)
        if which == 1:
            gb_ref[d] = total.astype(BF16)
        else:
            ga_ref[t, d] = total.astype(BF16)
        for k in range(1, 8):
            ag_copy(which, k).start()

    dl_over().wait_recv()
    dlow = (dlsum[...] + dlrecv[...].astype(F32)).astype(BF16)
    for n in range(4):
        dm_over(n).wait_recv()
    back_ref[...] = jnp.dot(dlow, at_ref[...], preferred_element_type=F32)

    @pl.loop(0, BLK // STRIP)
    def _(i):
        strip = pl.ds(pl.multiple_of(i * STRIP, STRIP), STRIP)
        _, normed, inverse, _, scale, _ = norm(
            pl.ds(pl.multiple_of(t * BLK + i * STRIP, STRIP), STRIP), t)
        dm = jnp.concatenate(
            [dmsum[n, strip, :] + dmrecv[n, strip, :].astype(F32) for n in range(4)], axis=1)
        dn = (dm + back_ref[strip, :]) * scale
        first = jnp.mean(dn, axis=-1, keepdims=True)
        second = jnp.mean(dn * normed, axis=-1, keepdims=True)
        out_grad = cf_ref[pl.ds(t, 1), 0:1] * miss_ref[strip, :]
        grad_ref[t, strip, :] = (
            out_grad + inverse * (dn - first - normed * second)).astype(BF16)

    def tg_copy(which):
        ref = ga_rows.at[t_y if which == 2 else t]
        return copy(ref, ref, tg_send.at[which], tg_recv.at[which],
                    over if which == 1 else mate)

    def tg_arrive(which):
        ref = ga_rows.at[[t_core, t_y, t_far][which]]
        copy(ref, ref, tg_send.at[which], tg_recv.at[which], mate).wait_recv()


    def g_copy(which):
        ref = grad_ref.at[t_y] if which == 2 else grad_ref.at[t]
        return copy(ref, ref, g_send.at[which], g_recv.at[which], over if which == 1 else mate)

    def g_arrive(which):
        ref = grad_ref.at[[t_core, t_y, t_far][which]]
        copy(ref, ref, g_send.at[which], g_recv.at[which], mate).wait_recv()

    def g_store(k, block):
        return pltpu.make_async_copy(
            grad_ref.at[block], grad_out.at[pl.ds(block * BLK, BLK), :], local.at[7 + k])

    g_copy(1).start()
    g_copy(0).start()
    for k in range(1, 8):
        ag_arrive(0, k)
    for k in range(8):
        ga_rows[t, :, k * wide:(k + 1) * wide] = ga_ref[t, k]
    tg_copy(1).start()
    tg_copy(0).start()
    g_store(0, t).start()

    g_arrive(1)
    g_copy(2).start()
    g_store(2, t_y).start()
    tg_arrive(1)
    tg_copy(2).start()
    for k in range(1, 8):
        ag_arrive(1, k)
    for k in range(8):
        gb_out[(k // 2) * 16:(k // 2 + 1) * 16, (k % 2) * half_b:(k % 2 + 1) * half_b] = (
            gb_ref[k])
    g_arrive(0)
    g_store(1, t_core).start()
    g_arrive(2)
    g_store(3, t_far).start()
    tg_arrive(0)
    tg_arrive(2)
    ga_out[...] = ga_rows[...].reshape(ga_out.shape)
    for k, block in enumerate((t, t_core, t_y, t_far)):
        g_store(k, block).wait()

    for m in range(2):
        for piece in range(9):
            x_copy(m, piece).wait_send()
        for kind in range(3):
            z_copy(m, kind, 0).wait_send()

            @pl.when(is_middle)
            def _():
                for which in range(1, 5):
                    z_copy(m, kind, which).wait_send()
    for j in range(4):
        y_core(j).wait_send()
        y_over(j).wait_send()
        dm_core(j).wait_send()
        dm_over(j).wait_send()
        for which in range(3):
            v_copy(j, which).wait_send()
    dl_core().wait_send()
    dl_over().wait_send()
    for k in range(3):
        e_copy(k).wait_send()
        at_copy(k).wait_send()
        g_copy(k).wait_send()
        tg_copy(k).wait_send()
    for which in range(2):
        for k in range(1, 8):
            rs_copy(which, k).wait_send()
            ag_copy(which, k).wait_send()


def fused_device(
    tokens, targets, modulation, live_block_count, preferred_blocks, last_block_rows,
    up_projection_weight, down_weight_transposed, adapter_input_factor, adapter_output_factor,
):
    width = tokens.shape[1]
    rank = adapter_input_factor.shape[1]
    hidden = adapter_output_factor.shape[1]
    dma = pltpu.SemaphoreType.DMA
    vm = pltpu.VMEM
    rows = CAP * BLK
    smem = pl.BlockSpec(memory_space=pltpu.SMEM)
    anywhere = pl.BlockSpec(memory_space=pl.ANY)
    whole = pl.BlockSpec(memory_space=pltpu.VMEM)
    losses, grad, grad_a, grad_b = pl.pallas_call(
        step_kernel,
        out_shape=(
            jax.ShapeDtypeStruct((1,), F32),
            jax.ShapeDtypeStruct((rows, width), BF16),
            jax.ShapeDtypeStruct((rank, width), BF16),
            jax.ShapeDtypeStruct((rank, hidden), BF16),
        ),
        in_specs=[smem] * 3 + [anywhere] * 7,
        out_specs=(smem, anywhere, whole, whole),
        scratch_shapes=[
            vm((rows, width), BF16),
            vm((rows, width), BF16),
            vm((3, 2, width), BF16),
            vm((PAD, hidden), BF16),
            vm((PAD, width), BF16),
            vm((CAP, 3, width), F32),
            vm((BLK, 1), F32),
            vm((8, PAD), F32),
            vm((CAP, BLK, width), BF16),
            vm((4, 8, 16, width // 8), BF16),
            vm((8, 16, hidden // 2), BF16),
            vm((4, 16, width), BF16),
            vm((2, rows, TILE), F32),
            vm((BLK, width), F32),
            dma((11,)),
            vm((2, width, hidden), BF16),
            vm((rows, width), BF16),
            vm((rows, PAD), BF16),
            vm((PAD, rows), BF16),
            vm((rows, hidden), F32),
            vm((2, rows, hidden), BF16),
            vm((4, 2, 2, 2, BLK, TILE), BF16),
            vm((4, 2, 2, BLK, TILE), BF16),
            vm((4, 2, BLK, TILE), BF16),
            vm((4, 2, BLK, TILE), BF16),
            vm((4, 2, BLK, TILE), F32),
            vm((BLK, width), F32),
            vm((CAP, BLK, width), BF16),
            vm((CAP, 8, PAD), F32),
            vm((8, PAD), F32),
            vm((rows, hidden), BF16),
            vm((4, 2, 2, BLK, TILE), BF16),
            vm((4, 2, BLK, TILE), BF16),
            vm((4, BLK, TILE), BF16),
            vm((4, BLK, TILE), BF16),
            vm((4, BLK, TILE), F32),
            vm((2, 2, BLK, PAD), BF16),
            vm((2, BLK, PAD), BF16),
            vm((BLK, PAD), BF16),
            vm((BLK, PAD), BF16),
            vm((BLK, PAD), F32),
            vm((4, 16, width), BF16),
            vm((3, 16, width), BF16),
            vm((8, 16, width // 8), BF16),
            vm((8, 16, width // 8), BF16),
            vm((8, 16, hidden // 2), BF16),
            vm((8, 16, hidden // 2), BF16),
            dma((2, 3, 5)), dma((2, 3, 4)), dma((2, 9)), dma((2, 9)),
            dma((4,)), dma((4,)), dma((4,)), dma((4,)), dma((4, 3)), dma((4, 3)),
            dma((3,)), dma((3,)), dma((5,)), dma((5,)), dma((5,)), dma((5,)),
            dma((3,)), dma((3,)), dma((3,)), dma((3,)),
            dma((2, 8)), dma((2, 8)), dma((2, 8)), dma((2, 8)), dma((3,)), dma((3,)),
        ],
        compiler_params=pltpu.CompilerParams(
            collective_id=0, has_side_effects=True, vmem_limit_bytes=60 * 1024 * 1024),
    )(live_block_count, preferred_blocks, last_block_rows, tokens, targets,
      modulation.transpose(1, 0, 2), up_projection_weight, down_weight_transposed,
      adapter_input_factor.T, adapter_output_factor)
    n_dp = lax.axis_size("dp")
    return losses, grad, grad_a.T.astype(F32) / n_dp, grad_b.astype(F32) / n_dp


def fits_fused(mesh):
    return dict(mesh.shape) == {"dp": 8, "tensor": 4}


def solution(mesh):
    return jax.shard_map(
        fused_device if fits_fused(mesh) else per_device,
        mesh=mesh,
        in_specs=(
            P("dp", None),
            P("dp", None),
            P("dp", None, None),
            P("dp"),
            P("dp"),
            P("dp", None),
            P("dp", "tensor"),
            P("dp", "tensor"),
            P(),
            P(None, "tensor"),
        ),
        out_specs=(P("dp"), P("dp", None), P(), P(None, "tensor")),
        check_vma=False,
    )
```
